32 devices in a mesh: rep: 8 (over z, x), shard: 4 (over y, core).
Axes of the slice: x: 2, y: 2, z: 4, core: 2. Of those that a mesh axis runs over, the one named last changes fastest.
Arguments:
- tokens: bfloat16 [4096, 1024], P(('rep', 'shard')), may hold values from -6 to 6
- cotangent: bfloat16 [4096, 1024], P(('rep', 'shard')), may hold values from -6 to 6
- w_qkv: bfloat16 [2, 1024, 3072], P(None, 'shard'), may hold values from -0.1875 to 0.1875
- w_out: bfloat16 [2, 1024, 1024], P(None, 'shard'), may hold values from -1.5 to 1.5
- w_up: bfloat16 [2, 1024, 4096], P(None, 'shard'), may hold values from -0.1875 to 0.1875
- w_down: bfloat16 [2, 4096, 1024], P(None, 'shard'), may hold values from -0.09375 to 0.09375
- ln_gain: bfloat16 [2, 1024, 2], P(None, 'shard'), may hold values from 0.25 to 1.75
- ln_bias: bfloat16 [2, 1024, 2], P(None, 'shard'), may hold values from -3 to 3
- positions: bfloat16 [512, 1024], P('shard'), may hold values from -6 to 6
- segments: int32 [4096], P(('rep', 'shard')), may hold values from 0 to 1, as said below
- keep_mask: int32 [4096], P(('rep', 'shard')), may hold values from 0 to 1, as said below
- buckets: int32 [255], replicated, may hold values from 161 to 351, as said below
Outputs:
- output: bfloat16 [4096, 1024], P(('rep', 'shard'))
- grad_tokens: float32 [4096, 1024], P(('rep', 'shard'))
- grad_qkv: float32 [2, 1024, 3072], P(None, 'shard')
- grad_out: float32 [2, 1024, 1024], P(None, 'shard')
- grad_up: float32 [2, 1024, 4096], P(None, 'shard')
- grad_down: float32 [2, 4096, 1024], P(None, 'shard')
- grad_gain: float32 [2, 1024, 2], P(None, 'shard')
- grad_bias: float32 [2, 1024, 2], P(None, 'shard')
- grad_positions: float32 [512, 1024], P('shard')
The draws below stay inside these ranges and needn't reach their ends.
Inputs may be any that keep to these rules, and one draw needn't show every extreme that they name: `segments`: in each sequence of 128 tokens the document numbers start at 0, never fall, rise by one at each new document, and every document holds 60 tokens or more. `keep_mask`: in each sequence of 128 tokens the ones come first; at most 30 tokens at the end are padding. `buckets`: 256 at distance 0, never falling as i - j rises, symmetric about distance 0, distances below 64 in size each with a bucket of their own.
All inputs are finite; a program needn't handle non-finite values.
Results may differ from the reference program's by a relative error of at most 0.028.
Values may be sent and summed in bfloat16 or wider, within the bound.
No kernel may reach another device: no remote copies, remote signals or barrier semaphores. Data moves between devices by JAX's collectives and lax.ppermute only.
A program may use at most 320 MiB of HBM per device.

```python
import math
import jax
import jax.numpy as jnp
from jax import lax

D = 1024
H = 16
DH = 64
FF = 4096
NB = 512
LAYERS = 2
LEN = 128
DOC_MIN = 60
MID = 64
TOKENS = 4096


def draw_segments(key, part):
    key = jax.random.fold_in(key, 11)
    seq_count = TOKENS // LEN
    most_docs = LEN // DOC_MIN
    count_key, cut_key, pick_key = jax.random.split(key, 3)
    counts = jax.random.randint(count_key, (seq_count,), 1, most_docs + 1)
    first = jax.random.randint(pick_key, (), 0, seq_count)
    second = (first + 1 + jax.random.randint(jax.random.fold_in(pick_key, 1), (), 0, seq_count - 1)) % seq_count
    rows = jnp.arange(seq_count)
    counts = jnp.where(rows == first, most_docs, jnp.where(rows == second, 1, counts))
    slack = LEN - counts * DOC_MIN
    cut_ids = jnp.arange(most_docs - 1)
    raw = jax.random.randint(cut_key, (seq_count, most_docs - 1), 0, slack[:, None] + 1)
    used = cut_ids[None, :] < counts[:, None] - 1
    raw = jnp.where(used, raw, LEN)
    ordered = jnp.sort(raw, axis=1)
    bounds = jnp.where(used, (cut_ids[None, :] + 1) * DOC_MIN + ordered, 2 * LEN)
    places = jnp.arange(LEN)
    ids = jnp.sum((places[None, :, None] >= bounds[:, None, :]).astype(jnp.int32), axis=2)
    return ids.reshape(TOKENS).astype(jnp.int32)


def draw_keep_mask(key, part):
    key = jax.random.fold_in(key, 12)
    seq_count = TOKENS // LEN
    pad_key, pick_key = jax.random.split(key, 2)
    padding = jax.random.randint(pad_key, (seq_count,), 0, DOC_MIN // 2 + 1)
    chosen = jax.random.randint(pick_key, (), 0, seq_count)
    padding = jnp.where(jnp.arange(seq_count) == chosen, DOC_MIN // 2, padding)
    flags = (jnp.arange(LEN)[None, :] < LEN - padding[:, None]).astype(jnp.int32)
    return flags.reshape(TOKENS)


def draw_buckets(key, part):
    key = jax.random.fold_in(key, 13)
    far_count = LEN - 1 - MID
    order = jax.random.permutation(key, far_count)
    flags = (order < far_count // 2).astype(jnp.int32)
    steps = jnp.concatenate([jnp.zeros((1,), jnp.int32), jnp.ones((MID,), jnp.int32), flags])
    offset = jnp.minimum(jnp.cumsum(steps), NB // 2 - 1)
    distance = jnp.arange(2 * LEN - 1) - (LEN - 1)
    return (NB // 2 + jnp.sign(distance) * offset[jnp.abs(distance)]).astype(jnp.int32)


def level_of(rng, extent, cuts, least, largest):
    level = 1.0
    for dim, shards_of in cuts:
        draws = jax.random.uniform(jax.random.fold_in(jax.random.fold_in(rng, 6), dim), (shards_of,), jnp.float32, least / len(cuts), largest / len(cuts))
        level = level * jnp.repeat(jnp.exp(draws), extent[dim] // shards_of).reshape((-1,) + (1,) * (len(extent) - 1 - dim))
    return level


def centred(key, dims, deviation, bound, cuts=(), kind=jnp.bfloat16):
    loudness = level_of(key, dims, cuts, -0.22, 0.18) if cuts else 1.0
    entries = jax.random.normal(key, dims, jnp.float32) * deviation * loudness
    return jnp.minimum(jnp.maximum(entries, -bound), bound).astype(kind)


def setup_inputs(seed: int = 0) -> dict:
    arg_keys = jax.random.split(jax.random.key(seed), 13)
    tokens = centred(arg_keys[0], (TOKENS, D), 1.0, 6.0, ((0, 32),))
    cotangent = centred(arg_keys[1], (TOKENS, D), 1.0, 6.0, ((0, 32),))
    w_qkv = centred(arg_keys[2], (LAYERS, D, 3 * D), D ** -0.5, 0.1875, ((1, 4),))
    w_out = centred(arg_keys[3], (LAYERS, D, D), (D // 64) ** -0.5, 1.5, ((1, 4),))
    w_up = centred(arg_keys[4], (LAYERS, D, FF), D ** -0.5, 0.1875, ((1, 4),))
    w_down = centred(arg_keys[5], (LAYERS, FF, D), FF ** -0.5, 0.09375, ((1, 4),))
    ln_gain = jnp.clip(1.0 + 0.15 * jax.random.normal(arg_keys[6], (LAYERS, D, 2), jnp.float32), 0.25, 1.75).astype(jnp.bfloat16)
    ln_bias = centred(arg_keys[7], (LAYERS, D, 2), 0.5, 3.0, ((1, 4),))
    positions = centred(arg_keys[8], (NB, D), 1.0, 6.0, ((0, 4),))
    segments = draw_segments(jax.random.fold_in(arg_keys[12], 71), 0)
    keep_mask = draw_keep_mask(jax.random.fold_in(arg_keys[12], 71), 0)
    buckets = draw_buckets(jax.random.fold_in(arg_keys[12], 71), 0)
    return {"tokens": tokens, "cotangent": cotangent, "w_qkv": w_qkv, "w_out": w_out, "w_up": w_up, "w_down": w_down, "ln_gain": ln_gain, "ln_bias": ln_bias, "positions": positions, "segments": segments, "keep_mask": keep_mask, "buckets": buckets}


PREC = lax.Precision.HIGHEST
NEG_FILL = -1e+30
NORM_EPS = 1e-07

@jax.custom_vjp
def low(v):
    return lax.optimization_barrier(v.astype(jnp.bfloat16)).astype(jnp.float32)

@jax.custom_vjp
def low_back(v):
    return v

def low_keep(v):
    return (low(v), None)

def low_pass(kept, grad):
    return (grad,)

def back_keep(v):
    return (v, None)

def back_low(kept, grad):
    return (low(grad),)
low.defvjp(low_keep, low_pass)
low_back.defvjp(back_keep, back_low)

def layer_norm(values, gain, bias):
    centre = values - lax.optimization_barrier(jnp.mean(values, axis=-1, keepdims=True))
    spread_sq = lax.optimization_barrier(jnp.mean(centre * centre, axis=-1, keepdims=True))
    return centre * lax.rsqrt(spread_sq + NORM_EPS) * gain + bias

def ref_layer(hidden, seg_ids, keep_ids, w_qkv, w_out, w_up, w_down, gains, biases, rel_base, bucket_idx):
    seqs = seg_ids.shape[0]
    hidden_low = low(hidden)
    qkv_all = low(low_back(jnp.dot(hidden_low, w_qkv, precision=PREC)))
    heads_q = qkv_all[:, :D].reshape(seqs, LEN, H, DH)
    heads_k = qkv_all[:, D:2 * D].reshape(seqs, LEN, H, DH)
    heads_v = qkv_all[:, 2 * D:].reshape(seqs, LEN, H, DH)
    rel_each = low_back(jnp.broadcast_to(rel_base, (seqs,) + rel_base.shape))
    rel_q = rel_each[:, :, :D].reshape(seqs, NB, H, DH)
    rel_k = rel_each[:, :, D:].reshape(seqs, NB, H, DH)
    direct = jnp.einsum('sihd,sjhd->shij', heads_q, heads_k, precision=PREC)
    by_key = jnp.einsum('sihd,sbhd->shib', heads_q, rel_k, precision=PREC)
    by_query = jnp.einsum('sjhd,sbhd->shjb', heads_k, rel_q, precision=PREC)
    gather_idx = jnp.broadcast_to(bucket_idx, (seqs, H, LEN, LEN))
    combined = direct + jnp.take_along_axis(by_key, gather_idx, axis=3)
    combined = combined + jnp.swapaxes(jnp.take_along_axis(by_query, gather_idx, axis=3), 2, 3)
    scores = low_back(combined / math.sqrt(3 * DH))
    allowed = (seg_ids[:, :, None] == seg_ids[:, None, :]) & (keep_ids[:, None, :] == 1)
    allowed = allowed | jnp.eye(LEN, dtype=bool)[None]
    probs = low(jax.nn.softmax(jnp.where(allowed[:, None], scores, NEG_FILL), axis=-1))
    context = low(low_back(jnp.einsum('shij,sjhd->sihd', probs, heads_v, precision=PREC)))
    context = context.reshape(seqs * LEN, D)
    attn_sum = hidden + low_back(jnp.dot(context, w_out, precision=PREC))
    mid_out = layer_norm(attn_sum, gains[:, 0], biases[:, 0])
    pre_act = low_back(jnp.dot(low(mid_out), w_up, precision=PREC))
    activation = low(jax.nn.gelu(pre_act, approximate=False))
    ffn_sum = mid_out + low_back(jnp.dot(activation, w_down, precision=PREC))
    return layer_norm(ffn_sum, gains[:, 1], biases[:, 1])

def reference(tokens, cotangent, w_qkv, w_out, w_up, w_down, ln_gain, ln_bias, positions, segments, keep_mask, buckets):
    offsets = jnp.arange(LEN)
    bucket_idx = buckets[offsets[:, None] - offsets[None, :] + LEN - 1]
    group_size = math.gcd(max(1, 4096 // LEN), TOKENS // LEN)
    group_count = TOKENS // (group_size * LEN)
    seg_groups = segments.reshape(group_count, group_size, LEN)
    keep_groups = keep_mask.reshape(group_count, group_size, LEN)

    def forward(hidden, wq_all, wo_all, wu_all, wd_all, gain_all, bias_all, pos_rows):
        rel_list = [low(jnp.dot(pos_rows, wq_all[layer_id][:, :2 * D], precision=PREC)) for layer_id in range(LAYERS)]

        def one_group(pieces):
            state, seg_ids, keep_ids = pieces
            for layer_id in range(LAYERS):
                state = ref_layer(state, seg_ids, keep_ids, wq_all[layer_id], wo_all[layer_id], wu_all[layer_id], wd_all[layer_id], gain_all[layer_id], bias_all[layer_id], rel_list[layer_id], bucket_idx)
            return state
        results = lax.map(jax.checkpoint(one_group), (hidden.reshape(group_count, group_size * LEN, D), seg_groups, keep_groups))
        return results.reshape(TOKENS, D)
    primals = tuple((source.astype(jnp.float32) for source in (tokens, w_qkv, w_out, w_up, w_down, ln_gain, ln_bias, positions)))
    result, pull_back = jax.vjp(forward, *primals)
    gradients = pull_back(cotangent.astype(jnp.float32))
    return (result.astype(jnp.bfloat16), gradients[0], gradients[1], gradients[2], gradients[3], gradients[4], gradients[5], gradients[6], gradients[7])
```

```python
from functools import partial
import math

import jax
import jax.numpy as jnp
from jax import lax
from jax.experimental import pallas as pl
from jax.experimental.pallas import tpu as pltpu
from jax.sharding import PartitionSpec as P

D = 1024
H = 16
DH = 64
LAYERS = 2
LEN = 128
SPAN = 2 * LEN
SCALE = 1.0 / math.sqrt(3 * DH)
NEG_FILL = -1e30
NORM_EPS = 1e-07
F32 = jnp.float32
BF16 = jnp.bfloat16


def mm(a, b):
    return jnp.dot(a, b, preferred_element_type=F32)


def mm_nt(a, b):
    return lax.dot_general(a, b, (((1,), (1,)), ((), ())), preferred_element_type=F32)


def mm_tn(a, b):
    return lax.dot_general(a, b, (((0,), (0,)), ((), ())), preferred_element_type=F32)


def swap(value, axis, mask):
    size = lax.axis_size(axis)
    return lax.ppermute(value, axis, [(i, i ^ mask) for i in range(size)])


def rising_masks(axis):
    size = lax.axis_size(axis)
    masks, mask = [], 1
    while mask < size:
        masks.append(mask)
        mask *= 2
    return masks


def group_order(axis):
    order = [0]
    for mask in reversed(rising_masks(axis)):
        order = order + [place ^ mask for place in order]
    return order


def gather_tokens(rows):
    for mask in reversed(rising_masks("shard")):
        rows = jnp.concatenate([rows, swap(rows, "shard", mask)], axis=0)
    return rows


def scatter_tokens(partial_rows):
    total = partial_rows
    for mask in rising_masks("shard"):
        half = total.shape[0] // 2
        sent = total[half:].astype(BF16)
        total = total[:half] + swap(sent, "shard", mask).astype(F32)
    return total


def by_columns(owned, me):
    rows, parts, n, c = owned.shape
    whole = jnp.zeros((n * rows, parts * c), owned.dtype)
    for mask in range(n):
        other = jnp.bitwise_xor(me, mask)
        block = lax.dynamic_index_in_dim(owned, other, 2, keepdims=False).reshape(rows, parts * c)
        if mask:
            block = swap(block, "shard", mask)
        whole = lax.dynamic_update_slice(whole, block, (other * rows, 0))
    return whole


def by_rows(columns, me, n, parts):
    rows = columns.shape[0] // n
    c = columns.shape[1] // parts
    whole = jnp.zeros((rows, parts, n, c), columns.dtype)
    for mask in range(n):
        other = jnp.bitwise_xor(me, mask)
        block = lax.dynamic_slice_in_dim(columns, other * rows, rows, 0)
        if mask:
            block = swap(block, "shard", mask)
        block = block.reshape(rows, parts, 1, c)
        whole = lax.dynamic_update_slice(whole, block, (0, 0, other, 0))
    return whole.reshape(rows, parts * n * c)


def attention_forward_kernel(heads, qkv_ref, rel_ref, allowed_ref, context_ref, probs_ref):
    width = heads * DH
    allowed = allowed_ref[0] > 0
    for head in range(heads):
        at = head * DH
        q = qkv_ref[:, at : at + DH]
        k = qkv_ref[:, width + at : width + at + DH]
        v = qkv_ref[:, 2 * width + at : 2 * width + at + DH]
        rel_q = rel_ref[:, at : at + DH]
        rel_k = rel_ref[:, width + at : width + at + DH]
        by_key = pltpu.roll(mm_nt(q, rel_k), LEN + 1, 1, stride=1, stride_axis=0)[:, :LEN]
        by_query = pltpu.roll(mm_nt(k, rel_q), LEN + 1, 1, stride=1, stride_axis=0)[:, :LEN]
        scores = (mm_nt(q, k) + by_key + by_query.T) * SCALE
        masked = jnp.where(allowed, scores, NEG_FILL)
        terms = jnp.exp(masked - jnp.max(masked, axis=1, keepdims=True))
        probs = terms / jnp.sum(terms, axis=1, keepdims=True)
        probs_ref[0, head] = probs
        context_ref[:, at : at + DH] = mm(probs.astype(BF16), v).astype(BF16)


def attention_forward(qkv, rel_back, allowed, heads):
    count = allowed.shape[0]
    width = heads * DH
    return pl.pallas_call(
        partial(attention_forward_kernel, heads),
        grid=(count,),
        in_specs=[
            pl.BlockSpec((LEN, 3 * width), lambda s: (s, 0)),
            pl.BlockSpec((SPAN, 2 * width), lambda s: (0, 0)),
            pl.BlockSpec((1, LEN, LEN), lambda s: (s, 0, 0)),
        ],
        out_specs=[
            pl.BlockSpec((LEN, width), lambda s: (s, 0)),
            pl.BlockSpec((1, heads, LEN, LEN), lambda s: (s, 0, 0, 0)),
        ],
        out_shape=[
            jax.ShapeDtypeStruct((count * LEN, width), BF16),
            jax.ShapeDtypeStruct((count, heads, LEN, LEN), F32),
        ],
        compiler_params=pltpu.CompilerParams(vmem_limit_bytes=24 * 1024 * 1024),
        name="attention_forward",
    )(qkv, rel_back, allowed)


def attention_backward_kernel(heads, qkv_ref, rel_ref, probs_ref, grad_ref, dqkv_ref, drel_ref):
    width = heads * DH

    @pl.when(pl.program_id(0) == 0)
    def _():
        drel_ref[...] = jnp.zeros_like(drel_ref)

    row = lax.broadcasted_iota(jnp.int32, (LEN, LEN), 0)
    column = lax.broadcasted_iota(jnp.int32, (LEN, LEN), 1)
    flip = jnp.where(row + column == LEN - 1, 1.0, 0.0).astype(BF16)
    blank = jnp.zeros((LEN, LEN), F32)

    def spread(flipped):
        wide = jnp.concatenate([flipped, blank], axis=1)
        return pltpu.roll(wide, 0, 1, stride=1, stride_axis=0).astype(BF16)

    for head in range(heads):
        at = head * DH
        q = qkv_ref[:, at : at + DH]
        k = qkv_ref[:, width + at : width + at + DH]
        v = qkv_ref[:, 2 * width + at : 2 * width + at + DH]
        rel_q = rel_ref[:, at : at + DH]
        rel_k = rel_ref[:, width + at : width + at + DH]
        grad = grad_ref[:, at : at + DH]
        probs = probs_ref[0, head]
        d_value = mm_tn(probs.astype(BF16), grad)
        d_probs = mm_nt(grad, v)
        inner = jnp.sum(d_probs * probs, axis=1, keepdims=True)
        d_scores = (probs * (d_probs - inner)).astype(BF16)
        key_side = spread(mm(d_scores, flip))
        query_side = spread(mm_tn(d_scores, flip))
        d_query = (mm(d_scores, k) + mm(key_side, rel_k)) * SCALE
        d_key = (mm_tn(d_scores, q) + mm(query_side, rel_q)) * SCALE
        dqkv_ref[:, at : at + DH] = d_query.astype(BF16)
        dqkv_ref[:, width + at : width + at + DH] = d_key.astype(BF16)
        dqkv_ref[:, 2 * width + at : 2 * width + at + DH] = d_value.astype(BF16)
        drel_ref[:, at : at + DH] += mm_tn(query_side, k) * SCALE
        drel_ref[:, width + at : width + at + DH] += mm_tn(key_side, q) * SCALE


def attention_backward(qkv, rel_ahead, probs, d_context, heads):
    count = probs.shape[0]
    width = heads * DH
    return pl.pallas_call(
        partial(attention_backward_kernel, heads),
        grid=(count,),
        in_specs=[
            pl.BlockSpec((LEN, 3 * width), lambda s: (s, 0)),
            pl.BlockSpec((SPAN, 2 * width), lambda s: (0, 0)),
            pl.BlockSpec((1, heads, LEN, LEN), lambda s: (s, 0, 0, 0)),
            pl.BlockSpec((LEN, width), lambda s: (s, 0)),
        ],
        out_specs=[
            pl.BlockSpec((LEN, 3 * width), lambda s: (s, 0)),
            pl.BlockSpec((SPAN, 2 * width), lambda s: (0, 0)),
        ],
        out_shape=[
            jax.ShapeDtypeStruct((count * LEN, 3 * width), BF16),
            jax.ShapeDtypeStruct((SPAN, 2 * width), F32),
        ],
        compiler_params=pltpu.CompilerParams(vmem_limit_bytes=24 * 1024 * 1024),
        name="attention_backward",
    )(qkv, rel_ahead, probs, d_context)


def normed(values):
    centre = values - jnp.mean(values, axis=-1, keepdims=True)
    inverse = lax.rsqrt(jnp.mean(centre * centre, axis=-1, keepdims=True) + NORM_EPS)
    return centre * inverse, inverse


def norm_backward(upstream, values, gain):
    hat, inverse = normed(values)
    pushed = upstream * gain
    first = jnp.mean(pushed, axis=-1, keepdims=True)
    second = jnp.mean(pushed * hat, axis=-1, keepdims=True)
    back = inverse * (pushed - first - hat * second)
    return back, jnp.sum(upstream * hat, axis=0), jnp.sum(upstream, axis=0)


def gelu(x):
    return 0.5 * x * (1.0 + lax.erf(x * math.sqrt(0.5)))


def gelu_slope(x):
    density = jnp.exp(-0.5 * x * x) * (1.0 / math.sqrt(2.0 * math.pi))
    return 0.5 * (1.0 + lax.erf(x * math.sqrt(0.5))) + x * density


def over_replicas(value):
    return lax.psum(value.astype(BF16), "rep").astype(F32)


def per_device(
    tokens,
    cotangent,
    w_qkv,
    w_out,
    w_up,
    w_down,
    ln_gain,
    ln_bias,
    positions,
    segments,
    keep_mask,
    buckets,
):
    n = lax.axis_size("shard")
    me = lax.axis_index("shard")
    own = D // n
    heads = H // n
    ff_own = w_down.shape[1]
    order = group_order("shard")

    labels = gather_tokens(jnp.stack([segments, keep_mask]).reshape(1, 2, LEN).astype(F32))
    segment, keep = labels[:, 0], labels[:, 1]
    allowed = (segment[:, :, None] == segment[:, None, :]) & (keep[:, None, :] == 1.0)
    allowed = (allowed | jnp.eye(LEN, dtype=bool)[None]).astype(F32)
    norms = jnp.stack([ln_gain, ln_bias]).reshape(1, 2, LAYERS, own, 2)
    norms = lax.all_gather(norms, "shard", axis=0, tiled=True)
    norms = norms.transpose(1, 2, 4, 0, 3).reshape(2, LAYERS, 2, D).astype(F32)
    gains, biases = norms[0], norms[1]
    all_positions = lax.all_gather(positions, "shard", axis=0, tiled=True)
    ahead = jnp.concatenate([buckets, buckets[-1:]])
    back = jnp.concatenate([buckets[::-1], buckets[:1]])
    rows_used = jnp.take(all_positions, jnp.concatenate([back, ahead]), axis=0)
    rows_ahead = rows_used[SPAN:]

    weights = []
    for layer in range(LAYERS):
        qkv_cols = by_columns(w_qkv[layer].reshape(own, 3, n, own), me)
        up_cols = by_columns(w_up[layer].reshape(own, 1, n, ff_own), me)
        weights.append((qkv_cols, w_out[layer], up_cols, w_down[layer]))

    hidden = tokens.astype(F32)
    kept = []
    for layer in range(LAYERS):
        qkv_cols, out_rows, up_cols, down_rows = weights[layer]
        hidden_all = gather_tokens(hidden.astype(BF16))
        qkv = mm(hidden_all, qkv_cols).astype(BF16)
        rel = mm(rows_used, qkv_cols[:, : 2 * own]).astype(BF16)
        context, probs = attention_forward(qkv, rel[:SPAN], allowed, heads)
        attn_sum = hidden + scatter_tokens(mm(context, out_rows))
        mid = normed(attn_sum)[0] * gains[layer, 0] + biases[layer, 0]
        mid_all = gather_tokens(mid.astype(BF16))
        pre_act = mm(mid_all, up_cols)
        activation = gelu(pre_act).astype(BF16)
        ffn_sum = mid + scatter_tokens(mm(activation, down_rows))
        hidden = normed(ffn_sum)[0] * gains[layer, 1] + biases[layer, 1]
        kept.append(
            (hidden_all, qkv, rel[SPAN:], context, probs, attn_sum, mid_all, pre_act, activation, ffn_sum)
        )
    output = hidden.astype(BF16)

    upstream = cotangent.astype(F32)
    grads = [None] * LAYERS
    small = [None] * LAYERS
    row_grads = jnp.zeros((SPAN, D), F32)
    for layer in reversed(range(LAYERS)):
        qkv_cols, out_rows, up_cols, down_rows = weights[layer]
        hidden_all, qkv, rel, context, probs, attn_sum, mid_all, pre_act, activation, ffn_sum = kept[layer]
        d_ffn, d_gain_two, d_bias_two = norm_backward(upstream, ffn_sum, gains[layer, 1])
        branch_all = gather_tokens(d_ffn.astype(BF16))
        g_down = mm_tn(activation, branch_all)
        d_pre = (mm_nt(branch_all, down_rows) * gelu_slope(pre_act)).astype(BF16)
        g_up = mm_tn(mid_all, d_pre)
        d_mid = d_ffn + scatter_tokens(mm_nt(d_pre, up_cols))
        d_attn, d_gain_one, d_bias_one = norm_backward(d_mid, attn_sum, gains[layer, 0])
        att_all = gather_tokens(d_attn.astype(BF16))
        g_out = mm_tn(context, att_all)
        d_context = mm_nt(att_all, out_rows).astype(BF16)
        d_qkv, d_rel = attention_backward(qkv, rel, probs, d_context, heads)
        d_rel = d_rel.astype(BF16)
        g_qkv = mm_tn(hidden_all, d_qkv)
        g_qkv = g_qkv.at[:, : 2 * own].add(mm_tn(rows_ahead, d_rel))
        row_grads = row_grads + mm_nt(d_rel, qkv_cols[:, : 2 * own])
        upstream = d_attn + scatter_tokens(mm_nt(d_qkv, qkv_cols))
        grads[layer] = (
            over_replicas(by_rows(g_qkv.astype(BF16), me, n, 3)),
            over_replicas(g_out),
            over_replicas(by_rows(g_up.astype(BF16), me, n, 1)),
            over_replicas(g_down),
        )
        small[layer] = (
            jnp.stack([d_gain_one, d_gain_two]),
            jnp.stack([d_bias_one, d_bias_two]),
        )

    owned_rows = positions.shape[0]
    owners = jnp.bitwise_xor(me, jnp.array(order))
    row_ids = (owners[:, None] * owned_rows + jnp.arange(owned_rows)[None, :]).reshape(-1)
    live = jnp.arange(SPAN) < 2 * LEN - 1
    picks = ((row_ids[:, None] == ahead[None, :]) & live[None, :]).astype(BF16)
    position_part = mm(picks, row_grads.astype(BF16)).reshape(n, owned_rows * D)
    norm_part = jnp.stack(
        [jnp.stack([entry[0] for entry in small]), jnp.stack([entry[1] for entry in small])]
    )
    norm_part = norm_part.reshape(2, LAYERS, 2, n, own).transpose(3, 0, 1, 2, 4)
    norm_part = jnp.take(norm_part, owners, axis=0).reshape(n, 2 * LAYERS * 2 * own)
    packed = jnp.concatenate([position_part, norm_part], axis=1)
    packed = scatter_tokens(packed)
    packed = over_replicas(packed)[0]
    grad_positions = packed[: owned_rows * D].reshape(owned_rows, D)
    norm_part = packed[owned_rows * D :].reshape(2, LAYERS, 2, own).transpose(0, 1, 3, 2)
    return (
        output,
        upstream,
        jnp.stack([entry[0] for entry in grads]),
        jnp.stack([entry[1] for entry in grads]),
        jnp.stack([entry[2] for entry in grads]),
        jnp.stack([entry[3] for entry in grads]),
        norm_part[0],
        norm_part[1],
        grad_positions,
    )


def solution(mesh):
    tokens = P(("rep", "shard"), None)
    rows = P(None, "shard", None)
    labels = P(("rep", "shard"))
    return jax.shard_map(
        per_device,
        mesh=mesh,
        in_specs=(
            tokens,
            tokens,
            rows,
            rows,
            rows,
            rows,
            rows,
            rows,
            P("shard", None),
            labels,
            labels,
            P(),
        ),
        out_specs=(tokens, tokens, rows, rows, rows, rows, rows, rows, P("shard", None)),
        check_vma=False,
    )
```

```python
from functools import partial
import math

import jax
import jax.numpy as jnp
from jax import lax
from jax.experimental import pallas as pl
from jax.experimental.pallas import tpu as pltpu
from jax.sharding import PartitionSpec as P

D = 1024
H = 16
DH = 64
LAYERS = 2
LEN = 128
SPAN = 2 * LEN
FIRST_ROW = 160
LIVE_ROWS = 192
SCALE = 1.0 / math.sqrt(3 * DH)
NEG_FILL = -1e30
NORM_EPS = 1e-07
F32 = jnp.float32
BF16 = jnp.bfloat16


def mm(a, b):
    return jnp.dot(a, b, preferred_element_type=F32)


def mm_nt(a, b):
    return lax.dot_general(a, b, (((1,), (1,)), ((), ())), preferred_element_type=F32)


def mm_tn(a, b):
    return lax.dot_general(a, b, (((0,), (0,)), ((), ())), preferred_element_type=F32)


def swap(value, axis, mask):
    size = lax.axis_size(axis)
    return lax.ppermute(value, axis, [(i, i ^ mask) for i in range(size)])


def rising_masks(axis):
    size = lax.axis_size(axis)
    masks, mask = [], 1
    while mask < size:
        masks.append(mask)
        mask *= 2
    return masks


def group_order(axis):
    order = [0]
    for mask in reversed(rising_masks(axis)):
        order = order + [place ^ mask for place in order]
    return order


def gather_tokens(rows):
    for mask in reversed(rising_masks("shard")):
        rows = jnp.concatenate([rows, swap(rows, "shard", mask)], axis=0)
    return rows


def gather_positions(positions, n, me):
    last_row = FIRST_ROW + LIVE_ROWS
    rows = positions.shape[0]
    if n != 4 or FIRST_ROW // rows != 1 or (last_row - 1) // rows != 2:
        whole = lax.all_gather(positions, "shard", axis=0, tiled=True)
        return whole[FIRST_ROW:last_row]
    size = LIVE_ROWS // 2
    mine = jnp.where(me == 1, positions[rows - size :], positions[:size])
    passed = lax.ppermute(mine, "shard", [(1, 3), (2, 0)])
    held = jnp.where((me == 1) | (me == 2), mine, passed)
    other = swap(held, "shard", 1)
    low = me % 2 == 1
    return jnp.concatenate([jnp.where(low, held, other), jnp.where(low, other, held)], axis=0)


def scatter_tokens(partial_rows):
    total = partial_rows
    for mask in rising_masks("shard"):
        half = total.shape[0] // 2
        sent = total[half:].astype(BF16)
        total = total[:half] + swap(sent, "shard", mask).astype(F32)
    return total


def by_columns(owned, me, n, parts):
    rows = owned.shape[0]
    c = owned.shape[1] // (parts * n)
    whole = jnp.zeros((n * rows, parts * c), owned.dtype)
    for mask in range(n):
        other = jnp.bitwise_xor(me, mask)
        block = [
            lax.dynamic_slice(owned, (0, (part * n + other) * c), (rows, c)) for part in range(parts)
        ]
        block = block[0] if parts == 1 else jnp.concatenate(block, axis=1)
        if mask:
            block = swap(block, "shard", mask)
        whole = lax.dynamic_update_slice(whole, block, (other * rows, 0))
    return whole


def halve(value, masks, axis):
    me = lax.axis_index("rep")
    for mask in masks:
        size = value.shape[axis] // 2
        upper = (jnp.bitwise_and(me, mask) != 0).astype(jnp.int32)
        sent = lax.dynamic_slice_in_dim(value, (1 - upper) * size, size, axis)
        held = lax.dynamic_slice_in_dim(value, upper * size, size, axis)
        value = (held.astype(F32) + swap(sent, "rep", mask).astype(F32)).astype(BF16)
    return value


def double(value, masks):
    for mask in reversed(masks[1:]):
        value = jnp.concatenate([value, swap(value, "rep", mask)], axis=0)
    return value, swap(value, "rep", masks[0])


def block_places(masks):
    reps = lax.axis_size("rep")
    order = [0]
    for mask in reversed(masks):
        order = order + [place ^ mask for place in order]
    owners = jnp.bitwise_xor(lax.axis_index("rep"), jnp.array(order, jnp.int32))
    places = jnp.zeros((reps,), jnp.int32)
    weight = reps
    for mask in masks:
        weight //= 2
        places = places + weight * (jnp.bitwise_and(owners, mask) != 0).astype(jnp.int32)
    return places


def place_kernel(parts, n, c, half, index_ref, near_ref, far_ref, *rest):
    out_ref = rest[-1]
    step = pl.program_id(0)

    def put(source):
        if n == 0:
            out_ref[0] = source[0].astype(F32)
            return
        for mask in range(n):
            start = index_ref[half * 2 + mask] * c
            for part in range(parts):
                at = pl.multiple_of(start + part * n * c, c)
                out_ref[0, :, pl.ds(at, c)] = source[0, mask, :, part * c : (part + 1) * c].astype(F32)

    @pl.when(step < half)
    def _():
        put(near_ref)

    @pl.when(step >= half)
    def _():
        put(far_ref)


def place(near, far, index, layer, out, shape, parts, n):
    half = near.shape[0]
    rows = shape[1] // (2 * half)
    block = (1,) + near.shape[1:]
    zeros = (0,) * (len(block) - 1)
    c = shape[2] // (parts * n) if n else 0
    in_specs = [
        pl.BlockSpec(block, lambda s, index: (jnp.minimum(s, half - 1),) + zeros),
        pl.BlockSpec(block, lambda s, index: (jnp.maximum(s - half, 0),) + zeros),
    ]
    operands = [index, near, far]
    aliases = {}
    if out is not None:
        in_specs.append(pl.BlockSpec(memory_space=pl.ANY))
        operands.append(out)
        aliases = {3: 0}
    return pl.pallas_call(
        partial(place_kernel, parts, n, c, half),
        grid_spec=pltpu.PrefetchScalarGridSpec(
            num_scalar_prefetch=1,
            grid=(2 * half,),
            in_specs=in_specs,
            out_specs=pl.BlockSpec((1, rows, shape[2]), lambda s, index: (layer, index[s], 0)),
        ),
        out_shape=jax.ShapeDtypeStruct(shape, F32),
        input_output_aliases=aliases,
        compiler_params=pltpu.CompilerParams(vmem_limit_bytes=24 * 1024 * 1024),
        name="place",
    )(*operands)


def reduced_rows(grad, masks, layer, out):
    rows, columns = grad.shape
    reps = lax.axis_size("rep")
    shape = (LAYERS, rows, columns)
    if (rows // reps) % 16:
        total = lax.psum(grad.astype(BF16), "rep").astype(F32)
        out = jnp.zeros(shape, F32) if out is None else out
        return out.at[layer].set(total)
    mine = halve(grad.astype(BF16), masks, 0)
    near, far = double(mine[None], masks)
    return place(near, far, block_places(masks), layer, out, shape, 1, 0)


def reduced_columns(grad, masks, layer, out, parts):
    n = lax.axis_size("shard")
    me = lax.axis_index("shard")
    reps = lax.axis_size("rep")
    rows = grad.shape[0] // n
    c = grad.shape[1] // parts
    shape = (LAYERS, rows, parts * n * c)
    grad = grad.astype(BF16).reshape(n, rows, parts * c)
    exact = (rows // reps) % 16 == 0 and c % 128 == 0
    if exact:
        grad = halve(grad, masks, 1)
    blocks = []
    for mask in range(n):
        block = lax.dynamic_index_in_dim(grad, jnp.bitwise_xor(me, mask), 0, keepdims=False)
        blocks.append(swap(block, "shard", mask) if mask else block)
    blocks = jnp.stack(blocks)
    others = jnp.bitwise_xor(me, jnp.arange(n, dtype=jnp.int32))
    if exact:
        near, far = double(blocks[None], masks)
        index = jnp.concatenate([block_places(masks), others])
        return place(near, far, index, layer, out, shape, parts, n)
    total = lax.psum(jnp.take(blocks, others, axis=0), "rep").astype(F32)
    total = total.reshape(n, rows, parts, c).transpose(1, 2, 0, 3).reshape(rows, parts * n * c)
    out = jnp.zeros(shape, F32) if out is None else out
    return out.at[layer].set(total)


def attention_forward_kernel(heads, qkv_ref, rel_ref, allowed_ref, context_ref, probs_ref):
    width = heads * DH
    allowed = allowed_ref[0] > 0
    for head in range(heads):
        at = head * DH
        q = qkv_ref[:, at : at + DH]
        k = qkv_ref[:, width + at : width + at + DH]
        v = qkv_ref[:, 2 * width + at : 2 * width + at + DH]
        rel_q = rel_ref[:, at : at + DH]
        rel_k = rel_ref[:, width + at : width + at + DH]
        by_key = pltpu.roll(mm_nt(q, rel_k), LEN + 1, 1, stride=1, stride_axis=0)[:, :LEN]
        by_query = pltpu.roll(mm_nt(k, rel_q), LEN + 1, 1, stride=1, stride_axis=0)[:, :LEN]
        scores = (mm_nt(q, k) + by_key + by_query.T) * SCALE
        masked = jnp.where(allowed, scores, NEG_FILL)
        terms = jnp.exp(masked - jnp.max(masked, axis=1, keepdims=True))
        probs = terms / jnp.sum(terms, axis=1, keepdims=True)
        probs_ref[0, head] = probs
        context_ref[:, at : at + DH] = mm(probs.astype(BF16), v).astype(BF16)


def attention_forward(qkv, rel_back, allowed, heads):
    count = allowed.shape[0]
    width = heads * DH
    return pl.pallas_call(
        partial(attention_forward_kernel, heads),
        grid=(count,),
        in_specs=[
            pl.BlockSpec((LEN, 3 * width), lambda s: (s, 0)),
            pl.BlockSpec((SPAN, 2 * width), lambda s: (0, 0)),
            pl.BlockSpec((1, LEN, LEN), lambda s: (s, 0, 0)),
        ],
        out_specs=[
            pl.BlockSpec((LEN, width), lambda s: (s, 0)),
            pl.BlockSpec((1, heads, LEN, LEN), lambda s: (s, 0, 0, 0)),
        ],
        out_shape=[
            jax.ShapeDtypeStruct((count * LEN, width), BF16),
            jax.ShapeDtypeStruct((count, heads, LEN, LEN), F32),
        ],
        compiler_params=pltpu.CompilerParams(vmem_limit_bytes=24 * 1024 * 1024),
        name="attention_forward",
    )(qkv, rel_back, allowed)


def attention_backward_kernel(heads, qkv_ref, rel_ref, probs_ref, grad_ref, dqkv_ref, drel_ref):
    width = heads * DH

    @pl.when(pl.program_id(0) == 0)
    def _():
        drel_ref[...] = jnp.zeros_like(drel_ref)

    row = lax.broadcasted_iota(jnp.int32, (LEN, LEN), 0)
    column = lax.broadcasted_iota(jnp.int32, (LEN, LEN), 1)
    flip = jnp.where(row + column == LEN - 1, 1.0, 0.0).astype(BF16)
    blank = jnp.zeros((LEN, LEN), F32)

    def spread(flipped):
        wide = jnp.concatenate([flipped, blank], axis=1)
        return pltpu.roll(wide, 0, 1, stride=1, stride_axis=0).astype(BF16)

    for head in range(heads):
        at = head * DH
        q = qkv_ref[:, at : at + DH]
        k = qkv_ref[:, width + at : width + at + DH]
        v = qkv_ref[:, 2 * width + at : 2 * width + at + DH]
        rel_q = rel_ref[:, at : at + DH]
        rel_k = rel_ref[:, width + at : width + at + DH]
        grad = grad_ref[:, at : at + DH]
        probs = probs_ref[0, head]
        d_value = mm_tn(probs.astype(BF16), grad)
        d_probs = mm_nt(grad, v)
        inner = jnp.sum(d_probs * probs, axis=1, keepdims=True)
        d_scores = (probs * (d_probs - inner)).astype(BF16)
        key_side = spread(mm(d_scores, flip))
        query_side = spread(mm_tn(d_scores, flip))
        d_query = (mm(d_scores, k) + mm(key_side, rel_k)) * SCALE
        d_key = (mm_tn(d_scores, q) + mm(query_side, rel_q)) * SCALE
        dqkv_ref[:, at : at + DH] = d_query.astype(BF16)
        dqkv_ref[:, width + at : width + at + DH] = d_key.astype(BF16)
        dqkv_ref[:, 2 * width + at : 2 * width + at + DH] = d_value.astype(BF16)
        drel_ref[:, at : at + DH] += mm_tn(query_side, k) * SCALE
        drel_ref[:, width + at : width + at + DH] += mm_tn(key_side, q) * SCALE


def attention_backward(qkv, rel_ahead, probs, d_context, heads):
    count = probs.shape[0]
    width = heads * DH
    return pl.pallas_call(
        partial(attention_backward_kernel, heads),
        grid=(count,),
        in_specs=[
            pl.BlockSpec((LEN, 3 * width), lambda s: (s, 0)),
            pl.BlockSpec((SPAN, 2 * width), lambda s: (0, 0)),
            pl.BlockSpec((1, heads, LEN, LEN), lambda s: (s, 0, 0, 0)),
            pl.BlockSpec((LEN, width), lambda s: (s, 0)),
        ],
        out_specs=[
            pl.BlockSpec((LEN, 3 * width), lambda s: (s, 0)),
            pl.BlockSpec((SPAN, 2 * width), lambda s: (0, 0)),
        ],
        out_shape=[
            jax.ShapeDtypeStruct((count * LEN, 3 * width), BF16),
            jax.ShapeDtypeStruct((SPAN, 2 * width), F32),
        ],
        compiler_params=pltpu.CompilerParams(vmem_limit_bytes=24 * 1024 * 1024),
        name="attention_backward",
    )(qkv, rel_ahead, probs, d_context)


def normed(values):
    centre = values - jnp.mean(values, axis=-1, keepdims=True)
    inverse = lax.rsqrt(jnp.mean(centre * centre, axis=-1, keepdims=True) + NORM_EPS)
    return centre * inverse, inverse


def norm_backward(upstream, values, gain):
    hat, inverse = normed(values)
    pushed = upstream * gain
    first = jnp.mean(pushed, axis=-1, keepdims=True)
    second = jnp.mean(pushed * hat, axis=-1, keepdims=True)
    back = inverse * (pushed - first - hat * second)
    return back, jnp.sum(upstream * hat, axis=0), jnp.sum(upstream, axis=0)


def gelu(x):
    return 0.5 * x * (1.0 + lax.erf(x * math.sqrt(0.5)))


def gelu_slope(x):
    density = jnp.exp(-0.5 * x * x) * (1.0 / math.sqrt(2.0 * math.pi))
    return 0.5 * (1.0 + lax.erf(x * math.sqrt(0.5))) + x * density


def per_device(
    tokens,
    cotangent,
    w_qkv,
    w_out,
    w_up,
    w_down,
    ln_gain,
    ln_bias,
    positions,
    segments,
    keep_mask,
    buckets,
):
    n = lax.axis_size("shard")
    me = lax.axis_index("shard")
    own = D // n
    heads = H // n
    order = group_order("shard")

    small_part = jnp.concatenate(
        [
            segments.astype(F32),
            keep_mask.astype(F32),
            jnp.stack([ln_gain, ln_bias]).transpose(0, 1, 3, 2).astype(F32).reshape(-1),
        ]
    )
    small_all = gather_tokens(small_part[None])
    segment, keep = small_all[:, :LEN], small_all[:, LEN : 2 * LEN]
    allowed = (segment[:, :, None] == segment[:, None, :]) & (keep[:, None, :] == 1.0)
    allowed = (allowed | jnp.eye(LEN, dtype=bool)[None]).astype(F32)
    places = [order.index(place) for place in range(n)]
    places = jnp.take(jnp.array(places), jnp.bitwise_xor(me, jnp.arange(n)))
    norms = jnp.take(small_all[:, 2 * LEN :], places, axis=0).reshape(n, 2, LAYERS, 2, own)
    norms = norms.transpose(1, 2, 3, 0, 4).reshape(2, LAYERS, 2, D)
    gains, biases = norms[0], norms[1]
    live_rows = gather_positions(positions, n, me)
    ahead = jnp.concatenate([buckets, buckets[-1:]])
    back = jnp.concatenate([buckets[::-1], buckets[:1]])
    wanted = jnp.concatenate([back, ahead]) - FIRST_ROW
    picks = (wanted[:, None] == jnp.arange(LIVE_ROWS)[None, :]).astype(BF16)
    rows_used = mm(picks, live_rows).astype(BF16)
    rows_ahead = rows_used[SPAN:]

    weights = []
    for layer in range(LAYERS):
        qkv_cols = by_columns(w_qkv[layer], me, n, 3)
        up_cols = by_columns(w_up[layer], me, n, 1)
        weights.append((qkv_cols, w_out[layer], up_cols, w_down[layer]))

    hidden = tokens.astype(F32)
    kept = []
    for layer in range(LAYERS):
        qkv_cols, out_rows, up_cols, down_rows = weights[layer]
        hidden_all = gather_tokens(hidden.astype(BF16))
        qkv = mm(hidden_all, qkv_cols).astype(BF16)
        rel = mm(rows_used, qkv_cols[:, : 2 * own]).astype(BF16)
        context, probs = attention_forward(qkv, rel[:SPAN], allowed, heads)
        attn_sum = hidden + scatter_tokens(mm(context, out_rows))
        mid = normed(attn_sum)[0] * gains[layer, 0] + biases[layer, 0]
        mid_all = gather_tokens(mid.astype(BF16))
        pre_act = mm(mid_all, up_cols)
        activation = gelu(pre_act).astype(BF16)
        ffn_sum = mid + scatter_tokens(mm(activation, down_rows))
        hidden = normed(ffn_sum)[0] * gains[layer, 1] + biases[layer, 1]
        kept.append(
            (hidden_all, qkv, rel[SPAN:], context, probs, attn_sum, mid_all, pre_act, activation, ffn_sum)
        )
    output = hidden.astype(BF16)

    upstream = cotangent.astype(F32)
    out_grads = [None] * 4
    masks = rising_masks("rep")
    small = [None] * LAYERS
    row_grads = jnp.zeros((SPAN, D), F32)
    for layer in reversed(range(LAYERS)):
        qkv_cols, out_rows, up_cols, down_rows = weights[layer]
        hidden_all, qkv, rel, context, probs, attn_sum, mid_all, pre_act, activation, ffn_sum = kept[layer]
        d_ffn, d_gain_two, d_bias_two = norm_backward(upstream, ffn_sum, gains[layer, 1])
        branch_all = gather_tokens(d_ffn.astype(BF16))
        g_down = mm_tn(activation, branch_all)
        d_pre = (mm_nt(branch_all, down_rows) * gelu_slope(pre_act)).astype(BF16)
        g_up = mm_tn(mid_all, d_pre)
        d_mid = d_ffn + scatter_tokens(mm_nt(d_pre, up_cols))
        d_attn, d_gain_one, d_bias_one = norm_backward(d_mid, attn_sum, gains[layer, 0])
        att_all = gather_tokens(d_attn.astype(BF16))
        g_out = mm_tn(context, att_all)
        d_context = mm_nt(att_all, out_rows).astype(BF16)
        d_qkv, d_rel = attention_backward(qkv, rel, probs, d_context, heads)
        d_rel = d_rel.astype(BF16)
        g_qkv = mm_tn(hidden_all, d_qkv)
        g_qkv = g_qkv.at[:, : 2 * own].add(mm_tn(rows_ahead, d_rel))
        row_grads = row_grads + mm_nt(d_rel, qkv_cols[:, : 2 * own])
        upstream = d_attn + scatter_tokens(mm_nt(d_qkv, qkv_cols))
        out_grads[0] = reduced_columns(g_qkv, masks, layer, out_grads[0], 3)
        out_grads[1] = reduced_rows(g_out, masks, layer, out_grads[1])
        out_grads[2] = reduced_columns(g_up, masks, layer, out_grads[2], 1)
        out_grads[3] = reduced_rows(g_down, masks, layer, out_grads[3])
        small[layer] = (
            jnp.stack([d_gain_one, d_gain_two]),
            jnp.stack([d_bias_one, d_bias_two]),
        )

    owned_rows = positions.shape[0]
    owners = jnp.bitwise_xor(me, jnp.array(order))
    row_ids = (owners[:, None] * owned_rows + jnp.arange(owned_rows)[None, :]).reshape(-1)
    live = jnp.arange(SPAN) < 2 * LEN - 1
    picks = ((row_ids[:, None] == ahead[None, :]) & live[None, :]).astype(BF16)
    position_part = mm(picks, row_grads.astype(BF16)).reshape(n, owned_rows * D)
    norm_part = jnp.stack(
        [jnp.stack([entry[0] for entry in small]), jnp.stack([entry[1] for entry in small])]
    )
    norm_part = norm_part.reshape(2, LAYERS, 2, n, own).transpose(3, 0, 1, 2, 4)
    norm_part = jnp.take(norm_part, owners, axis=0).reshape(n, 2 * LAYERS * 2 * own)
    packed = jnp.concatenate([position_part, norm_part], axis=1)
    packed = scatter_tokens(packed).astype(BF16)[0]
    near, far = double(halve(packed, masks, 0)[None], masks)
    packed = jnp.concatenate([near, far], axis=0)
    packed = jnp.zeros_like(packed).at[block_places(masks)].set(packed).reshape(-1).astype(F32)
    grad_positions = packed[: owned_rows * D].reshape(owned_rows, D)
    norm_part = packed[owned_rows * D :].reshape(2, LAYERS, 2, own).transpose(0, 1, 3, 2)
    return (
        output,
        upstream,
        *out_grads,
        norm_part[0],
        norm_part[1],
        grad_positions,
    )


def solution(mesh):
    tokens = P(("rep", "shard"), None)
    rows = P(None, "shard", None)
    labels = P(("rep", "shard"))
    return jax.shard_map(
        per_device,
        mesh=mesh,
        in_specs=(
            tokens,
            tokens,
            rows,
            rows,
            rows,
            rows,
            rows,
            rows,
            P("shard", None),
            labels,
            labels,
            P(),
        ),
        out_specs=(tokens, tokens, rows, rows, rows, rows, rows, rows, P("shard", None)),
        check_vma=False,
    )
```

```python
from functools import partial
import math

import jax
import jax.numpy as jnp
from jax import lax
from jax.experimental import pallas as pl
from jax.experimental.pallas import tpu as pltpu
from jax.sharding import PartitionSpec as P

D = 1024
H = 16
DH = 64
LAYERS = 2
LEN = 128
SPAN = 2 * LEN
FIRST_ROW = 160
LIVE_ROWS = 192
SCALE = 1.0 / math.sqrt(3 * DH)
NEG_FILL = -1e30
NORM_EPS = 1e-07
F32 = jnp.float32
BF16 = jnp.bfloat16


def mm(a, b):
    return jnp.dot(a, b, preferred_element_type=F32)


def mm_nt(a, b):
    return lax.dot_general(a, b, (((1,), (1,)), ((), ())), preferred_element_type=F32)


def mm_tn(a, b):
    return lax.dot_general(a, b, (((0,), (0,)), ((), ())), preferred_element_type=F32)


def swap(value, axis, mask):
    size = lax.axis_size(axis)
    return lax.ppermute(value, axis, [(i, i ^ mask) for i in range(size)])


def far_order(n):
    span, mask = [0], n // 2
    while mask > 1:
        span = span + [place ^ mask for place in span]
        mask //= 2
    return span[1:]


def group_order(n):
    far = far_order(n)
    return [0, 1] + far + [place ^ 1 for place in far]


def gather_sides(own):
    n = lax.axis_size("shard")
    near = jnp.concatenate([own, swap(own, "shard", 1)], axis=0)
    span, mask = own, n // 2
    while mask > 1:
        passed = swap(span, "shard", mask)
        span = passed if mask == 2 and n == 4 else jnp.concatenate([span, passed], axis=0)
        mask //= 2
    far = span if n == 4 else span[own.shape[0] :]
    return near, jnp.concatenate([far, swap(far, "shard", 1)], axis=0)


def gather_group(own):
    return jnp.concatenate(gather_sides(own), axis=0)


def scatter_positions(row_grads, ahead, rows, n, me):
    live = jnp.arange(SPAN) < SPAN - 1
    if n == 4 and rows == 128:
        wanted = FIRST_ROW + jnp.arange(LIVE_ROWS)
    else:
        owners = jnp.bitwise_xor(me, jnp.array(group_order(n)))
        wanted = (owners[:, None] * rows + jnp.arange(rows)[None, :]).reshape(-1)
    picks = ((wanted[:, None] == ahead[None, :]) & live[None, :]).astype(BF16)
    by_row = mm(picks, row_grads.astype(BF16))
    if n != 4 or rows != 128:
        return scatter_sides(by_row[: 2 * rows], by_row[2 * rows :])
    size = LIVE_ROWS // 2
    odd = me % 2 == 1
    mine = jnp.where(odd, by_row[:size], by_row[size:])
    total = mine + swap(jnp.where(odd, by_row[size:], by_row[:size]).astype(BF16), "shard", 1).astype(F32)
    return total + swap(total.astype(BF16), "shard", 2).astype(F32)


def scatter_sides(near, far):
    n = lax.axis_size("shard")
    half = far.shape[0] // 2
    far = far[:half] + swap(far[half:].astype(BF16), "shard", 1).astype(F32)
    half = near.shape[0] // 2
    near = near[:half] + swap(near[half:].astype(BF16), "shard", 1).astype(F32)
    if n == 4:
        return near + swap(far.astype(BF16), "shard", 2).astype(F32)
    total, mask = jnp.concatenate([near, far], axis=0), 2
    while mask < n:
        half = total.shape[0] // 2
        total = total[:half] + swap(total[half:].astype(BF16), "shard", mask).astype(F32)
        mask *= 2
    return total


def gather_positions(positions, n, me):
    last_row = FIRST_ROW + LIVE_ROWS
    rows = positions.shape[0]
    if n != 4 or rows != 128:
        whole = lax.all_gather(positions, "shard", axis=0, tiled=True)
        return whole[FIRST_ROW:last_row]
    size = LIVE_ROWS // 2
    mine = jnp.where(me == 1, positions[rows - size :], positions[:size])
    passed = lax.ppermute(mine, "shard", [(1, 3), (2, 0)])
    held = jnp.where((me == 1) | (me == 2), mine, passed)
    other = swap(held, "shard", 1)
    low = me % 2 == 1
    return jnp.concatenate([jnp.where(low, held, other), jnp.where(low, other, held)], axis=0)


def copy_blocks_kernel(n, me_ref, *refs):
    for source, target in zip(refs[:n], refs[n:]):
        target[...] = source[0]


def deal(weight, layer, me, n, parts):
    rows = weight.shape[1]
    c = weight.shape[2] // (parts * n)
    if c % 128:
        blocks = []
        for mask in range(n):
            other = jnp.bitwise_xor(me, mask)
            pieces = [
                lax.dynamic_slice(weight, (layer, 0, (part * n + other) * c), (1, rows, c))[0]
                for part in range(parts)
            ]
            blocks.append(jnp.concatenate(pieces, axis=1))
        return blocks
    split = 1 if parts > 1 or c % 512 else 4

    def source_spec(mask):
        def where(part, cut, me):
            return (layer, 0, (part * n + jnp.bitwise_xor(me[0], mask)) * split + cut)

        return pl.BlockSpec((1, rows, c // split), where)

    target = pl.BlockSpec((rows, c // split), lambda part, cut, me: (0, part * split + cut))
    return pl.pallas_call(
        partial(copy_blocks_kernel, n),
        grid_spec=pltpu.PrefetchScalarGridSpec(
            num_scalar_prefetch=1,
            grid=(parts, split),
            in_specs=[source_spec(mask) for mask in range(n)],
            out_specs=[target] * n,
        ),
        out_shape=[jax.ShapeDtypeStruct((rows, parts * c), BF16)] * n,
        compiler_params=pltpu.CompilerParams(vmem_limit_bytes=24 * 1024 * 1024),
        name="deal",
    )(me.reshape(1), *([weight] * n))


def collect_kernel(n, me_ref, *refs):
    step = pl.program_id(1)
    for mask in range(n):

        @pl.when(step == jnp.bitwise_xor(me_ref[0], mask))
        def _():
            refs[n][...] = refs[mask][...]


def collect(blocks, me, n):
    rows, width = blocks[0].shape
    if rows % 16 or width % 256:
        whole = jnp.zeros((n * rows, width), BF16)
        for mask, block in enumerate(blocks):
            other = jnp.bitwise_xor(me, mask)
            whole = lax.dynamic_update_slice(whole, block, (other * rows, 0))
        return whole
    c = width // 2
    return pl.pallas_call(
        partial(collect_kernel, n),
        grid_spec=pltpu.PrefetchScalarGridSpec(
            num_scalar_prefetch=1,
            grid=(width // c, n),
            in_specs=[pl.BlockSpec((rows, c), lambda cut, step, me: (0, cut))] * n,
            out_specs=pl.BlockSpec((rows, c), lambda cut, step, me: (step, cut)),
        ),
        out_shape=jax.ShapeDtypeStruct((n * rows, width), BF16),
        compiler_params=pltpu.CompilerParams(vmem_limit_bytes=24 * 1024 * 1024),
        name="collect",
    )(me.reshape(1), *blocks)


def passed_around(blocks, n):
    return [swap(block, "shard", mask) if mask else block for mask, block in enumerate(blocks)]


def to_owners(columns, me, n):
    blocks = []
    for mask in range(n):
        block = lax.dynamic_index_in_dim(columns, jnp.bitwise_xor(me, mask), 0, keepdims=False)
        blocks.append(swap(block, "shard", mask) if mask else block)
    return jnp.stack(blocks)


def tie(value, after):
    return lax.optimization_barrier((value, after))[0]


INWARDS = [(0, 2), (1, 3), (6, 4), (7, 5)]
ACROSS = [(2, 4), (3, 5), (4, 2), (5, 3)]
OUTWARDS = [(2, 0), (3, 1), (4, 6), (5, 7)]


def line_stages(value):
    rep = lax.axis_index("rep")
    for pairs in (INWARDS, ACROSS):
        passed = yield value, lax.ppermute(value, "rep", pairs)
        value = (value.astype(F32) + passed.astype(F32)).astype(BF16)
    passed = yield value, lax.ppermute(value, "rep", OUTWARDS)
    return jnp.where((rep >= 2) & (rep < 6), value, passed)


def halves_of(grads, upper):
    pieces = []
    for grad in grads:
        size = grad.shape[-2] // 2
        pieces.append(lax.dynamic_slice_in_dim(grad, upper * size, size, grad.ndim - 2))
    return pieces[0] if len(pieces) == 1 else jnp.concatenate(pieces, axis=0)


def half_stages(grads):
    upper = lax.axis_index("rep") % 2
    me = lax.axis_index("shard")
    sent = halves_of(grads, 1 - upper)
    held = halves_of(grads, upper)
    passed = yield sent, swap(sent, "rep", 1)
    value = (held.astype(F32) + passed.astype(F32)).astype(BF16)
    value = yield from line_stages(value)
    if value.ndim == 3:
        blocks = []
        for mask in range(value.shape[0]):
            other = jnp.bitwise_xor(me, mask)
            blocks.append(lax.dynamic_index_in_dim(value, other, 0, keepdims=False))
        moved = [swap(block, "shard", mask) if mask else block for mask, block in enumerate(blocks)]
        blocks = yield blocks, moved
        value = jnp.stack(blocks)
    far = yield value, swap(value, "rep", 1)
    return value, far


class Sums:
    def __init__(self, index, shapes):
        self.index, self.shapes = index, shapes
        self.outs = [None] * len(shapes)
        self.stages, self.moving, self.results = {}, {}, {}
        self.last, self.placed = (), None

    def ordered(self, value):
        out = () if self.placed is None else self.outs[self.placed]
        value, _, out = lax.optimization_barrier((value, self.last, out))
        if self.placed is not None:
            self.outs[self.placed] = out
            self.placed = None
        return value

    def start(self, name, *grads):
        grads = self.ordered([grad.astype(BF16) for grad in grads])
        self.stages[name] = half_stages(grads)
        self.last, self.moving[name] = next(self.stages[name])

    def step(self, *names):
        for name in names:
            moving = self.ordered(self.moving.pop(name))
            try:
                self.last, self.moving[name] = self.stages[name].send(moving)
            except StopIteration as stop:
                self.results[name] = stop.value

    def place(self, total, which, layer, parts, n, offset=0):
        shape, out = self.shapes[which], self.outs[which]
        total = self.ordered(total)
        if isinstance(total, tuple):
            out = place(total, self.index, layer, out, shape, parts, n, offset)
        else:
            out = place_whole(total, self.index, layer, out, shape, parts, n)
        self.outs[which], self.placed = out, which


def place_kernel(parts, n, c, steps, index_ref, near_ref, far_ref, *rest):
    out_ref = rest[-1]

    def put(source):
        if n == 0:
            out_ref[0] = source[...].astype(F32)
            return
        for mask in range(n):
            for part in range(parts):
                at = pl.multiple_of(index_ref[1 + mask] * c + part * n * c, c)
                out_ref[0, :, pl.ds(at, c)] = source[mask, :, part * c : (part + 1) * c].astype(F32)

    @pl.when(pl.program_id(0) < steps)
    def _():
        put(near_ref)

    @pl.when(pl.program_id(0) >= steps)
    def _():
        put(far_ref)


def place(halves, index, layer, out, shape, parts, n, offset):
    size = shape[1] // 2
    rows = size // 4 if size % 64 == 0 else size
    steps, skip = size // rows, offset // rows
    c = shape[2] // (parts * n) if n else 0
    lead = (n,) if n else ()
    block = lead + (rows, parts * c if n else shape[2])
    zeros = (0,) * len(lead)

    def target(s, index):
        first = index[0] * steps + s
        second = (1 - index[0]) * steps + s - steps
        return (layer, jnp.where(s < steps, first, second), 0)

    in_specs = [
        pl.BlockSpec(block, lambda s, index: zeros + (skip + jnp.minimum(s, steps - 1), 0)),
        pl.BlockSpec(block, lambda s, index: zeros + (skip + jnp.maximum(s - steps, 0), 0)),
    ]
    operands = [index, *halves]
    aliases = {}
    if out is not None:
        in_specs.append(pl.BlockSpec(memory_space=pl.ANY))
        operands.append(out)
        aliases = {3: 0}
    return pl.pallas_call(
        partial(place_kernel, parts, n, c, steps),
        grid_spec=pltpu.PrefetchScalarGridSpec(
            num_scalar_prefetch=1,
            grid=(2 * steps,),
            in_specs=in_specs,
            out_specs=pl.BlockSpec((1, rows, shape[2]), target),
        ),
        out_shape=jax.ShapeDtypeStruct(shape, F32),
        input_output_aliases=aliases,
        compiler_params=pltpu.CompilerParams(vmem_limit_bytes=32 * 1024 * 1024),
        name="place",
    )(*operands)


def place_whole_kernel(parts, n, c, index_ref, blocks_ref, *rest):
    out_ref = rest[-1]
    if n == 0:
        out_ref[0] = blocks_ref[...].astype(F32)
        return
    for mask in range(n):
        for part in range(parts):
            at = pl.multiple_of(index_ref[1 + mask] * c + part * n * c, c)
            out_ref[0, :, pl.ds(at, c)] = blocks_ref[mask, :, part * c : (part + 1) * c].astype(F32)


def place_whole(blocks, index, layer, out, shape, parts, n):
    rows = shape[1] // 8
    c = shape[2] // (parts * n) if n else 0
    lead = (n,) if n else ()
    zeros = (0,) * len(lead)
    block = lead + (rows, parts * c if n else shape[2])
    in_specs = [pl.BlockSpec(block, lambda s, index: zeros + (s, 0))]
    operands, aliases = [index, blocks], {}
    if out is not None:
        in_specs.append(pl.BlockSpec(memory_space=pl.ANY))
        operands.append(out)
        aliases = {2: 0}
    return pl.pallas_call(
        partial(place_whole_kernel, parts, n, c),
        grid_spec=pltpu.PrefetchScalarGridSpec(
            num_scalar_prefetch=1,
            grid=(shape[1] // rows,),
            in_specs=in_specs,
            out_specs=pl.BlockSpec((1, rows, shape[2]), lambda s, index: (layer, s, 0)),
        ),
        out_shape=jax.ShapeDtypeStruct(shape, F32),
        input_output_aliases=aliases,
        compiler_params=pltpu.CompilerParams(vmem_limit_bytes=32 * 1024 * 1024),
        name="place_whole",
    )(*operands)


def put_layer(total, layer, out, shape):
    out = jnp.zeros(shape, F32) if out is None else out
    return out.at[layer].set(total.astype(F32))


def attention_forward_kernel(heads, qkv_ref, rel_ref, allowed_ref, context_ref, probs_ref):
    width = heads * DH
    allowed = allowed_ref[0] > 0
    for head in range(heads):
        at = head * DH
        q = qkv_ref[:, at : at + DH]
        k = qkv_ref[:, width + at : width + at + DH]
        v = qkv_ref[:, 2 * width + at : 2 * width + at + DH]
        rel_q = rel_ref[:, at : at + DH]
        rel_k = rel_ref[:, width + at : width + at + DH]
        by_key = pltpu.roll(mm_nt(q, rel_k), LEN + 1, 1, stride=1, stride_axis=0)[:, :LEN]
        by_query = pltpu.roll(mm_nt(k, rel_q), LEN + 1, 1, stride=1, stride_axis=0)[:, :LEN]
        scores = (mm_nt(q, k) + by_key + by_query.T) * SCALE
        masked = jnp.where(allowed, scores, NEG_FILL)
        terms = jnp.exp(masked - jnp.max(masked, axis=1, keepdims=True))
        probs = terms / jnp.sum(terms, axis=1, keepdims=True)
        probs_ref[0, head] = probs
        context_ref[:, at : at + DH] = mm(probs.astype(BF16), v).astype(BF16)


def attention_forward(qkv, rel_back, allowed, heads):
    count = allowed.shape[0]
    width = heads * DH
    return pl.pallas_call(
        partial(attention_forward_kernel, heads),
        grid=(count,),
        in_specs=[
            pl.BlockSpec((LEN, 3 * width), lambda s: (s, 0)),
            pl.BlockSpec((SPAN, 2 * width), lambda s: (0, 0)),
            pl.BlockSpec((1, LEN, LEN), lambda s: (s, 0, 0)),
        ],
        out_specs=[
            pl.BlockSpec((LEN, width), lambda s: (s, 0)),
            pl.BlockSpec((1, heads, LEN, LEN), lambda s: (s, 0, 0, 0)),
        ],
        out_shape=[
            jax.ShapeDtypeStruct((count * LEN, width), BF16),
            jax.ShapeDtypeStruct((count, heads, LEN, LEN), F32),
        ],
        compiler_params=pltpu.CompilerParams(vmem_limit_bytes=24 * 1024 * 1024),
        name="attention_forward",
    )(qkv, rel_back, allowed)


def attention_backward_kernel(heads, qkv_ref, rel_ref, probs_ref, grad_ref, dqkv_ref, drel_ref):
    width = heads * DH

    @pl.when(pl.program_id(0) == 0)
    def _():
        drel_ref[...] = jnp.zeros_like(drel_ref)

    row = lax.broadcasted_iota(jnp.int32, (LEN, LEN), 0)
    column = lax.broadcasted_iota(jnp.int32, (LEN, LEN), 1)
    flip = jnp.where(row + column == LEN - 1, 1.0, 0.0).astype(BF16)
    blank = jnp.zeros((LEN, LEN), F32)

    def spread(flipped):
        wide = jnp.concatenate([flipped, blank], axis=1)
        return pltpu.roll(wide, 0, 1, stride=1, stride_axis=0).astype(BF16)

    for head in range(heads):
        at = head * DH
        q = qkv_ref[:, at : at + DH]
        k = qkv_ref[:, width + at : width + at + DH]
        v = qkv_ref[:, 2 * width + at : 2 * width + at + DH]
        rel_q = rel_ref[:, at : at + DH]
        rel_k = rel_ref[:, width + at : width + at + DH]
        grad = grad_ref[:, at : at + DH]
        probs = probs_ref[0, head]
        d_value = mm_tn(probs.astype(BF16), grad)
        d_probs = mm_nt(grad, v)
        inner = jnp.sum(d_probs * probs, axis=1, keepdims=True)
        d_scores = (probs * (d_probs - inner)).astype(BF16)
        key_side = spread(mm(d_scores, flip))
        query_side = spread(mm_tn(d_scores, flip))
        d_query = (mm(d_scores, k) + mm(key_side, rel_k)) * SCALE
        d_key = (mm_tn(d_scores, q) + mm(query_side, rel_q)) * SCALE
        dqkv_ref[:, at : at + DH] = d_query.astype(BF16)
        dqkv_ref[:, width + at : width + at + DH] = d_key.astype(BF16)
        dqkv_ref[:, 2 * width + at : 2 * width + at + DH] = d_value.astype(BF16)
        drel_ref[:, at : at + DH] += mm_tn(query_side, k) * SCALE
        drel_ref[:, width + at : width + at + DH] += mm_tn(key_side, q) * SCALE


def attention_backward(qkv, rel_ahead, probs, d_context, heads):
    count = probs.shape[0]
    width = heads * DH
    return pl.pallas_call(
        partial(attention_backward_kernel, heads),
        grid=(count,),
        in_specs=[
            pl.BlockSpec((LEN, 3 * width), lambda s: (s, 0)),
            pl.BlockSpec((SPAN, 2 * width), lambda s: (0, 0)),
            pl.BlockSpec((1, heads, LEN, LEN), lambda s: (s, 0, 0, 0)),
            pl.BlockSpec((LEN, width), lambda s: (s, 0)),
        ],
        out_specs=[
            pl.BlockSpec((LEN, 3 * width), lambda s: (s, 0)),
            pl.BlockSpec((SPAN, 2 * width), lambda s: (0, 0)),
        ],
        out_shape=[
            jax.ShapeDtypeStruct((count * LEN, 3 * width), BF16),
            jax.ShapeDtypeStruct((SPAN, 2 * width), F32),
        ],
        compiler_params=pltpu.CompilerParams(vmem_limit_bytes=24 * 1024 * 1024),
        name="attention_backward",
    )(qkv, rel_ahead, probs, d_context)


def normed(values):
    centre = values - jnp.mean(values, axis=-1, keepdims=True)
    inverse = lax.rsqrt(jnp.mean(centre * centre, axis=-1, keepdims=True) + NORM_EPS)
    return centre * inverse, inverse


def norm_backward(upstream, values, gain):
    hat, inverse = normed(values)
    pushed = upstream * gain
    first = jnp.mean(pushed, axis=-1, keepdims=True)
    second = jnp.mean(pushed * hat, axis=-1, keepdims=True)
    back = inverse * (pushed - first - hat * second)
    return back, jnp.sum(upstream * hat, axis=0), jnp.sum(upstream, axis=0)


def gelu(x):
    return 0.5 * x * (1.0 + lax.erf(x * math.sqrt(0.5)))


def gelu_slope(x):
    density = jnp.exp(-0.5 * x * x) * (1.0 / math.sqrt(2.0 * math.pi))
    return 0.5 * (1.0 + lax.erf(x * math.sqrt(0.5))) + x * density


def per_device(
    tokens,
    cotangent,
    w_qkv,
    w_out,
    w_up,
    w_down,
    ln_gain,
    ln_bias,
    positions,
    segments,
    keep_mask,
    buckets,
):
    n = lax.axis_size("shard")
    me = lax.axis_index("shard")
    own = D // n
    heads = H // n
    order = group_order(n)

    qkv_blocks = deal(w_qkv, 0, me, n, 3)
    up_blocks = deal(w_up, 0, me, n, 1)
    hidden = tokens.astype(F32)
    small_part = jnp.concatenate(
        [
            segments.astype(BF16),
            keep_mask.astype(BF16),
            jnp.stack([ln_gain, ln_bias]).transpose(0, 1, 3, 2).reshape(-1),
        ]
    )
    small_count = small_part.shape[0]
    small_part = jnp.pad(small_part, (0, 16 * D - small_count)).reshape(16, D)
    sides = gather_sides(jnp.concatenate([tokens, small_part], axis=0))
    sides = [side.reshape(-1, LEN + 16, D) for side in sides]
    hidden_sides = [side[:, :LEN].reshape(-1, D) for side in sides]
    small_all = jnp.concatenate([side[:, LEN:] for side in sides], axis=0)
    small_all = small_all.reshape(n, 16 * D)[:, :small_count].astype(F32)
    segment, keep = small_all[:, :LEN], small_all[:, LEN : 2 * LEN]
    allowed = (segment[:, :, None] == segment[:, None, :]) & (keep[:, None, :] == 1.0)
    allowed = (allowed | jnp.eye(LEN, dtype=bool)[None]).astype(F32)
    allowed_sides = (allowed[:2], allowed[2:])
    live_rows = gather_positions(positions, n, me)
    ahead = jnp.concatenate([buckets, buckets[-1:]])
    back = jnp.concatenate([buckets[::-1], buckets[:1]])
    wanted = jnp.concatenate([back, ahead]) - FIRST_ROW
    picks = (wanted[:, None] == jnp.arange(LIVE_ROWS)[None, :]).astype(BF16)
    rows_used = mm(picks, live_rows).astype(BF16)
    rows_ahead = rows_used[SPAN:]
    places = [order.index(place) for place in range(n)]
    places = jnp.take(jnp.array(places), jnp.bitwise_xor(me, jnp.arange(n)))
    norms = jnp.take(small_all[:, 2 * LEN :], places, axis=0).reshape(n, 2, LAYERS, 2, own)
    norms = norms.transpose(1, 2, 3, 0, 4).reshape(2, LAYERS, 2, D)
    gains, biases = norms[0], norms[1]

    weights = []
    for layer in range(LAYERS):
        if layer:
            qkv_blocks = deal(w_qkv, layer, me, n, 3)
            qkv_blocks = [tie(block, up_blocks[-1]) for block in qkv_blocks]
        qkv_blocks = passed_around(qkv_blocks, n)
        if layer:
            up_blocks = deal(w_up, layer, me, n, 1)
        up_blocks = passed_around([tie(block, qkv_blocks[-1]) for block in up_blocks], n)
        qkv_cols = collect(qkv_blocks, me, n)
        weights.append((qkv_cols, w_out[layer], collect(up_blocks, me, n), w_down[layer]))

    staged = lax.axis_size("rep") == 8 and n == 4
    kept = []
    for layer in range(LAYERS):
        qkv_cols, out_rows, up_cols, down_rows = weights[layer]
        rel = mm(rows_used, qkv_cols[:, : 2 * own]).astype(BF16)
        qkv = [mm(side, qkv_cols).astype(BF16) for side in hidden_sides]
        attended = [
            attention_forward(side, rel[:SPAN], mask, heads)
            for side, mask in zip(qkv, allowed_sides)
        ]
        context = [side[0] for side in attended]
        probs = [side[1] for side in attended]
        attn_sum = hidden + scatter_sides(*[mm(side, out_rows) for side in context])
        mid = normed(attn_sum)[0] * gains[layer, 0] + biases[layer, 0]
        mid_sides = gather_sides(mid.astype(BF16))
        pre_act = [mm(side, up_cols) for side in mid_sides]
        activation = [gelu(side).astype(BF16) for side in pre_act]
        ffn_sum = mid + scatter_sides(*[mm(side, down_rows) for side in activation])
        kept.append((hidden_sides, qkv, rel[SPAN:], context, probs, attn_sum, mid_sides, pre_act, activation, ffn_sum))
        hidden = normed(ffn_sum)[0] * gains[layer, 1] + biases[layer, 1]
        if layer < LAYERS - 1:
            hidden_sides = gather_sides(hidden.astype(BF16))
    output = hidden.astype(BF16)

    def over_tokens(left, right):
        return mm_tn(left[0], right[0]) + mm_tn(left[1], right[1])

    upstream = cotangent.astype(F32)
    others = jnp.bitwise_xor(me, jnp.arange(n, dtype=jnp.int32))
    shapes = [(LAYERS,) + weight.shape[1:] for weight in (w_qkv, w_out, w_up, w_down)]
    upper = lax.axis_index("rep") % 2
    sums = Sums(jnp.concatenate([upper.reshape(1), others]), shapes)
    grads = {}
    small = [None] * LAYERS
    row_grads = jnp.zeros((SPAN, D), F32)
    top = LAYERS - 1

    for layer in reversed(range(LAYERS)):
        qkv_cols, out_rows, up_cols, down_rows = weights[layer]
        hidden_sides, qkv, rel, context, probs, attn_sum, mid_sides, pre_act, activation, ffn_sum = kept[layer]
        d_ffn, d_gain_two, d_bias_two = norm_backward(upstream, ffn_sum, gains[layer, 1])
        branch = gather_sides(d_ffn.astype(BF16))
        if staged and layer < top:
            sums.last = branch
            sums.start("Q1", grads[top][0])
            branch = sums.ordered(branch)
        d_pre = [
            (mm_nt(side, down_rows) * gelu_slope(pre)).astype(BF16)
            for side, pre in zip(branch, pre_act)
        ]
        d_mid = d_ffn + scatter_sides(*[mm_nt(side, up_cols) for side in d_pre])
        g_down = over_tokens(activation, branch).astype(BF16)
        g_up = over_tokens(mid_sides, d_pre).astype(BF16).reshape(n, own, -1)
        if staged:
            d_mid, g_down = lax.optimization_barrier((d_mid, g_down))
            if layer == top:
                sums.start("D1", g_down)
            else:
                sums.last = d_mid
                sums.step("D1", "U1")
                sums.start("D0", g_down, out_top)
            d_mid = sums.ordered(d_mid)
        d_attn, d_gain_one, d_bias_one = norm_backward(d_mid, attn_sum, gains[layer, 0])
        att = gather_sides(d_attn.astype(BF16))
        d_context = [mm_nt(side, out_rows).astype(BF16) for side in att]
        attended = [
            attention_backward(side, rel, p, grad, heads)
            for side, p, grad in zip(qkv, probs, d_context)
        ]
        d_qkv = [part[0] for part in attended]
        d_rel = (attended[0][1] + attended[1][1]).astype(BF16)
        if staged:
            sums.last = d_qkv
            if layer == top:
                sums.step("D1")
                sums.start("U1", g_up)
            else:
                sums.step("D1", "U1", "Q1", "D0")
                sums.start("U0", g_up)
            d_qkv = sums.ordered(d_qkv)
        upstream = d_attn + scatter_sides(*[mm_nt(side, qkv_cols) for side in d_qkv])
        g_out = over_tokens(context, att).astype(BF16)
        g_qkv = over_tokens(hidden_sides, d_qkv) + mm_tn(
            rows_ahead, jnp.concatenate([d_rel, jnp.zeros((SPAN, own), BF16)], axis=1)
        )
        g_qkv = g_qkv.astype(BF16).reshape(n, own, -1)
        row_grads = row_grads + mm_nt(d_rel, qkv_cols[:, : 2 * own])
        small[layer] = (
            jnp.stack([d_gain_one, d_gain_two]),
            jnp.stack([d_bias_one, d_bias_two]),
        )
        if staged and layer < top:
            sums.last = (upstream, g_out, g_qkv)
            sums.start("Q0", g_qkv)
            upstream = sums.ordered(upstream)
        out_top = g_out
        grads[layer] = (g_qkv, g_out, g_up, g_down)

    owners = jnp.bitwise_xor(me, jnp.array(order))
    norm_part = jnp.stack(
        [jnp.stack([entry[0] for entry in small]), jnp.stack([entry[1] for entry in small])]
    )
    norm_part = norm_part.reshape(2, LAYERS, 2, n, own).transpose(3, 0, 1, 2, 4)
    norm_part = jnp.take(norm_part, owners, axis=0).reshape(n, 2 * LAYERS * 2 * own)
    norm_part = scatter_sides(norm_part[:2], norm_part[2:])
    position_part = scatter_positions(row_grads, ahead, positions.shape[0], n, me)
    norm_count = 2 * LAYERS * 2 * own
    norm_rows = (norm_count + D - 1) // D
    norm_part = jnp.pad(norm_part.reshape(-1), (0, norm_rows * D - norm_count)).reshape(norm_rows, D)
    packed = jnp.concatenate([position_part, norm_part], axis=0).astype(BF16)

    if staged:
        rows = packed.shape[0]
        packed = jnp.pad(packed, ((0, -rows % 32), (0, 0)))
        sums.start("R", g_out, packed)
        sums.step("D1", "U1", "Q1", "D0", "U0")
        sums.step("U1", "Q1")
        sums.step("D1")
        sums.place(sums.results["D1"], 3, 1, 1, 0)
        sums.step("D0", "U0", "Q0", "U1", "Q1")
        sums.step("D0", "U0", "Q0", "R", "Q1")
        sums.step("U1")
        sums.place(sums.results["U1"], 2, 1, 1, n)
        sums.step("U0", "Q0", "R")
        sums.step("U0", "D0")
        sums.place(sums.results["D0"], 3, 0, 1, 0)
        sums.place(sums.results["D0"], 1, 1, 1, 0, own * 2)
        sums.step("Q0", "R", "Q0")
        sums.step("Q1")
        sums.place(sums.results["Q1"], 0, 1, 3, n)
        sums.step("R", "U0")
        sums.place(sums.results["U0"], 2, 0, 1, n)
        sums.step("Q0")
        sums.place(sums.results["Q0"], 0, 0, 3, n)
        sums.step("R")
        sums.place(sums.results["R"], 1, 0, 1, 0)
        out_grads = sums.outs
        near, far = [half[own // 2 :] for half in sums.results["R"]]
        lower, higher = jnp.where(upper == 0, near, far), jnp.where(upper == 0, far, near)
        packed = jnp.concatenate([lower, higher], axis=0)[:rows]
    else:
        packed = lax.psum(packed, "rep")
        out_grads = []
        for which, shape in enumerate(shapes):
            out = None
            for layer in range(LAYERS):
                total = grads[layer][which].astype(BF16)
                if which in (0, 2):
                    parts = 3 if which == 0 else 1
                    total = to_owners(total.reshape(n, own, -1), me, n)
                    total = jnp.take(total, others, axis=0).reshape(n, own, parts, -1)
                    total = total.transpose(1, 2, 0, 3).reshape(shape[1:])
                out = put_layer(lax.psum(total, "rep"), layer, out, shape)
            out_grads.append(out)

    grad_positions = packed[:-norm_rows].astype(F32)
    if grad_positions.shape[0] < positions.shape[0]:
        gap = positions.shape[0] - grad_positions.shape[0]
        grad_positions = jnp.where(
            me == 1,
            jnp.pad(grad_positions, ((gap, 0), (0, 0))),
            jnp.where(me == 2, jnp.pad(grad_positions, ((0, gap), (0, 0))), 0.0),
        )
    norm_part = packed[-norm_rows:].astype(F32).reshape(-1)[:norm_count].reshape(2, LAYERS, 2, own).transpose(0, 1, 3, 2)
    return (output, upstream, *out_grads, norm_part[0], norm_part[1], grad_positions)


def solution(mesh):
    tokens = P(("rep", "shard"), None)
    rows = P(None, "shard", None)
    labels = P(("rep", "shard"))
    return jax.shard_map(
        per_device,
        mesh=mesh,
        in_specs=(
            tokens,
            tokens,
            rows,
            rows,
            rows,
            rows,
            rows,
            rows,
            P("shard", None),
            labels,
            labels,
            P(),
        ),
        out_specs=(tokens, tokens, rows, rows, rows, rows, rows, rows, P("shard", None)),
        check_vma=False,
    )
```

```python
from functools import partial
import math

import jax
import jax.numpy as jnp
from jax import lax
from jax.experimental import pallas as pl
from jax.experimental.pallas import tpu as pltpu
from jax.sharding import PartitionSpec as P

D = 1024
H = 16
DH = 64
LAYERS = 2
LEN = 128
SPAN = 2 * LEN
FIRST_ROW = 160
LIVE_ROWS = 192
SCALE = 1.0 / math.sqrt(3 * DH)
NEG_FILL = -1e30
NORM_EPS = 1e-07
F32 = jnp.float32
BF16 = jnp.bfloat16


def mm(a, b):
    return jnp.dot(a, b, preferred_element_type=F32)


def mm_nt(a, b):
    return lax.dot_general(a, b, (((1,), (1,)), ((), ())), preferred_element_type=F32)


def mm_tn(a, b):
    return lax.dot_general(a, b, (((0,), (0,)), ((), ())), preferred_element_type=F32)


def swap(value, axis, mask):
    size = lax.axis_size(axis)
    return lax.ppermute(value, axis, [(i, i ^ mask) for i in range(size)])


def far_order(n):
    span, mask = [0], n // 2
    while mask > 1:
        span = span + [place ^ mask for place in span]
        mask //= 2
    return span[1:]


def group_order(n):
    far = far_order(n)
    return [0, 1] + far + [place ^ 1 for place in far]


def gather_sides(own, meanwhile=None):
    n = lax.axis_size("shard")
    near = jnp.concatenate([own, swap(own, "shard", 1)], axis=0)
    span, mask = own, n // 2
    while mask > 1:
        passed = swap(span, "shard", mask)
        span = passed if mask == 2 and n == 4 else jnp.concatenate([span, passed], axis=0)
        mask //= 2
    far = span if n == 4 else span[own.shape[0] :]
    if meanwhile is not None:
        far = tie(far, meanwhile(own))
    return near, jnp.concatenate([far, swap(far, "shard", 1)], axis=0)


def gather_group(own):
    return jnp.concatenate(gather_sides(own), axis=0)


def scatter_positions(row_grads, ahead, rows, n, me):
    live = jnp.arange(SPAN) < SPAN - 1
    if n == 4 and rows == 128:
        wanted = FIRST_ROW + jnp.arange(LIVE_ROWS)
    else:
        owners = jnp.bitwise_xor(me, jnp.array(group_order(n)))
        wanted = (owners[:, None] * rows + jnp.arange(rows)[None, :]).reshape(-1)
    picks = ((wanted[:, None] == ahead[None, :]) & live[None, :]).astype(BF16)
    by_row = mm(picks, row_grads.astype(BF16))
    if n != 4 or rows != 128:
        return scatter_sides(by_row[: 2 * rows], by_row[2 * rows :])
    size = LIVE_ROWS // 2
    odd = me % 2 == 1
    mine = jnp.where(odd, by_row[:size], by_row[size:])
    total = mine + swap(jnp.where(odd, by_row[size:], by_row[:size]).astype(BF16), "shard", 1).astype(F32)
    return total + swap(total.astype(BF16), "shard", 2).astype(F32)


def scatter_sides(near, far, meanwhile=None):
    n = lax.axis_size("shard")
    half = far.shape[0] // 2
    far = far[:half] + swap(far[half:].astype(BF16), "shard", 1).astype(F32)
    half = near.shape[0] // 2
    near = near[:half] + swap(near[half:].astype(BF16), "shard", 1).astype(F32)
    if n == 4:
        far = far.astype(BF16)
        passed = swap(far, "shard", 2)
        if meanwhile is not None:
            passed = tie(passed, meanwhile(far))
        return near + passed.astype(F32)
    total, mask = jnp.concatenate([near, far], axis=0), 2
    while mask < n:
        half = total.shape[0] // 2
        total = total[:half] + swap(total[half:].astype(BF16), "shard", mask).astype(F32)
        mask *= 2
    return total


def gather_positions(positions, n, me):
    last_row = FIRST_ROW + LIVE_ROWS
    rows = positions.shape[0]
    if n != 4 or rows != 128:
        whole = lax.all_gather(positions, "shard", axis=0, tiled=True)
        return whole[FIRST_ROW:last_row]
    size = LIVE_ROWS // 2
    mine = jnp.where(me == 1, positions[rows - size :], positions[:size])
    passed = lax.ppermute(mine, "shard", [(1, 3), (2, 0)])
    held = jnp.where((me == 1) | (me == 2), mine, passed)
    other = swap(held, "shard", 1)
    low = me % 2 == 1
    return jnp.concatenate([jnp.where(low, held, other), jnp.where(low, other, held)], axis=0)


def copy_blocks_kernel(n, me_ref, *refs):
    for source, target in zip(refs[:n], refs[n:]):
        target[...] = source[0]


def deal(weight, layer, me, n, parts, shared=False):
    rows = weight.shape[1]
    c = weight.shape[2] // (parts * n)
    if c % 128:
        blocks = []
        for mask in range(n):
            other = jnp.bitwise_xor(me, mask)
            pieces = [
                lax.dynamic_slice(weight, (layer, 0, (part * n + other) * c), (1, rows, c))[0]
                for part in range(parts)
            ]
            blocks.append(jnp.concatenate(pieces, axis=1))
        return blocks
    split = 1 if parts > 1 or c % 512 else 4

    heights = [rows // 2 if shared and mask > 1 else rows for mask in range(n)]

    def source_spec(mask):
        def where(part, cut, me):
            half = me[1] if heights[mask] < rows else 0
            return (layer, half, (part * n + jnp.bitwise_xor(me[0], mask)) * split + cut)

        return pl.BlockSpec((1, heights[mask], c // split), where)

    def target(mask):
        return pl.BlockSpec((heights[mask], c // split), lambda part, cut, me: (0, part * split + cut))

    return pl.pallas_call(
        partial(copy_blocks_kernel, n),
        grid_spec=pltpu.PrefetchScalarGridSpec(
            num_scalar_prefetch=1,
            grid=(parts, split),
            in_specs=[source_spec(mask) for mask in range(n)],
            out_specs=[target(mask) for mask in range(n)],
        ),
        out_shape=[jax.ShapeDtypeStruct((height, parts * c), BF16) for height in heights],
        compiler_params=pltpu.CompilerParams(vmem_limit_bytes=24 * 1024 * 1024),
        name="deal",
    )(place_of(me), *([weight] * n))


def collect_kernel(n, me_ref, *refs):
    step = pl.program_id(1)
    out_ref, at = refs[-1], 0
    for mask in range(n):
        sources = refs[at : at + 1]
        if sources[0].shape[0] < out_ref.shape[0]:
            sources = refs[at : at + 2]
        at += len(sources)

        @pl.when(step == jnp.bitwise_xor(me_ref[0], mask))
        def _():
            if len(sources) == 1:
                out_ref[...] = sources[0][...]
                return
            size = sources[0].shape[0]
            for source, half in zip(sources, (me_ref[1], 1 - me_ref[1])):
                out_ref[pl.ds(pl.multiple_of(half * size, size), size), :] = source[...]


def collect(blocks, me, n):
    rows, width = blocks[0].shape
    if rows % 32 or width % 256:
        whole = jnp.zeros((n * rows, width), BF16)
        for mask, block in enumerate(blocks):
            other = jnp.bitwise_xor(me, mask)
            whole = lax.dynamic_update_slice(whole, block, (other * rows, 0))
        return whole
    c = width // 2
    arrays = [array for block in blocks for array in (block if isinstance(block, tuple) else (block,))]
    return pl.pallas_call(
        partial(collect_kernel, n),
        grid_spec=pltpu.PrefetchScalarGridSpec(
            num_scalar_prefetch=1,
            grid=(width // c, n),
            in_specs=[
                pl.BlockSpec((array.shape[0], c), lambda cut, step, me: (0, cut)) for array in arrays
            ],
            out_specs=pl.BlockSpec((rows, c), lambda cut, step, me: (step, cut)),
        ),
        out_shape=jax.ShapeDtypeStruct((n * rows, width), BF16),
        compiler_params=pltpu.CompilerParams(vmem_limit_bytes=24 * 1024 * 1024),
        name="collect",
    )(place_of(me), *arrays)


def place_of(me):
    return jnp.stack([me, lax.axis_index("rep") % 2])


def passed_around(blocks, n):
    rows = blocks[0].shape[0]
    passed = [swap(block, "shard", mask) if mask else block for mask, block in enumerate(blocks)]
    return [block if block.shape[0] == rows else (block, swap(block, "rep", 1)) for block in passed]


def to_owners(columns, me, n):
    blocks = []
    for mask in range(n):
        block = lax.dynamic_index_in_dim(columns, jnp.bitwise_xor(me, mask), 0, keepdims=False)
        blocks.append(swap(block, "shard", mask) if mask else block)
    return jnp.stack(blocks)


def tie(value, after):
    return lax.optimization_barrier((value, after))[0]


INWARDS = [(0, 2), (1, 3), (6, 4), (7, 5)]
ACROSS = [(2, 4), (3, 5), (4, 2), (5, 3)]
OUTWARDS = [(2, 0), (3, 1), (4, 6), (5, 7)]


def line_stages(value):
    rep = lax.axis_index("rep")
    for pairs in (INWARDS, ACROSS):
        passed = yield value, lax.ppermute(value, "rep", pairs)
        value = (value.astype(F32) + passed.astype(F32)).astype(BF16)
    passed = yield value, lax.ppermute(value, "rep", OUTWARDS)
    return jnp.where((rep >= 2) & (rep < 6), value, passed)


def halves_of(grads, upper):
    pieces = []
    for grad in grads:
        size = grad.shape[-2] // 2
        pieces.append(lax.dynamic_slice_in_dim(grad, upper * size, size, grad.ndim - 2))
    return pieces[0] if len(pieces) == 1 else jnp.concatenate(pieces, axis=0)


def half_stages(grads):
    upper = lax.axis_index("rep") % 2
    me = lax.axis_index("shard")
    sent = halves_of(grads, 1 - upper)
    held = halves_of(grads, upper)
    passed = yield sent, swap(sent, "rep", 1)
    value = (held.astype(F32) + passed.astype(F32)).astype(BF16)
    value = yield from line_stages(value)
    if value.ndim == 3:
        blocks = []
        for mask in range(value.shape[0]):
            other = jnp.bitwise_xor(me, mask)
            blocks.append(lax.dynamic_index_in_dim(value, other, 0, keepdims=False))
        moved = [swap(block, "shard", mask) if mask else block for mask, block in enumerate(blocks)]
        blocks = yield blocks, moved
        value = jnp.stack(blocks)
    far = yield value, swap(value, "rep", 1)
    return value, far


class Sums:
    def __init__(self, index, shapes):
        self.index, self.shapes = index, shapes
        self.outs = [None] * len(shapes)
        self.stages, self.moving, self.results = {}, {}, {}
        self.last, self.placed = (), None

    def ordered(self, value):
        out = () if self.placed is None else self.outs[self.placed]
        value, _, out = lax.optimization_barrier((value, self.last, out))
        if self.placed is not None:
            self.outs[self.placed] = out
            self.placed = None
        return value

    def start(self, name, *grads):
        grads = self.ordered([grad.astype(BF16) for grad in grads])
        self.stages[name] = half_stages(grads)
        self.last, self.moving[name] = next(self.stages[name])

    def step(self, *names):
        for name in names:
            moving = self.ordered(self.moving.pop(name))
            try:
                self.last, self.moving[name] = self.stages[name].send(moving)
            except StopIteration as stop:
                self.results[name] = stop.value

    def place(self, total, which, layer, parts, n, offset=0):
        shape, out = self.shapes[which], self.outs[which]
        total = self.ordered(total)
        if isinstance(total, tuple):
            out = place(total, self.index, layer, out, shape, parts, n, offset)
        else:
            out = place_whole(total, self.index, layer, out, shape, parts, n)
        self.outs[which], self.placed = out, which


def place_kernel(parts, n, c, steps, index_ref, near_ref, far_ref, *rest):
    out_ref = rest[-1]

    def put(source):
        if n == 0:
            out_ref[0] = source[...].astype(F32)
            return
        for mask in range(n):
            for part in range(parts):
                at = pl.multiple_of(index_ref[1 + mask] * c + part * n * c, c)
                out_ref[0, :, pl.ds(at, c)] = source[mask, :, part * c : (part + 1) * c].astype(F32)

    @pl.when(pl.program_id(0) < steps)
    def _():
        put(near_ref)

    @pl.when(pl.program_id(0) >= steps)
    def _():
        put(far_ref)


def place(halves, index, layer, out, shape, parts, n, offset):
    size = shape[1] // 2
    rows = size // 4 if size % 64 == 0 else size
    steps, skip = size // rows, offset // rows
    c = shape[2] // (parts * n) if n else 0
    lead = (n,) if n else ()
    block = lead + (rows, parts * c if n else shape[2])
    zeros = (0,) * len(lead)

    def target(s, index):
        first = index[0] * steps + s
        second = (1 - index[0]) * steps + s - steps
        return (layer, jnp.where(s < steps, first, second), 0)

    in_specs = [
        pl.BlockSpec(block, lambda s, index: zeros + (skip + jnp.minimum(s, steps - 1), 0)),
        pl.BlockSpec(block, lambda s, index: zeros + (skip + jnp.maximum(s - steps, 0), 0)),
    ]
    operands = [index, *halves]
    aliases = {}
    if out is not None:
        in_specs.append(pl.BlockSpec(memory_space=pl.ANY))
        operands.append(out)
        aliases = {3: 0}
    return pl.pallas_call(
        partial(place_kernel, parts, n, c, steps),
        grid_spec=pltpu.PrefetchScalarGridSpec(
            num_scalar_prefetch=1,
            grid=(2 * steps,),
            in_specs=in_specs,
            out_specs=pl.BlockSpec((1, rows, shape[2]), target),
        ),
        out_shape=jax.ShapeDtypeStruct(shape, F32),
        input_output_aliases=aliases,
        compiler_params=pltpu.CompilerParams(vmem_limit_bytes=32 * 1024 * 1024),
        name="place",
    )(*operands)


def place_whole_kernel(parts, n, c, index_ref, blocks_ref, *rest):
    out_ref = rest[-1]
    if n == 0:
        out_ref[0] = blocks_ref[...].astype(F32)
        return
    for mask in range(n):
        for part in range(parts):
            at = pl.multiple_of(index_ref[1 + mask] * c + part * n * c, c)
            out_ref[0, :, pl.ds(at, c)] = blocks_ref[mask, :, part * c : (part + 1) * c].astype(F32)


def place_whole(blocks, index, layer, out, shape, parts, n):
    rows = shape[1] // 8
    c = shape[2] // (parts * n) if n else 0
    lead = (n,) if n else ()
    zeros = (0,) * len(lead)
    block = lead + (rows, parts * c if n else shape[2])
    in_specs = [pl.BlockSpec(block, lambda s, index: zeros + (s, 0))]
    operands, aliases = [index, blocks], {}
    if out is not None:
        in_specs.append(pl.BlockSpec(memory_space=pl.ANY))
        operands.append(out)
        aliases = {2: 0}
    return pl.pallas_call(
        partial(place_whole_kernel, parts, n, c),
        grid_spec=pltpu.PrefetchScalarGridSpec(
            num_scalar_prefetch=1,
            grid=(shape[1] // rows,),
            in_specs=in_specs,
            out_specs=pl.BlockSpec((1, rows, shape[2]), lambda s, index: (layer, s, 0)),
        ),
        out_shape=jax.ShapeDtypeStruct(shape, F32),
        input_output_aliases=aliases,
        compiler_params=pltpu.CompilerParams(vmem_limit_bytes=32 * 1024 * 1024),
        name="place_whole",
    )(*operands)


def put_layer(total, layer, out, shape):
    out = jnp.zeros(shape, F32) if out is None else out
    return out.at[layer].set(total.astype(F32))


def attention_forward_kernel(heads, qkv_ref, rel_ref, allowed_ref, context_ref, probs_ref):
    width = heads * DH
    allowed = allowed_ref[0] > 0

    def pick(ref, group, head):
        at = group * width + head * DH
        return ref[:, at : at + DH]

    def skew(table):
        return pltpu.roll(table, LEN + 1, 1, stride=1, stride_axis=0)[:, :LEN]

    every = range(heads)
    q = [pick(qkv_ref, 0, head) for head in every]
    k = [pick(qkv_ref, 1, head) for head in every]
    by_key = [mm_nt(q[head], pick(rel_ref, 1, head)) for head in every]
    by_query = [mm_nt(k[head], pick(rel_ref, 0, head)) for head in every]
    direct = [mm_nt(q[head], k[head]) for head in every]
    by_key = [skew(table) for table in by_key]
    by_query = [skew(table) for table in by_query]
    scores = [(direct[head] + by_key[head] + by_query[head].T) * SCALE for head in every]
    scores = [jnp.where(allowed, score, NEG_FILL) for score in scores]
    tops = [jnp.max(score, axis=1, keepdims=True) for score in scores]
    terms = [jnp.exp(score - most) for score, most in zip(scores, tops)]
    totals = [jnp.sum(term, axis=1, keepdims=True) for term in terms]
    probs = [term / total for term, total in zip(terms, totals)]
    for head in every:
        probs_ref[0, head] = probs[head]
    context = [mm(probs[head].astype(BF16), pick(qkv_ref, 2, head)).astype(BF16) for head in every]
    context_ref[...] = jnp.concatenate(context, axis=1)


def attention_forward(qkv, rel_back, allowed, heads):
    count = allowed.shape[0]
    width = heads * DH
    return pl.pallas_call(
        partial(attention_forward_kernel, heads),
        grid=(count,),
        in_specs=[
            pl.BlockSpec((LEN, 3 * width), lambda s: (s, 0)),
            pl.BlockSpec((SPAN, 2 * width), lambda s: (0, 0)),
            pl.BlockSpec((1, LEN, LEN), lambda s: (s, 0, 0)),
        ],
        out_specs=[
            pl.BlockSpec((LEN, width), lambda s: (s, 0)),
            pl.BlockSpec((1, heads, LEN, LEN), lambda s: (s, 0, 0, 0)),
        ],
        out_shape=[
            jax.ShapeDtypeStruct((count * LEN, width), BF16),
            jax.ShapeDtypeStruct((count, heads, LEN, LEN), F32),
        ],
        compiler_params=pltpu.CompilerParams(vmem_limit_bytes=24 * 1024 * 1024),
        name="attention_forward",
    )(qkv, rel_back, allowed)


def attention_backward_kernel(heads, qkv_ref, rel_ref, probs_ref, grad_ref, dqkv_ref, drel_ref):
    width = heads * DH

    @pl.when(pl.program_id(0) == 0)
    def _():
        drel_ref[...] = jnp.zeros_like(drel_ref)

    row = lax.broadcasted_iota(jnp.int32, (LEN, LEN), 0)
    column = lax.broadcasted_iota(jnp.int32, (LEN, LEN), 1)
    flip = jnp.where(row + column == LEN - 1, 1.0, 0.0).astype(BF16)
    blank = jnp.zeros((LEN, LEN), F32)

    def pick(ref, group, head):
        at = group * width + head * DH
        return ref[:, at : at + DH]

    def spread(flipped):
        wide = jnp.concatenate([flipped, blank], axis=1)
        return pltpu.roll(wide, 0, 1, stride=1, stride_axis=0).astype(BF16)

    every = range(heads)
    q, k, v = [[pick(qkv_ref, group, head) for head in every] for group in range(3)]
    grad = [pick(grad_ref, 0, head) for head in every]
    probs = [probs_ref[0, head] for head in every]
    d_probs = [mm_nt(grad[head], v[head]) for head in every]
    d_value = [mm_tn(probs[head].astype(BF16), grad[head]) for head in every]
    inner = [jnp.sum(d_probs[head] * probs[head], axis=1, keepdims=True) for head in every]
    d_scores = [(probs[head] * (d_probs[head] - inner[head])).astype(BF16) for head in every]
    key_side = [mm(d_score, flip) for d_score in d_scores]
    query_side = [mm_tn(d_score, flip) for d_score in d_scores]
    key_side = [spread(flipped) for flipped in key_side]
    query_side = [spread(flipped) for flipped in query_side]
    d_query = [
        (mm(d_scores[head], k[head]) + mm(key_side[head], pick(rel_ref, 1, head))) * SCALE
        for head in every
    ]
    d_key = [
        (mm_tn(d_scores[head], q[head]) + mm(query_side[head], pick(rel_ref, 0, head))) * SCALE
        for head in every
    ]
    dqkv_ref[...] = jnp.concatenate(d_query + d_key + d_value, axis=1).astype(BF16)
    d_rel_q = [mm_tn(query_side[head], k[head]) * SCALE for head in every]
    d_rel_k = [mm_tn(key_side[head], q[head]) * SCALE for head in every]
    drel_ref[...] += jnp.concatenate(d_rel_q + d_rel_k, axis=1)


def attention_backward(qkv, rel_ahead, probs, d_context, heads):
    count = probs.shape[0]
    width = heads * DH
    return pl.pallas_call(
        partial(attention_backward_kernel, heads),
        grid=(count,),
        in_specs=[
            pl.BlockSpec((LEN, 3 * width), lambda s: (s, 0)),
            pl.BlockSpec((SPAN, 2 * width), lambda s: (0, 0)),
            pl.BlockSpec((1, heads, LEN, LEN), lambda s: (s, 0, 0, 0)),
            pl.BlockSpec((LEN, width), lambda s: (s, 0)),
        ],
        out_specs=[
            pl.BlockSpec((LEN, 3 * width), lambda s: (s, 0)),
            pl.BlockSpec((SPAN, 2 * width), lambda s: (0, 0)),
        ],
        out_shape=[
            jax.ShapeDtypeStruct((count * LEN, 3 * width), BF16),
            jax.ShapeDtypeStruct((SPAN, 2 * width), F32),
        ],
        compiler_params=pltpu.CompilerParams(vmem_limit_bytes=24 * 1024 * 1024),
        name="attention_backward",
    )(qkv, rel_ahead, probs, d_context)


def normed(values):
    centre = values - jnp.mean(values, axis=-1, keepdims=True)
    inverse = lax.rsqrt(jnp.mean(centre * centre, axis=-1, keepdims=True) + NORM_EPS)
    return centre * inverse, inverse


def norm_backward(upstream, values, gain):
    hat, inverse = normed(values)
    pushed = upstream * gain
    first = jnp.mean(pushed, axis=-1, keepdims=True)
    second = jnp.mean(pushed * hat, axis=-1, keepdims=True)
    back = inverse * (pushed - first - hat * second)
    return back, jnp.sum(upstream * hat, axis=0), jnp.sum(upstream, axis=0)


def gelu(x):
    return 0.5 * x * (1.0 + lax.erf(x * math.sqrt(0.5)))


def gelu_slope(x):
    density = jnp.exp(-0.5 * x * x) * (1.0 / math.sqrt(2.0 * math.pi))
    return 0.5 * (1.0 + lax.erf(x * math.sqrt(0.5))) + x * density


def per_device(
    tokens,
    cotangent,
    w_qkv,
    w_out,
    w_up,
    w_down,
    ln_gain,
    ln_bias,
    positions,
    segments,
    keep_mask,
    buckets,
):
    n = lax.axis_size("shard")
    me = lax.axis_index("shard")
    own = D // n
    heads = H // n
    order = group_order(n)

    staged = lax.axis_size("rep") == 8 and n == 4
    qkv_blocks = deal(w_qkv, 0, me, n, 3)
    up_blocks = deal(w_up, 0, me, n, 1, staged)
    hidden = tokens.astype(F32)
    small_part = jnp.concatenate(
        [
            segments.astype(BF16),
            keep_mask.astype(BF16),
            jnp.stack([ln_gain, ln_bias]).transpose(0, 1, 3, 2).reshape(-1),
        ]
    )
    small_count = small_part.shape[0]
    small_part = jnp.pad(small_part, (0, 16 * D - small_count)).reshape(16, D)
    sides = gather_sides(jnp.concatenate([tokens, small_part], axis=0))
    sides = [side.reshape(-1, LEN + 16, D) for side in sides]
    hidden_sides = [side[:, :LEN].reshape(-1, D) for side in sides]
    small_all = jnp.concatenate([side[:, LEN:] for side in sides], axis=0)
    small_all = small_all.reshape(n, 16 * D)[:, :small_count].astype(F32)
    segment, keep = small_all[:, :LEN], small_all[:, LEN : 2 * LEN]
    allowed = (segment[:, :, None] == segment[:, None, :]) & (keep[:, None, :] == 1.0)
    allowed = (allowed | jnp.eye(LEN, dtype=bool)[None]).astype(F32)
    allowed_sides = (allowed[:2], allowed[2:])
    live_rows = gather_positions(positions, n, me)
    ahead = jnp.concatenate([buckets, buckets[-1:]])
    back = jnp.concatenate([buckets[::-1], buckets[:1]])
    wanted = jnp.concatenate([back, ahead]) - FIRST_ROW
    picks = (wanted[:, None] == jnp.arange(LIVE_ROWS)[None, :]).astype(BF16)
    rows_used = mm(picks, live_rows).astype(BF16)
    rows_ahead = rows_used[SPAN:]
    places = [order.index(place) for place in range(n)]
    places = jnp.take(jnp.array(places), jnp.bitwise_xor(me, jnp.arange(n)))
    norms = jnp.take(small_all[:, 2 * LEN :], places, axis=0).reshape(n, 2, LAYERS, 2, own)
    norms = norms.transpose(1, 2, 3, 0, 4).reshape(2, LAYERS, 2, D)
    gains, biases = norms[0], norms[1]

    weights = []
    for layer in range(LAYERS):
        if layer:
            qkv_blocks = deal(w_qkv, layer, me, n, 3, staged)
            qkv_blocks = [tie(block, up_blocks[-1]) for block in qkv_blocks]
            up_blocks = deal(w_up, layer, me, n, 1, staged)
        qkv_blocks = passed_around(qkv_blocks, n)
        up_blocks = passed_around([tie(block, qkv_blocks[-1]) for block in up_blocks], n)
        qkv_cols = collect(qkv_blocks, me, n)
        weights.append((qkv_cols, w_out[layer], collect(up_blocks, me, n), w_down[layer]))

    kept = []
    for layer in range(LAYERS):
        qkv_cols, out_rows, up_cols, down_rows = weights[layer]
        rel = mm(rows_used, qkv_cols[:, : 2 * own]).astype(BF16)
        qkv = [mm(side, qkv_cols).astype(BF16) for side in hidden_sides]
        attended = [
            attention_forward(side, rel[:SPAN], mask, heads)
            for side, mask in zip(qkv, allowed_sides)
        ]
        context = [side[0] for side in attended]
        probs = [side[1] for side in attended]
        attn_sum = hidden + scatter_sides(*[mm(side, out_rows) for side in context])
        mid = normed(attn_sum)[0] * gains[layer, 0] + biases[layer, 0]
        mid_sides = gather_sides(mid.astype(BF16))
        pre_act = [mm(side, up_cols) for side in mid_sides]
        activation = [gelu(side).astype(BF16) for side in pre_act]
        ffn_sum = mid + scatter_sides(*[mm(side, down_rows) for side in activation])
        kept.append((hidden_sides, qkv, rel[SPAN:], context, probs, attn_sum, mid_sides, pre_act, activation, ffn_sum))
        hidden = normed(ffn_sum)[0] * gains[layer, 1] + biases[layer, 1]
        if layer < LAYERS - 1:
            hidden_sides = gather_sides(hidden.astype(BF16))
    output = hidden.astype(BF16)

    def over_tokens(left, right):
        return mm_tn(left[0], right[0]) + mm_tn(left[1], right[1])

    upstream = cotangent.astype(F32)
    others = jnp.bitwise_xor(me, jnp.arange(n, dtype=jnp.int32))
    shapes = [(LAYERS,) + weight.shape[1:] for weight in (w_qkv, w_out, w_up, w_down)]
    upper = lax.axis_index("rep") % 2
    sums = Sums(jnp.concatenate([upper.reshape(1), others]), shapes)
    grads = {}
    small = [None] * LAYERS
    row_grads = jnp.zeros((SPAN, D), F32)
    top = LAYERS - 1

    def served(*actions):
        if not staged:
            return None

        def meanwhile(sent):
            sums.last = (sums.last, sent)
            for action in actions:
                action()
            return sums.last

        return meanwhile

    def stepping(*names):
        return lambda: sums.step(*names)

    for layer in reversed(range(LAYERS)):
        qkv_cols, out_rows, up_cols, down_rows = weights[layer]
        hidden_sides, qkv, rel, context, probs, attn_sum, mid_sides, pre_act, activation, ffn_sum = kept[layer]
        first = layer == top
        d_ffn, d_gain_two, d_bias_two = norm_backward(upstream, ffn_sum, gains[layer, 1])
        hook = None if first else served(lambda: sums.start("Q1", grads[top][0]))
        branch = gather_sides(d_ffn.astype(BF16), hook)
        d_pre = [
            (mm_nt(side, down_rows) * gelu_slope(pre)).astype(BF16)
            for side, pre in zip(branch, pre_act)
        ]
        g_down = over_tokens(activation, branch).astype(BF16)
        if first:
            hook = served(lambda: sums.start("D1", g_down))
        else:
            hook = served(stepping("D1", "U1"), lambda: sums.start("D0", g_down, grads[top][1]))
        d_mid = d_ffn + scatter_sides(*[mm_nt(side, up_cols) for side in d_pre], hook)
        g_up = over_tokens(mid_sides, d_pre).astype(BF16).reshape(n, own, -1)
        d_attn, d_gain_one, d_bias_one = norm_backward(d_mid, attn_sum, gains[layer, 0])
        hook = None if first else served(stepping("Q1"))
        att = gather_sides(d_attn.astype(BF16), hook)
        d_context = [mm_nt(side, out_rows).astype(BF16) for side in att]
        attended = [
            attention_backward(side, rel, p, grad, heads)
            for side, p, grad in zip(qkv, probs, d_context)
        ]
        d_qkv = [part[0] for part in attended]
        d_rel = (attended[0][1] + attended[1][1]).astype(BF16)
        if first:
            hook = served(stepping("D1"), lambda: sums.start("U1", g_up))
        else:
            hook = served(stepping("D1", "U1"), lambda: sums.start("U0", g_up))
        upstream = d_attn + scatter_sides(*[mm_nt(side, qkv_cols) for side in d_qkv], hook)
        g_out = over_tokens(context, att).astype(BF16)
        g_qkv = over_tokens(hidden_sides, d_qkv) + mm_tn(
            rows_ahead, jnp.concatenate([d_rel, jnp.zeros((SPAN, own), BF16)], axis=1)
        )
        g_qkv = g_qkv.astype(BF16).reshape(n, own, -1)
        row_grads = row_grads + mm_nt(d_rel, qkv_cols[:, : 2 * own])
        small[layer] = (
            jnp.stack([d_gain_one, d_gain_two]),
            jnp.stack([d_bias_one, d_bias_two]),
        )
        grads[layer] = (g_qkv, g_out, g_up, g_down)

    owners = jnp.bitwise_xor(me, jnp.array(order))
    norm_part = jnp.stack(
        [jnp.stack([entry[0] for entry in small]), jnp.stack([entry[1] for entry in small])]
    )
    norm_part = norm_part.reshape(2, LAYERS, 2, n, own).transpose(3, 0, 1, 2, 4)
    norm_part = jnp.take(norm_part, owners, axis=0).reshape(n, 2 * LAYERS * 2 * own)
    norm_part = scatter_sides(norm_part[:2], norm_part[2:])
    position_part = scatter_positions(row_grads, ahead, positions.shape[0], n, me)
    norm_count = 2 * LAYERS * 2 * own
    norm_rows = (norm_count + D - 1) // D
    norm_part = jnp.pad(norm_part.reshape(-1), (0, norm_rows * D - norm_count)).reshape(norm_rows, D)
    packed = jnp.concatenate([position_part, norm_part], axis=0).astype(BF16)

    if staged:
        rows = packed.shape[0]
        packed = jnp.pad(packed, ((0, -rows % 32), (0, 0)))
        def finish(name, which, layer, parts, n_from, offset=0):
            if name not in sums.results:
                sums.step(name)
            sums.place(sums.results[name], which, layer, parts, n_from, offset)

        sums.last = (sums.last, upstream)
        sums.step("D0")
        sums.start("Q0", g_qkv)
        sums.step("Q1")
        sums.start("R", g_out, packed)
        sums.step("D1", "U1", "U0", "D0", "Q1", "U1", "Q0")
        finish("D1", 3, 1, 1, 0)
        sums.step("U0", "U1", "Q1", "D0", "R", "Q0", "Q1")
        finish("U1", 2, 1, 1, n)
        sums.step("U0", "R", "D0")
        finish("Q1", 0, 1, 3, n)
        sums.step("Q0", "R", "U0")
        finish("D0", 3, 0, 1, 0)
        finish("D0", 1, 1, 1, 0, own * 2)
        sums.step("U0", "Q0", "R", "Q0")
        finish("U0", 2, 0, 1, n)
        finish("R", 1, 0, 1, 0)
        finish("Q0", 0, 0, 3, n)
        out_grads = sums.outs
        near, far = [half[own // 2 :] for half in sums.results["R"]]
        lower, higher = jnp.where(upper == 0, near, far), jnp.where(upper == 0, far, near)
        packed = jnp.concatenate([lower, higher], axis=0)[:rows]
    else:
        packed = lax.psum(packed, "rep")
        out_grads = []
        for which, shape in enumerate(shapes):
            out = None
            for layer in range(LAYERS):
                total = grads[layer][which].astype(BF16)
                if which in (0, 2):
                    parts = 3 if which == 0 else 1
                    total = to_owners(total.reshape(n, own, -1), me, n)
                    total = jnp.take(total, others, axis=0).reshape(n, own, parts, -1)
                    total = total.transpose(1, 2, 0, 3).reshape(shape[1:])
                out = put_layer(lax.psum(total, "rep"), layer, out, shape)
            out_grads.append(out)

    grad_positions = packed[:-norm_rows].astype(F32)
    if grad_positions.shape[0] < positions.shape[0]:
        gap = positions.shape[0] - grad_positions.shape[0]
        grad_positions = jnp.where(
            me == 1,
            jnp.pad(grad_positions, ((gap, 0), (0, 0))),
            jnp.where(me == 2, jnp.pad(grad_positions, ((0, gap), (0, 0))), 0.0),
        )
    norm_part = packed[-norm_rows:].astype(F32).reshape(-1)[:norm_count].reshape(2, LAYERS, 2, own).transpose(0, 1, 3, 2)
    return (output, upstream, *out_grads, norm_part[0], norm_part[1], grad_positions)


def solution(mesh):
    tokens = P(("rep", "shard"), None)
    rows = P(None, "shard", None)
    labels = P(("rep", "shard"))
    return jax.shard_map(
        per_device,
        mesh=mesh,
        in_specs=(
            tokens,
            tokens,
            rows,
            rows,
            rows,
            rows,
            rows,
            rows,
            P("shard", None),
            labels,
            labels,
            P(),
        ),
        out_specs=(tokens, tokens, rows, rows, rows, rows, rows, rows, P("shard", None)),
        check_vma=False,
    )
```

```python
from functools import partial
import math

import jax
import jax.numpy as jnp
from jax import lax
from jax.experimental import pallas as pl
from jax.experimental.pallas import tpu as pltpu
from jax.sharding import PartitionSpec as P

D = 1024
H = 16
DH = 64
LAYERS = 2
LEN = 128
SPAN = 2 * LEN
FIRST_ROW = 160
LIVE_ROWS = 192
SCALE = 1.0 / math.sqrt(3 * DH)
NEG_FILL = -1e30
NORM_EPS = 1e-07
F32 = jnp.float32
BF16 = jnp.bfloat16


def mm(a, b):
    return jnp.dot(a, b, preferred_element_type=F32)


def mm_nt(a, b):
    return lax.dot_general(a, b, (((1,), (1,)), ((), ())), preferred_element_type=F32)


def mm_tn(a, b):
    return lax.dot_general(a, b, (((0,), (0,)), ((), ())), preferred_element_type=F32)


def swap(value, axis, mask):
    size = lax.axis_size(axis)
    return lax.ppermute(value, axis, [(i, i ^ mask) for i in range(size)])


def far_order(n):
    span, mask = [0], n // 2
    while mask > 1:
        span = span + [place ^ mask for place in span]
        mask //= 2
    return span[1:]


def group_order(n):
    far = far_order(n)
    return [0, 1] + far + [place ^ 1 for place in far]


def gather_sides(own, meanwhile=None):
    n = lax.axis_size("shard")
    near = jnp.concatenate([own, swap(own, "shard", 1)], axis=0)
    span, mask = own, n // 2
    while mask > 1:
        passed = swap(span, "shard", mask)
        span = passed if mask == 2 and n == 4 else jnp.concatenate([span, passed], axis=0)
        mask //= 2
    far = span if n == 4 else span[own.shape[0] :]
    if meanwhile is not None:
        far = tie(far, meanwhile(own))
    return near, jnp.concatenate([far, swap(far, "shard", 1)], axis=0)


def gather_group(own):
    return jnp.concatenate(gather_sides(own), axis=0)


def scatter_positions(row_grads, ahead, rows, n, me):
    live = jnp.arange(SPAN) < SPAN - 1
    if n == 4 and rows == 128:
        wanted = FIRST_ROW + jnp.arange(LIVE_ROWS)
    else:
        owners = jnp.bitwise_xor(me, jnp.array(group_order(n)))
        wanted = (owners[:, None] * rows + jnp.arange(rows)[None, :]).reshape(-1)
    picks = ((wanted[:, None] == ahead[None, :]) & live[None, :]).astype(BF16)
    by_row = mm(picks, row_grads.astype(BF16))
    if n != 4 or rows != 128:
        return scatter_sides(by_row[: 2 * rows], by_row[2 * rows :])
    size = LIVE_ROWS // 2
    odd = me % 2 == 1
    mine = jnp.where(odd, by_row[:size], by_row[size:])
    total = mine + swap(jnp.where(odd, by_row[size:], by_row[:size]).astype(BF16), "shard", 1).astype(F32)
    return total + swap(total.astype(BF16), "shard", 2).astype(F32)


def scatter_sides(near, far, meanwhile=None):
    n = lax.axis_size("shard")
    half = far.shape[0] // 2
    far = far[:half] + swap(far[half:].astype(BF16), "shard", 1).astype(F32)
    half = near.shape[0] // 2
    near = near[:half] + swap(near[half:].astype(BF16), "shard", 1).astype(F32)
    if n == 4:
        far = far.astype(BF16)
        passed = swap(far, "shard", 2)
        if meanwhile is not None:
            passed = tie(passed, meanwhile(far))
        return near + passed.astype(F32)
    total, mask = jnp.concatenate([near, far], axis=0), 2
    while mask < n:
        half = total.shape[0] // 2
        total = total[:half] + swap(total[half:].astype(BF16), "shard", mask).astype(F32)
        mask *= 2
    return total


def gather_positions(positions, n, me):
    last_row = FIRST_ROW + LIVE_ROWS
    rows = positions.shape[0]
    if n != 4 or rows != 128:
        whole = lax.all_gather(positions, "shard", axis=0, tiled=True)
        return whole[FIRST_ROW:last_row]
    size = LIVE_ROWS // 2
    mine = jnp.where(me == 1, positions[rows - size :], positions[:size])
    passed = lax.ppermute(mine, "shard", [(1, 3), (2, 0)])
    held = jnp.where((me == 1) | (me == 2), mine, passed)
    other = swap(held, "shard", 1)
    low = me % 2 == 1
    return jnp.concatenate([jnp.where(low, held, other), jnp.where(low, other, held)], axis=0)


def copy_blocks_kernel(n, me_ref, *refs):
    for source, target in zip(refs[:n], refs[n:]):
        target[...] = source[0]


def deal(weight, layer, me, n, parts, shared=False):
    rows = weight.shape[1]
    c = weight.shape[2] // (parts * n)
    if c % 128:
        blocks = []
        for mask in range(n):
            other = jnp.bitwise_xor(me, mask)
            pieces = [
                lax.dynamic_slice(weight, (layer, 0, (part * n + other) * c), (1, rows, c))[0]
                for part in range(parts)
            ]
            blocks.append(jnp.concatenate(pieces, axis=1))
        return blocks
    split = 1 if parts > 1 or c % 512 else 4

    count = n - 1 if shared else n

    def source_spec(mask):
        def where(part, cut, me):
            other = jnp.bitwise_xor(me[0], mask + me[1] if shared and mask == 2 else mask)
            return (layer, 0, (part * n + other) * split + cut)

        return pl.BlockSpec((1, rows, c // split), where)

    target = pl.BlockSpec((rows, c // split), lambda part, cut, me: (0, part * split + cut))
    return pl.pallas_call(
        partial(copy_blocks_kernel, count),
        grid_spec=pltpu.PrefetchScalarGridSpec(
            num_scalar_prefetch=1,
            grid=(parts, split),
            in_specs=[source_spec(mask) for mask in range(count)],
            out_specs=[target] * count,
        ),
        out_shape=[jax.ShapeDtypeStruct((rows, parts * c), BF16)] * count,
        compiler_params=pltpu.CompilerParams(vmem_limit_bytes=24 * 1024 * 1024),
        name="deal",
    )(place_of(me), *([weight] * count))


def collect_kernel(n, shared, me_ref, *refs):
    step = pl.program_id(1)
    for at in range(n):
        mask = at
        if shared and at > 1:
            mask = 2 + me_ref[1] if at == 2 else 3 - me_ref[1]

        @pl.when(step == jnp.bitwise_xor(me_ref[0], mask))
        def _():
            refs[n][...] = refs[at][...]


def collect(blocks, me, n, shared):
    rows, width = blocks[0].shape
    if rows % 16 or width % 256:
        whole = jnp.zeros((n * rows, width), BF16)
        for mask, block in enumerate(blocks):
            other = jnp.bitwise_xor(me, mask)
            whole = lax.dynamic_update_slice(whole, block, (other * rows, 0))
        return whole
    c = width // 2
    return pl.pallas_call(
        partial(collect_kernel, n, shared),
        grid_spec=pltpu.PrefetchScalarGridSpec(
            num_scalar_prefetch=1,
            grid=(width // c, n),
            in_specs=[pl.BlockSpec((rows, c), lambda cut, step, me: (0, cut))] * n,
            out_specs=pl.BlockSpec((rows, c), lambda cut, step, me: (step, cut)),
        ),
        out_shape=jax.ShapeDtypeStruct((n * rows, width), BF16),
        compiler_params=pltpu.CompilerParams(vmem_limit_bytes=24 * 1024 * 1024),
        name="collect",
    )(place_of(me), *blocks)


def place_of(me):
    return jnp.stack([me, lax.axis_index("rep") % 2])


def passed_around(blocks, n):
    passed = [swap(block, "shard", mask) if mask else block for mask, block in enumerate(blocks[:2])]
    if len(blocks) == n:
        return passed + [swap(block, "shard", mask + 2) for mask, block in enumerate(blocks[2:])]
    size = lax.axis_size("rep")
    pairs = [(r * n + i, r * n + (i ^ (2 + r % 2))) for r in range(size) for i in range(n)]
    across = lax.ppermute(blocks[2], ("rep", "shard"), pairs)
    return passed + [across, swap(across, "rep", 1)]


def to_owners(columns, me, n):
    blocks = []
    for mask in range(n):
        block = lax.dynamic_index_in_dim(columns, jnp.bitwise_xor(me, mask), 0, keepdims=False)
        blocks.append(swap(block, "shard", mask) if mask else block)
    return jnp.stack(blocks)


def tie(value, after):
    return lax.optimization_barrier((value, after))[0]


INWARDS = [(0, 2), (1, 3), (6, 4), (7, 5)]
ACROSS = [(2, 4), (3, 5), (4, 2), (5, 3)]
OUTWARDS = [(2, 0), (3, 1), (4, 6), (5, 7)]
TAIL = (
    "D0", "U1", "Q1", "Q0", "D1", "R", "U0", "D0", "Q1", "U1", "Q0", "R", "U1", "U0", "D0",
    "Q1", "D1", "Q0", "Q1", "U0", "R", "D0", "U1", "Q1", "R", "U0", "Q0", "R", "U0", "D0",
    "Q0", "Q0", "R", "U0", "Q0",
)


def line_stages(value):
    rep = lax.axis_index("rep")
    for pairs in (INWARDS, ACROSS):
        passed = yield value, lax.ppermute(value, "rep", pairs)
        value = (value.astype(F32) + passed.astype(F32)).astype(BF16)
    passed = yield value, lax.ppermute(value, "rep", OUTWARDS)
    return jnp.where((rep >= 2) & (rep < 6), value, passed)


def halves_of(grads, upper):
    pieces = []
    for grad in grads:
        size = grad.shape[-2] // 2
        pieces.append(lax.dynamic_slice_in_dim(grad, upper * size, size, grad.ndim - 2))
    return pieces[0] if len(pieces) == 1 else jnp.concatenate(pieces, axis=0)


def half_stages(grads):
    upper = lax.axis_index("rep") % 2
    me = lax.axis_index("shard")
    sent = halves_of(grads, 1 - upper)
    held = halves_of(grads, upper)
    passed = yield sent, swap(sent, "rep", 1)
    value = (held.astype(F32) + passed.astype(F32)).astype(BF16)
    value = yield from line_stages(value)
    if value.ndim == 3:
        blocks = []
        for mask in range(value.shape[0]):
            other = jnp.bitwise_xor(me, mask)
            blocks.append(lax.dynamic_index_in_dim(value, other, 0, keepdims=False))
        moved = [swap(block, "shard", mask) if mask else block for mask, block in enumerate(blocks)]
        blocks = yield blocks, moved
        value = jnp.stack(blocks)
    far = yield value, swap(value, "rep", 1)
    return value, far


class Sums:
    def __init__(self, index, shapes):
        self.index, self.shapes = index, shapes
        self.outs = [None] * len(shapes)
        self.stages, self.moving, self.results = {}, {}, {}
        self.last, self.placed = (), None

    def ordered(self, value):
        out = () if self.placed is None else self.outs[self.placed]
        value, _, out = lax.optimization_barrier((value, self.last, out))
        if self.placed is not None:
            self.outs[self.placed] = out
            self.placed = None
        return value

    def start(self, name, *grads):
        grads = self.ordered([grad.astype(BF16) for grad in grads])
        self.stages[name] = half_stages(grads)
        self.last, self.moving[name] = next(self.stages[name])

    def step(self, *names):
        for name in names:
            moving = self.ordered(self.moving.pop(name))
            try:
                self.last, self.moving[name] = self.stages[name].send(moving)
            except StopIteration as stop:
                self.results[name] = stop.value

    def place(self, total, which, layer, parts, n, offset=0):
        shape, out = self.shapes[which], self.outs[which]
        total = self.ordered(total)
        if isinstance(total, tuple):
            out = place(total, self.index, layer, out, shape, parts, n, offset)
        else:
            out = place_whole(total, self.index, layer, out, shape, parts, n)
        self.outs[which], self.placed = out, which


def place_kernel(parts, n, c, steps, index_ref, near_ref, far_ref, *rest):
    out_ref = rest[-1]

    def put(source):
        if n == 0:
            out_ref[0] = source[...].astype(F32)
            return
        for mask in range(n):
            for part in range(parts):
                at = pl.multiple_of(index_ref[1 + mask] * c + part * n * c, c)
                out_ref[0, :, pl.ds(at, c)] = source[mask, :, part * c : (part + 1) * c].astype(F32)

    @pl.when(pl.program_id(0) < steps)
    def _():
        put(near_ref)

    @pl.when(pl.program_id(0) >= steps)
    def _():
        put(far_ref)


def place(halves, index, layer, out, shape, parts, n, offset):
    size = shape[1] // 2
    rows = size // 4 if size % 64 == 0 else size
    steps, skip = size // rows, offset // rows
    c = shape[2] // (parts * n) if n else 0
    lead = (n,) if n else ()
    block = lead + (rows, parts * c if n else shape[2])
    zeros = (0,) * len(lead)

    def target(s, index):
        first = index[0] * steps + s
        second = (1 - index[0]) * steps + s - steps
        return (layer, jnp.where(s < steps, first, second), 0)

    in_specs = [
        pl.BlockSpec(block, lambda s, index: zeros + (skip + jnp.minimum(s, steps - 1), 0)),
        pl.BlockSpec(block, lambda s, index: zeros + (skip + jnp.maximum(s - steps, 0), 0)),
    ]
    operands = [index, *halves]
    aliases = {}
    if out is not None:
        in_specs.append(pl.BlockSpec(memory_space=pl.ANY))
        operands.append(out)
        aliases = {3: 0}
    return pl.pallas_call(
        partial(place_kernel, parts, n, c, steps),
        grid_spec=pltpu.PrefetchScalarGridSpec(
            num_scalar_prefetch=1,
            grid=(2 * steps,),
            in_specs=in_specs,
            out_specs=pl.BlockSpec((1, rows, shape[2]), target),
        ),
        out_shape=jax.ShapeDtypeStruct(shape, F32),
        input_output_aliases=aliases,
        compiler_params=pltpu.CompilerParams(vmem_limit_bytes=32 * 1024 * 1024),
        name="place",
    )(*operands)


def place_whole_kernel(parts, n, c, index_ref, blocks_ref, *rest):
    out_ref = rest[-1]
    if n == 0:
        out_ref[0] = blocks_ref[...].astype(F32)
        return
    for mask in range(n):
        for part in range(parts):
            at = pl.multiple_of(index_ref[1 + mask] * c + part * n * c, c)
            out_ref[0, :, pl.ds(at, c)] = blocks_ref[mask, :, part * c : (part + 1) * c].astype(F32)


def place_whole(blocks, index, layer, out, shape, parts, n):
    rows = shape[1] // 8
    c = shape[2] // (parts * n) if n else 0
    lead = (n,) if n else ()
    zeros = (0,) * len(lead)
    block = lead + (rows, parts * c if n else shape[2])
    in_specs = [pl.BlockSpec(block, lambda s, index: zeros + (s, 0))]
    operands, aliases = [index, blocks], {}
    if out is not None:
        in_specs.append(pl.BlockSpec(memory_space=pl.ANY))
        operands.append(out)
        aliases = {2: 0}
    return pl.pallas_call(
        partial(place_whole_kernel, parts, n, c),
        grid_spec=pltpu.PrefetchScalarGridSpec(
            num_scalar_prefetch=1,
            grid=(shape[1] // rows,),
            in_specs=in_specs,
            out_specs=pl.BlockSpec((1, rows, shape[2]), lambda s, index: (layer, s, 0)),
        ),
        out_shape=jax.ShapeDtypeStruct(shape, F32),
        input_output_aliases=aliases,
        compiler_params=pltpu.CompilerParams(vmem_limit_bytes=32 * 1024 * 1024),
        name="place_whole",
    )(*operands)


def put_layer(total, layer, out, shape):
    out = jnp.zeros(shape, F32) if out is None else out
    return out.at[layer].set(total.astype(F32))


def attention_forward_kernel(heads, qkv_ref, rel_ref, allowed_ref, context_ref, probs_ref):
    width = heads * DH
    allowed = allowed_ref[0] > 0

    def pick(ref, group, head):
        at = group * width + head * DH
        return ref[:, at : at + DH]

    def skew(table):
        return pltpu.roll(table, LEN + 1, 1, stride=1, stride_axis=0)[:, :LEN]

    every = range(heads)
    q = [pick(qkv_ref, 0, head) for head in every]
    k = [pick(qkv_ref, 1, head) for head in every]
    by_key = [mm_nt(q[head], pick(rel_ref, 1, head)) for head in every]
    by_query = [mm_nt(k[head], pick(rel_ref, 0, head)) for head in every]
    direct = [mm_nt(q[head], k[head]) for head in every]
    by_key = [skew(table) for table in by_key]
    by_query = [skew(table) for table in by_query]
    scores = [(direct[head] + by_key[head] + by_query[head].T) * SCALE for head in every]
    scores = [jnp.where(allowed, score, NEG_FILL) for score in scores]
    tops = [jnp.max(score, axis=1, keepdims=True) for score in scores]
    terms = [jnp.exp(score - most) for score, most in zip(scores, tops)]
    totals = [jnp.sum(term, axis=1, keepdims=True) for term in terms]
    probs = [term / total for term, total in zip(terms, totals)]
    for head in every:
        probs_ref[0, head] = probs[head]
    context = [mm(probs[head].astype(BF16), pick(qkv_ref, 2, head)).astype(BF16) for head in every]
    context_ref[...] = jnp.concatenate(context, axis=1)


def attention_forward(qkv, rel_back, allowed, heads):
    count = allowed.shape[0]
    width = heads * DH
    return pl.pallas_call(
        partial(attention_forward_kernel, heads),
        grid=(count,),
        in_specs=[
            pl.BlockSpec((LEN, 3 * width), lambda s: (s, 0)),
            pl.BlockSpec((SPAN, 2 * width), lambda s: (0, 0)),
            pl.BlockSpec((1, LEN, LEN), lambda s: (s, 0, 0)),
        ],
        out_specs=[
            pl.BlockSpec((LEN, width), lambda s: (s, 0)),
            pl.BlockSpec((1, heads, LEN, LEN), lambda s: (s, 0, 0, 0)),
        ],
        out_shape=[
            jax.ShapeDtypeStruct((count * LEN, width), BF16),
            jax.ShapeDtypeStruct((count, heads, LEN, LEN), F32),
        ],
        compiler_params=pltpu.CompilerParams(vmem_limit_bytes=24 * 1024 * 1024),
        name="attention_forward",
    )(qkv, rel_back, allowed)


def attention_backward_kernel(heads, qkv_ref, rel_ref, probs_ref, grad_ref, dqkv_ref, drel_ref):
    width = heads * DH

    @pl.when(pl.program_id(0) == 0)
    def _():
        drel_ref[...] = jnp.zeros_like(drel_ref)

    row = lax.broadcasted_iota(jnp.int32, (LEN, LEN), 0)
    column = lax.broadcasted_iota(jnp.int32, (LEN, LEN), 1)
    flip = jnp.where(row + column == LEN - 1, 1.0, 0.0).astype(BF16)
    blank = jnp.zeros((LEN, LEN), F32)

    def pick(ref, group, head):
        at = group * width + head * DH
        return ref[:, at : at + DH]

    def spread(flipped):
        wide = jnp.concatenate([flipped, blank], axis=1)
        return pltpu.roll(wide, 0, 1, stride=1, stride_axis=0).astype(BF16)

    every = range(heads)
    q, k, v = [[pick(qkv_ref, group, head) for head in every] for group in range(3)]
    grad = [pick(grad_ref, 0, head) for head in every]
    probs = [probs_ref[0, head] for head in every]
    d_probs = [mm_nt(grad[head], v[head]) for head in every]
    d_value = [mm_tn(probs[head].astype(BF16), grad[head]) for head in every]
    inner = [jnp.sum(d_probs[head] * probs[head], axis=1, keepdims=True) for head in every]
    d_scores = [(probs[head] * (d_probs[head] - inner[head])).astype(BF16) for head in every]
    key_side = [mm(d_score, flip) for d_score in d_scores]
    query_side = [mm_tn(d_score, flip) for d_score in d_scores]
    key_side = [spread(flipped) for flipped in key_side]
    query_side = [spread(flipped) for flipped in query_side]
    d_query = [
        (mm(d_scores[head], k[head]) + mm(key_side[head], pick(rel_ref, 1, head))) * SCALE
        for head in every
    ]
    d_key = [
        (mm_tn(d_scores[head], q[head]) + mm(query_side[head], pick(rel_ref, 0, head))) * SCALE
        for head in every
    ]
    dqkv_ref[...] = jnp.concatenate(d_query + d_key + d_value, axis=1).astype(BF16)
    d_rel_q = [mm_tn(query_side[head], k[head]) * SCALE for head in every]
    d_rel_k = [mm_tn(key_side[head], q[head]) * SCALE for head in every]
    drel_ref[...] += jnp.concatenate(d_rel_q + d_rel_k, axis=1)


def attention_backward(qkv, rel_ahead, probs, d_context, heads):
    count = probs.shape[0]
    width = heads * DH
    return pl.pallas_call(
        partial(attention_backward_kernel, heads),
        grid=(count,),
        in_specs=[
            pl.BlockSpec((LEN, 3 * width), lambda s: (s, 0)),
            pl.BlockSpec((SPAN, 2 * width), lambda s: (0, 0)),
            pl.BlockSpec((1, heads, LEN, LEN), lambda s: (s, 0, 0, 0)),
            pl.BlockSpec((LEN, width), lambda s: (s, 0)),
        ],
        out_specs=[
            pl.BlockSpec((LEN, 3 * width), lambda s: (s, 0)),
            pl.BlockSpec((SPAN, 2 * width), lambda s: (0, 0)),
        ],
        out_shape=[
            jax.ShapeDtypeStruct((count * LEN, 3 * width), BF16),
            jax.ShapeDtypeStruct((SPAN, 2 * width), F32),
        ],
        compiler_params=pltpu.CompilerParams(vmem_limit_bytes=24 * 1024 * 1024),
        name="attention_backward",
    )(qkv, rel_ahead, probs, d_context)


def normed(values):
    centre = values - jnp.mean(values, axis=-1, keepdims=True)
    inverse = lax.rsqrt(jnp.mean(centre * centre, axis=-1, keepdims=True) + NORM_EPS)
    return centre * inverse, inverse


def norm_backward(upstream, values, gain):
    hat, inverse = normed(values)
    pushed = upstream * gain
    first = jnp.mean(pushed, axis=-1, keepdims=True)
    second = jnp.mean(pushed * hat, axis=-1, keepdims=True)
    back = inverse * (pushed - first - hat * second)
    return back, jnp.sum(upstream * hat, axis=0), jnp.sum(upstream, axis=0)


def gelu(x):
    return 0.5 * x * (1.0 + lax.erf(x * math.sqrt(0.5)))


def gelu_slope(x):
    density = jnp.exp(-0.5 * x * x) * (1.0 / math.sqrt(2.0 * math.pi))
    return 0.5 * (1.0 + lax.erf(x * math.sqrt(0.5))) + x * density


def per_device(
    tokens,
    cotangent,
    w_qkv,
    w_out,
    w_up,
    w_down,
    ln_gain,
    ln_bias,
    positions,
    segments,
    keep_mask,
    buckets,
):
    n = lax.axis_size("shard")
    me = lax.axis_index("shard")
    own = D // n
    heads = H // n
    order = group_order(n)

    staged = lax.axis_size("rep") == 8 and n == 4
    qkv_blocks = deal(w_qkv, 0, me, n, 3)
    up_blocks = deal(w_up, 0, me, n, 1)
    hidden = tokens.astype(F32)
    small_part = jnp.concatenate(
        [
            segments.astype(BF16),
            keep_mask.astype(BF16),
            jnp.stack([ln_gain, ln_bias]).transpose(0, 1, 3, 2).reshape(-1),
        ]
    )
    small_count = small_part.shape[0]
    small_part = jnp.pad(small_part, (0, 16 * D - small_count)).reshape(16, D)
    sides = gather_sides(jnp.concatenate([tokens, small_part], axis=0))
    sides = [side.reshape(-1, LEN + 16, D) for side in sides]
    hidden_sides = [side[:, :LEN].reshape(-1, D) for side in sides]
    small_all = jnp.concatenate([side[:, LEN:] for side in sides], axis=0)
    small_all = small_all.reshape(n, 16 * D)[:, :small_count].astype(F32)
    segment, keep = small_all[:, :LEN], small_all[:, LEN : 2 * LEN]
    allowed = (segment[:, :, None] == segment[:, None, :]) & (keep[:, None, :] == 1.0)
    allowed = (allowed | jnp.eye(LEN, dtype=bool)[None]).astype(F32)
    allowed_sides = (allowed[:2], allowed[2:])
    live_rows = gather_positions(positions, n, me)
    ahead = jnp.concatenate([buckets, buckets[-1:]])
    back = jnp.concatenate([buckets[::-1], buckets[:1]])
    wanted = jnp.concatenate([back, ahead]) - FIRST_ROW
    picks = (wanted[:, None] == jnp.arange(LIVE_ROWS)[None, :]).astype(BF16)
    rows_used = mm(picks, live_rows).astype(BF16)
    rows_ahead = rows_used[SPAN:]
    places = [order.index(place) for place in range(n)]
    places = jnp.take(jnp.array(places), jnp.bitwise_xor(me, jnp.arange(n)))
    norms = jnp.take(small_all[:, 2 * LEN :], places, axis=0).reshape(n, 2, LAYERS, 2, own)
    norms = norms.transpose(1, 2, 3, 0, 4).reshape(2, LAYERS, 2, D)
    gains, biases = norms[0], norms[1]

    weights = []
    for layer in range(LAYERS):
        if layer:
            qkv_blocks = deal(w_qkv, layer, me, n, 3, staged)
            qkv_blocks = [tie(block, up_blocks[-1]) for block in qkv_blocks]
            up_blocks = deal(w_up, layer, me, n, 1, staged)
        qkv_blocks = passed_around(qkv_blocks, n)
        up_blocks = passed_around([tie(block, qkv_blocks[-1]) for block in up_blocks], n)
        qkv_cols = collect(qkv_blocks, me, n, staged and layer > 0)
        up_cols = collect(up_blocks, me, n, staged and layer > 0)
        weights.append((qkv_cols, w_out[layer], up_cols, w_down[layer]))

    kept = []
    for layer in range(LAYERS):
        qkv_cols, out_rows, up_cols, down_rows = weights[layer]
        rel = mm(rows_used, qkv_cols[:, : 2 * own]).astype(BF16)
        qkv = [mm(side, qkv_cols).astype(BF16) for side in hidden_sides]
        attended = [
            attention_forward(side, rel[:SPAN], mask, heads)
            for side, mask in zip(qkv, allowed_sides)
        ]
        context = [side[0] for side in attended]
        probs = [side[1] for side in attended]
        attn_sum = hidden + scatter_sides(*[mm(side, out_rows) for side in context])
        mid = normed(attn_sum)[0] * gains[layer, 0] + biases[layer, 0]
        mid_sides = gather_sides(mid.astype(BF16))
        pre_act = [mm(side, up_cols) for side in mid_sides]
        activation = [gelu(side).astype(BF16) for side in pre_act]
        ffn_sum = mid + scatter_sides(*[mm(side, down_rows) for side in activation])
        kept.append((hidden_sides, qkv, rel[SPAN:], context, probs, attn_sum, mid_sides, pre_act, activation, ffn_sum))
        hidden = normed(ffn_sum)[0] * gains[layer, 1] + biases[layer, 1]
        if layer < LAYERS - 1:
            hidden_sides = gather_sides(hidden.astype(BF16))
    output = hidden.astype(BF16)

    def over_tokens(left, right):
        return mm_tn(left[0], right[0]) + mm_tn(left[1], right[1])

    upstream = cotangent.astype(F32)
    others = jnp.bitwise_xor(me, jnp.arange(n, dtype=jnp.int32))
    shapes = [(LAYERS,) + weight.shape[1:] for weight in (w_qkv, w_out, w_up, w_down)]
    upper = lax.axis_index("rep") % 2
    sums = Sums(jnp.concatenate([upper.reshape(1), others]), shapes)
    grads = {}
    small = [None] * LAYERS
    row_grads = jnp.zeros((SPAN, D), F32)
    top = LAYERS - 1

    def served(*actions):
        if not staged:
            return None

        def meanwhile(sent):
            sums.last = (sums.last, sent)
            for action in actions:
                action()
            return sums.last

        return meanwhile

    def stepping(*names):
        return lambda: sums.step(*names)

    for layer in reversed(range(LAYERS)):
        qkv_cols, out_rows, up_cols, down_rows = weights[layer]
        hidden_sides, qkv, rel, context, probs, attn_sum, mid_sides, pre_act, activation, ffn_sum = kept[layer]
        first = layer == top
        d_ffn, d_gain_two, d_bias_two = norm_backward(upstream, ffn_sum, gains[layer, 1])
        hook = None if first else served(lambda: sums.start("Q1", grads[top][0]))
        branch = gather_sides(d_ffn.astype(BF16), hook)
        d_pre = [
            (mm_nt(side, down_rows) * gelu_slope(pre)).astype(BF16)
            for side, pre in zip(branch, pre_act)
        ]
        g_down = over_tokens(activation, branch).astype(BF16)
        if first:
            hook = served(lambda: sums.start("D1", g_down))
        else:
            hook = served(stepping("D1", "U1"), lambda: sums.start("D0", g_down, grads[top][1]))
        d_mid = d_ffn + scatter_sides(*[mm_nt(side, up_cols) for side in d_pre], hook)
        g_up = over_tokens(mid_sides, d_pre).astype(BF16).reshape(n, own, -1)
        d_attn, d_gain_one, d_bias_one = norm_backward(d_mid, attn_sum, gains[layer, 0])
        hook = None if first else served(stepping("Q1"))
        att = gather_sides(d_attn.astype(BF16), hook)
        d_context = [mm_nt(side, out_rows).astype(BF16) for side in att]
        attended = [
            attention_backward(side, rel, p, grad, heads)
            for side, p, grad in zip(qkv, probs, d_context)
        ]
        d_qkv = [part[0] for part in attended]
        d_rel = (attended[0][1] + attended[1][1]).astype(BF16)
        if first:
            hook = served(stepping("D1"), lambda: sums.start("U1", g_up))
        else:
            hook = served(stepping("D1", "U1"), lambda: sums.start("U0", g_up))
        upstream = d_attn + scatter_sides(*[mm_nt(side, qkv_cols) for side in d_qkv], hook)
        g_out = over_tokens(context, att).astype(BF16)
        g_qkv = over_tokens(hidden_sides, d_qkv) + mm_tn(
            rows_ahead, jnp.concatenate([d_rel, jnp.zeros((SPAN, own), BF16)], axis=1)
        )
        g_qkv = g_qkv.astype(BF16).reshape(n, own, -1)
        row_grads = row_grads + mm_nt(d_rel, qkv_cols[:, : 2 * own])
        small[layer] = (
            jnp.stack([d_gain_one, d_gain_two]),
            jnp.stack([d_bias_one, d_bias_two]),
        )
        grads[layer] = (g_qkv, g_out, g_up, g_down)

    owners = jnp.bitwise_xor(me, jnp.array(order))
    norm_part = jnp.stack(
        [jnp.stack([entry[0] for entry in small]), jnp.stack([entry[1] for entry in small])]
    )
    norm_part = norm_part.reshape(2, LAYERS, 2, n, own).transpose(3, 0, 1, 2, 4)
    norm_part = jnp.take(norm_part, owners, axis=0).reshape(n, 2 * LAYERS * 2 * own)
    norm_part = scatter_sides(norm_part[:2], norm_part[2:])
    position_part = scatter_positions(row_grads, ahead, positions.shape[0], n, me)
    norm_count = 2 * LAYERS * 2 * own
    norm_rows = (norm_count + D - 1) // D
    norm_part = jnp.pad(norm_part.reshape(-1), (0, norm_rows * D - norm_count)).reshape(norm_rows, D)
    packed = jnp.concatenate([position_part, norm_part], axis=0).astype(BF16)

    if staged:
        rows = packed.shape[0]
        packed = jnp.pad(packed, ((0, -rows % 32), (0, 0)))
        finishers = {
            "D1": [(3, 1, 1, 0, 0)],
            "U1": [(2, 1, 1, n, 0)],
            "Q1": [(0, 1, 3, n, 0)],
            "D0": [(3, 0, 1, 0, 0), (1, 1, 1, 0, own * 2)],
            "U0": [(2, 0, 1, n, 0)],
            "Q0": [(0, 0, 3, n, 0)],
            "R": [(1, 0, 1, 0, 0)],
        }
        starters = {"Q0": [g_qkv], "R": [g_out, packed]}
        sums.last = (sums.last, upstream)
        for name in TAIL:
            if name not in sums.stages:
                sums.start(name, *starters[name])
                continue
            sums.step(name)
            if name in sums.results:
                for target in finishers[name]:
                    sums.place(sums.results[name], *target)
        out_grads = sums.outs
        near, far = [half[own // 2 :] for half in sums.results["R"]]
        lower, higher = jnp.where(upper == 0, near, far), jnp.where(upper == 0, far, near)
        packed = jnp.concatenate([lower, higher], axis=0)[:rows]
    else:
        packed = lax.psum(packed, "rep")
        out_grads = []
        for which, shape in enumerate(shapes):
            out = None
            for layer in range(LAYERS):
                total = grads[layer][which].astype(BF16)
                if which in (0, 2):
                    parts = 3 if which == 0 else 1
                    total = to_owners(total.reshape(n, own, -1), me, n)
                    total = jnp.take(total, others, axis=0).reshape(n, own, parts, -1)
                    total = total.transpose(1, 2, 0, 3).reshape(shape[1:])
                out = put_layer(lax.psum(total, "rep"), layer, out, shape)
            out_grads.append(out)

    grad_positions = packed[:-norm_rows].astype(F32)
    if grad_positions.shape[0] < positions.shape[0]:
        gap = positions.shape[0] - grad_positions.shape[0]
        grad_positions = jnp.where(
            me == 1,
            jnp.pad(grad_positions, ((gap, 0), (0, 0))),
            jnp.where(me == 2, jnp.pad(grad_positions, ((0, gap), (0, 0))), 0.0),
        )
    norm_part = packed[-norm_rows:].astype(F32).reshape(-1)[:norm_count].reshape(2, LAYERS, 2, own).transpose(0, 1, 3, 2)
    return (output, upstream, *out_grads, norm_part[0], norm_part[1], grad_positions)


def solution(mesh):
    tokens = P(("rep", "shard"), None)
    rows = P(None, "shard", None)
    labels = P(("rep", "shard"))
    return jax.shard_map(
        per_device,
        mesh=mesh,
        in_specs=(
            tokens,
            tokens,
            rows,
            rows,
            rows,
            rows,
            rows,
            rows,
            P("shard", None),
            labels,
            labels,
            P(),
        ),
        out_specs=(tokens, tokens, rows, rows, rows, rows, rows, rows, P("shard", None)),
        check_vma=False,
    )
```

```python
from functools import partial
import math

import jax
import jax.numpy as jnp
from jax import lax
from jax.experimental import pallas as pl
from jax.experimental.pallas import tpu as pltpu
from jax.sharding import PartitionSpec as P

D = 1024
H = 16
DH = 64
LAYERS = 2
LEN = 128
SPAN = 2 * LEN
FIRST_ROW = 160
LIVE_ROWS = 192
SCALE = 1.0 / math.sqrt(3 * DH)
NEG_FILL = -1e30
NORM_EPS = 1e-07
F32 = jnp.float32
BF16 = jnp.bfloat16


def mm(a, b):
    return jnp.dot(a, b, preferred_element_type=F32)


def mm_nt(a, b):
    return lax.dot_general(a, b, (((1,), (1,)), ((), ())), preferred_element_type=F32)


def mm_tn(a, b):
    return lax.dot_general(a, b, (((0,), (0,)), ((), ())), preferred_element_type=F32)


def swap(value, axis, mask):
    size = lax.axis_size(axis)
    return lax.ppermute(value, axis, [(i, i ^ mask) for i in range(size)])


def far_order(n):
    span, mask = [0], n // 2
    while mask > 1:
        span = span + [place ^ mask for place in span]
        mask //= 2
    return span[1:]


def group_order(n):
    far = far_order(n)
    return [0, 1] + far + [place ^ 1 for place in far]


def gather_sides(own, meanwhile=None):
    n = lax.axis_size("shard")
    near = jnp.concatenate([own, swap(own, "shard", 1)], axis=0)
    span, mask = own, n // 2
    while mask > 1:
        passed = swap(span, "shard", mask)
        span = passed if mask == 2 and n == 4 else jnp.concatenate([span, passed], axis=0)
        mask //= 2
    far = span if n == 4 else span[own.shape[0] :]
    if meanwhile is not None:
        far = tie(far, meanwhile(own))
    return near, jnp.concatenate([far, swap(far, "shard", 1)], axis=0)


def gather_group(own):
    return jnp.concatenate(gather_sides(own), axis=0)


def scatter_positions(row_grads, ahead, rows, n, me):
    live = jnp.arange(SPAN) < SPAN - 1
    if n == 4 and rows == 128:
        wanted = FIRST_ROW + jnp.arange(LIVE_ROWS)
    else:
        owners = jnp.bitwise_xor(me, jnp.array(group_order(n)))
        wanted = (owners[:, None] * rows + jnp.arange(rows)[None, :]).reshape(-1)
    picks = ((wanted[:, None] == ahead[None, :]) & live[None, :]).astype(BF16)
    by_row = mm(picks, row_grads.astype(BF16))
    if n != 4 or rows != 128:
        return scatter_sides(by_row[: 2 * rows], by_row[2 * rows :])
    size = LIVE_ROWS // 2
    odd = me % 2 == 1
    mine = jnp.where(odd, by_row[:size], by_row[size:])
    total = mine + swap(jnp.where(odd, by_row[size:], by_row[:size]).astype(BF16), "shard", 1).astype(F32)
    return total + swap(total.astype(BF16), "shard", 2).astype(F32)


def scatter_sides(near, far, meanwhile=None):
    n = lax.axis_size("shard")
    half = far.shape[0] // 2
    far = far[:half] + swap(far[half:].astype(BF16), "shard", 1).astype(F32)
    half = near.shape[0] // 2
    near = near[:half] + swap(near[half:].astype(BF16), "shard", 1).astype(F32)
    if n == 4:
        far = far.astype(BF16)
        passed = swap(far, "shard", 2)
        if meanwhile is not None:
            passed = tie(passed, meanwhile(far))
        return near + passed.astype(F32)
    total, mask = jnp.concatenate([near, far], axis=0), 2
    while mask < n:
        half = total.shape[0] // 2
        total = total[:half] + swap(total[half:].astype(BF16), "shard", mask).astype(F32)
        mask *= 2
    return total


def gather_positions(positions, n, me):
    last_row = FIRST_ROW + LIVE_ROWS
    rows = positions.shape[0]
    if n != 4 or rows != 128:
        whole = lax.all_gather(positions, "shard", axis=0, tiled=True)
        return whole[FIRST_ROW:last_row]
    size = LIVE_ROWS // 2
    mine = jnp.where(me == 1, positions[rows - size :], positions[:size])
    passed = lax.ppermute(mine, "shard", [(1, 3), (2, 0)])
    held = jnp.where((me == 1) | (me == 2), mine, passed)
    other = swap(held, "shard", 1)
    low = me % 2 == 1
    return jnp.concatenate([jnp.where(low, held, other), jnp.where(low, other, held)], axis=0)


def copy_blocks_kernel(n, me_ref, *refs):
    for source, target in zip(refs[:n], refs[n:]):
        target[...] = source[0]


def deal(weight, layer, me, n, parts, shared=False):
    rows = weight.shape[1]
    c = weight.shape[2] // (parts * n)
    if c % 128:
        blocks = []
        for mask in range(n):
            other = jnp.bitwise_xor(me, mask)
            pieces = [
                lax.dynamic_slice(weight, (layer, 0, (part * n + other) * c), (1, rows, c))[0]
                for part in range(parts)
            ]
            blocks.append(jnp.concatenate(pieces, axis=1))
        return blocks
    split = 1 if parts > 1 or c % 512 else 4

    count = n - 1 if shared else n

    def source_spec(mask):
        def where(part, cut, me):
            other = jnp.bitwise_xor(me[0], mask + me[1] if shared and mask == 2 else mask)
            return (layer, 0, (part * n + other) * split + cut)

        return pl.BlockSpec((1, rows, c // split), where)

    target = pl.BlockSpec((rows, c // split), lambda part, cut, me: (0, part * split + cut))
    return pl.pallas_call(
        partial(copy_blocks_kernel, count),
        grid_spec=pltpu.PrefetchScalarGridSpec(
            num_scalar_prefetch=1,
            grid=(parts, split),
            in_specs=[source_spec(mask) for mask in range(count)],
            out_specs=[target] * count,
        ),
        out_shape=[jax.ShapeDtypeStruct((rows, parts * c), BF16)] * count,
        compiler_params=pltpu.CompilerParams(vmem_limit_bytes=24 * 1024 * 1024),
        name="deal",
    )(place_of(me), *([weight] * count))


def collect_kernel(n, shared, me_ref, *refs):
    step = pl.program_id(1)
    for at in range(n):
        mask = at
        if shared and at > 1:
            mask = 2 + me_ref[1] if at == 2 else 3 - me_ref[1]

        @pl.when(step == jnp.bitwise_xor(me_ref[0], mask))
        def _():
            refs[n][...] = refs[at][...]


def collect(blocks, me, n, shared):
    rows, width = blocks[0].shape
    if rows % 16 or width % 256:
        whole = jnp.zeros((n * rows, width), BF16)
        for mask, block in enumerate(blocks):
            other = jnp.bitwise_xor(me, mask)
            whole = lax.dynamic_update_slice(whole, block, (other * rows, 0))
        return whole
    c = width // 2
    return pl.pallas_call(
        partial(collect_kernel, n, shared),
        grid_spec=pltpu.PrefetchScalarGridSpec(
            num_scalar_prefetch=1,
            grid=(width // c, n),
            in_specs=[pl.BlockSpec((rows, c), lambda cut, step, me: (0, cut))] * n,
            out_specs=pl.BlockSpec((rows, c), lambda cut, step, me: (step, cut)),
        ),
        out_shape=jax.ShapeDtypeStruct((n * rows, width), BF16),
        compiler_params=pltpu.CompilerParams(vmem_limit_bytes=24 * 1024 * 1024),
        name="collect",
    )(place_of(me), *blocks)


def place_of(me):
    return jnp.stack([me, lax.axis_index("rep") % 2])


def passed_around(blocks, n):
    passed = [swap(block, "shard", mask) if mask else block for mask, block in enumerate(blocks[:2])]
    if len(blocks) == n:
        return passed + [swap(block, "shard", mask + 2) for mask, block in enumerate(blocks[2:])]
    size = lax.axis_size("rep")
    pairs = [(r * n + i, r * n + (i ^ (2 + r % 2))) for r in range(size) for i in range(n)]
    across = lax.ppermute(blocks[2], ("rep", "shard"), pairs)
    return passed + [across, swap(across, "rep", 1)]


def to_owners(columns, me, n):
    blocks = []
    for mask in range(n):
        block = lax.dynamic_index_in_dim(columns, jnp.bitwise_xor(me, mask), 0, keepdims=False)
        blocks.append(swap(block, "shard", mask) if mask else block)
    return jnp.stack(blocks)


def tie(value, after):
    return lax.optimization_barrier((value, after))[0]


INWARDS = [(0, 2), (1, 3), (6, 4), (7, 5)]
ACROSS = [(2, 4), (3, 5), (4, 2), (5, 3)]
OUTWARDS = [(2, 0), (3, 1), (4, 6), (5, 7)]
TAIL = (
    "D0", "U1", "Q1", "Q0", "D1", "R", "U0", "D0", "Q1", "U1", "Q0", "R", "U1", "U0", "D0",
    "Q1", "D1", "Q0", "Q1", "U0", "R", "D0", "U1", "Q1", "R", "U0", "Q0", "R", "U0", "D0",
    "Q0", "Q0", "R", "U0", "Q0",
)


def line_stages(value):
    rep = lax.axis_index("rep")
    for pairs in (INWARDS, ACROSS):
        passed = yield value, lax.ppermute(value, "rep", pairs)
        value = (value.astype(F32) + passed.astype(F32)).astype(BF16)
    passed = yield value, lax.ppermute(value, "rep", OUTWARDS)
    return jnp.where((rep >= 2) & (rep < 6), value, passed)


def halves_of(grads, upper):
    pieces = []
    for grad in grads:
        size = grad.shape[-2] // 2
        pieces.append(lax.dynamic_slice_in_dim(grad, upper * size, size, grad.ndim - 2))
    return pieces[0] if len(pieces) == 1 else jnp.concatenate(pieces, axis=0)


def half_stages(grads):
    upper = lax.axis_index("rep") % 2
    me = lax.axis_index("shard")
    sent = halves_of(grads, 1 - upper)
    held = halves_of(grads, upper)
    passed = yield sent, swap(sent, "rep", 1)
    value = (held.astype(F32) + passed.astype(F32)).astype(BF16)
    value = yield from line_stages(value)
    if value.ndim == 3:
        blocks = []
        for mask in range(value.shape[0]):
            other = jnp.bitwise_xor(me, mask)
            blocks.append(lax.dynamic_index_in_dim(value, other, 0, keepdims=False))
        moved = [swap(block, "shard", mask) if mask else block for mask, block in enumerate(blocks)]
        blocks = yield blocks, moved
        value = jnp.stack(blocks)
    far = yield value, swap(value, "rep", 1)
    return value, far


class Sums:
    def __init__(self, index, shapes):
        self.index, self.shapes = index, shapes
        self.outs = [None] * len(shapes)
        self.stages, self.moving, self.results = {}, {}, {}
        self.last, self.placed, self.last_sent = (), None, {}

    def ordered(self, value):
        out = () if self.placed is None else self.outs[self.placed]
        value, _, out = lax.optimization_barrier((value, self.last, out))
        if self.placed is not None:
            self.outs[self.placed] = out
            self.placed = None
        return value

    def start(self, name, *grads):
        grads = self.ordered([grad.astype(BF16) for grad in grads])
        self.stages[name] = half_stages(grads)
        self.last, self.moving[name] = next(self.stages[name])

    def step(self, *names):
        for name in names:
            moving = self.ordered(self.moving.pop(name))
            try:
                self.last, self.moving[name] = self.stages[name].send(moving)
                self.last_sent[name] = self.last
            except StopIteration as stop:
                self.results[name] = stop.value

    def place_apart(self, name, which, layer, parts, n):
        args = (self.index, layer)
        near = self.ordered(self.last_sent[name])
        out = place_half(near, False, *args, self.outs[which], self.shapes[which], parts, n)
        self.outs[which], self.placed = out, which
        self.step(name)
        far = self.ordered(self.results[name][1])
        out = place_half(far, True, *args, self.outs[which], self.shapes[which], parts, n)
        self.outs[which], self.placed = out, which

    def place(self, total, which, layer, parts, n, offset=0):
        shape, out = self.shapes[which], self.outs[which]
        total = self.ordered(total)
        if isinstance(total, tuple):
            out = place(total, self.index, layer, out, shape, parts, n, offset)
        else:
            out = place_whole(total, self.index, layer, out, shape, parts, n)
        self.outs[which], self.placed = out, which


def place_kernel(parts, n, c, steps, index_ref, near_ref, far_ref, *rest):
    out_ref = rest[-1]

    def put(source):
        if n == 0:
            out_ref[0] = source[...].astype(F32)
            return
        for mask in range(n):
            for part in range(parts):
                at = pl.multiple_of(index_ref[1 + mask] * c + part * n * c, c)
                out_ref[0, :, pl.ds(at, c)] = source[mask, :, part * c : (part + 1) * c].astype(F32)

    @pl.when(pl.program_id(0) < steps)
    def _():
        put(near_ref)

    @pl.when(pl.program_id(0) >= steps)
    def _():
        put(far_ref)


def place(halves, index, layer, out, shape, parts, n, offset):
    size = shape[1] // 2
    rows = size // 4 if size % 64 == 0 else size
    steps, skip = size // rows, offset // rows
    c = shape[2] // (parts * n) if n else 0
    lead = (n,) if n else ()
    block = lead + (rows, parts * c if n else shape[2])
    zeros = (0,) * len(lead)

    def target(s, index):
        first = index[0] * steps + s
        second = (1 - index[0]) * steps + s - steps
        return (layer, jnp.where(s < steps, first, second), 0)

    in_specs = [
        pl.BlockSpec(block, lambda s, index: zeros + (skip + jnp.minimum(s, steps - 1), 0)),
        pl.BlockSpec(block, lambda s, index: zeros + (skip + jnp.maximum(s - steps, 0), 0)),
    ]
    operands = [index, *halves]
    aliases = {}
    if out is not None:
        in_specs.append(pl.BlockSpec(memory_space=pl.ANY))
        operands.append(out)
        aliases = {3: 0}
    return pl.pallas_call(
        partial(place_kernel, parts, n, c, steps),
        grid_spec=pltpu.PrefetchScalarGridSpec(
            num_scalar_prefetch=1,
            grid=(2 * steps,),
            in_specs=in_specs,
            out_specs=pl.BlockSpec((1, rows, shape[2]), target),
        ),
        out_shape=jax.ShapeDtypeStruct(shape, F32),
        input_output_aliases=aliases,
        compiler_params=pltpu.CompilerParams(vmem_limit_bytes=32 * 1024 * 1024),
        name="place",
    )(*operands)


def place_whole_kernel(parts, n, c, index_ref, blocks_ref, *rest):
    out_ref = rest[-1]
    if n == 0:
        out_ref[0] = blocks_ref[...].astype(F32)
        return
    for mask in range(n):
        for part in range(parts):
            at = pl.multiple_of(index_ref[1 + mask] * c + part * n * c, c)
            out_ref[0, :, pl.ds(at, c)] = blocks_ref[mask, :, part * c : (part + 1) * c].astype(F32)


def place_whole(blocks, index, layer, out, shape, parts, n):
    rows = shape[1] // 8
    c = shape[2] // (parts * n) if n else 0
    lead = (n,) if n else ()
    zeros = (0,) * len(lead)
    block = lead + (rows, parts * c if n else shape[2])
    in_specs = [pl.BlockSpec(block, lambda s, index: zeros + (s, 0))]
    operands, aliases = [index, blocks], {}
    if out is not None:
        in_specs.append(pl.BlockSpec(memory_space=pl.ANY))
        operands.append(out)
        aliases = {2: 0}
    return pl.pallas_call(
        partial(place_whole_kernel, parts, n, c),
        grid_spec=pltpu.PrefetchScalarGridSpec(
            num_scalar_prefetch=1,
            grid=(shape[1] // rows,),
            in_specs=in_specs,
            out_specs=pl.BlockSpec((1, rows, shape[2]), lambda s, index: (layer, s, 0)),
        ),
        out_shape=jax.ShapeDtypeStruct(shape, F32),
        input_output_aliases=aliases,
        compiler_params=pltpu.CompilerParams(vmem_limit_bytes=32 * 1024 * 1024),
        name="place_whole",
    )(*operands)


def place_half(source, second, index, layer, out, shape, parts, n):
    size = shape[1] // 2
    rows = size // 4 if size % 64 == 0 else size
    steps, c = size // rows, shape[2] // (parts * n)

    def kernel(index_ref, source_ref, *rest):
        for mask in range(n):
            for part in range(parts):
                at = pl.multiple_of(index_ref[1 + mask] * c + part * n * c, c)
                piece = source_ref[mask, :, part * c : (part + 1) * c]
                rest[-1][0, :, pl.ds(at, c)] = piece.astype(F32)

    def target(s, index):
        half = 1 - index[0] if second else index[0]
        return (layer, half * steps + s, 0)

    in_specs = [pl.BlockSpec((n, rows, parts * c), lambda s, index: (0, s, 0))]
    operands, aliases = [index, source], {}
    if out is not None:
        in_specs.append(pl.BlockSpec(memory_space=pl.ANY))
        operands.append(out)
        aliases = {2: 0}
    return pl.pallas_call(
        kernel,
        grid_spec=pltpu.PrefetchScalarGridSpec(
            num_scalar_prefetch=1,
            grid=(steps,),
            in_specs=in_specs,
            out_specs=pl.BlockSpec((1, rows, shape[2]), target),
        ),
        out_shape=jax.ShapeDtypeStruct(shape, F32),
        input_output_aliases=aliases,
        compiler_params=pltpu.CompilerParams(vmem_limit_bytes=32 * 1024 * 1024),
        name="place_half",
    )(*operands)


def put_layer(total, layer, out, shape):
    out = jnp.zeros(shape, F32) if out is None else out
    return out.at[layer].set(total.astype(F32))


def attention_forward_kernel(heads, qkv_ref, rel_ref, allowed_ref, context_ref, probs_ref):
    width = heads * DH
    allowed = allowed_ref[0] > 0

    def pick(ref, group, head):
        at = group * width + head * DH
        return ref[:, at : at + DH]

    def skew(table):
        return pltpu.roll(table, LEN + 1, 1, stride=1, stride_axis=0)[:, :LEN]

    every = range(heads)
    q = [pick(qkv_ref, 0, head) for head in every]
    k = [pick(qkv_ref, 1, head) for head in every]
    by_key = [mm_nt(q[head], pick(rel_ref, 1, head)) for head in every]
    by_query = [mm_nt(k[head], pick(rel_ref, 0, head)) for head in every]
    direct = [mm_nt(q[head], k[head]) for head in every]
    by_key = [skew(table) for table in by_key]
    by_query = [skew(table) for table in by_query]
    scores = [(direct[head] + by_key[head] + by_query[head].T) * SCALE for head in every]
    scores = [jnp.where(allowed, score, NEG_FILL) for score in scores]
    tops = [jnp.max(score, axis=1, keepdims=True) for score in scores]
    terms = [jnp.exp(score - most) for score, most in zip(scores, tops)]
    totals = [jnp.sum(term, axis=1, keepdims=True) for term in terms]
    probs = [term / total for term, total in zip(terms, totals)]
    for head in every:
        probs_ref[0, head] = probs[head]
    context = [mm(probs[head].astype(BF16), pick(qkv_ref, 2, head)).astype(BF16) for head in every]
    context_ref[...] = jnp.concatenate(context, axis=1)


def attention_forward(qkv, rel_back, allowed, heads):
    count = allowed.shape[0]
    width = heads * DH
    return pl.pallas_call(
        partial(attention_forward_kernel, heads),
        grid=(count,),
        in_specs=[
            pl.BlockSpec((LEN, 3 * width), lambda s: (s, 0)),
            pl.BlockSpec((SPAN, 2 * width), lambda s: (0, 0)),
            pl.BlockSpec((1, LEN, LEN), lambda s: (s, 0, 0)),
        ],
        out_specs=[
            pl.BlockSpec((LEN, width), lambda s: (s, 0)),
            pl.BlockSpec((1, heads, LEN, LEN), lambda s: (s, 0, 0, 0)),
        ],
        out_shape=[
            jax.ShapeDtypeStruct((count * LEN, width), BF16),
            jax.ShapeDtypeStruct((count, heads, LEN, LEN), F32),
        ],
        compiler_params=pltpu.CompilerParams(vmem_limit_bytes=24 * 1024 * 1024),
        name="attention_forward",
    )(qkv, rel_back, allowed)


def attention_backward_kernel(heads, qkv_ref, rel_ref, probs_ref, grad_ref, dqkv_ref, drel_ref):
    width = heads * DH

    @pl.when(pl.program_id(0) == 0)
    def _():
        drel_ref[...] = jnp.zeros_like(drel_ref)

    row = lax.broadcasted_iota(jnp.int32, (LEN, LEN), 0)
    column = lax.broadcasted_iota(jnp.int32, (LEN, LEN), 1)
    flip = jnp.where(row + column == LEN - 1, 1.0, 0.0).astype(BF16)
    blank = jnp.zeros((LEN, LEN), F32)

    def pick(ref, group, head):
        at = group * width + head * DH
        return ref[:, at : at + DH]

    def spread(flipped):
        wide = jnp.concatenate([flipped, blank], axis=1)
        return pltpu.roll(wide, 0, 1, stride=1, stride_axis=0).astype(BF16)

    every = range(heads)
    q, k, v = [[pick(qkv_ref, group, head) for head in every] for group in range(3)]
    grad = [pick(grad_ref, 0, head) for head in every]
    probs = [probs_ref[0, head] for head in every]
    d_probs = [mm_nt(grad[head], v[head]) for head in every]
    d_value = [mm_tn(probs[head].astype(BF16), grad[head]) for head in every]
    inner = [jnp.sum(d_probs[head] * probs[head], axis=1, keepdims=True) for head in every]
    d_scores = [(probs[head] * (d_probs[head] - inner[head])).astype(BF16) for head in every]
    key_side = [mm(d_score, flip) for d_score in d_scores]
    query_side = [mm_tn(d_score, flip) for d_score in d_scores]
    key_side = [spread(flipped) for flipped in key_side]
    query_side = [spread(flipped) for flipped in query_side]
    d_query = [
        (mm(d_scores[head], k[head]) + mm(key_side[head], pick(rel_ref, 1, head))) * SCALE
        for head in every
    ]
    d_key = [
        (mm_tn(d_scores[head], q[head]) + mm(query_side[head], pick(rel_ref, 0, head))) * SCALE
        for head in every
    ]
    dqkv_ref[...] = jnp.concatenate(d_query + d_key + d_value, axis=1).astype(BF16)
    d_rel_q = [mm_tn(query_side[head], k[head]) * SCALE for head in every]
    d_rel_k = [mm_tn(key_side[head], q[head]) * SCALE for head in every]
    drel_ref[...] += jnp.concatenate(d_rel_q + d_rel_k, axis=1)


def attention_backward(qkv, rel_ahead, probs, d_context, heads):
    count = probs.shape[0]
    width = heads * DH
    return pl.pallas_call(
        partial(attention_backward_kernel, heads),
        grid=(count,),
        in_specs=[
            pl.BlockSpec((LEN, 3 * width), lambda s: (s, 0)),
            pl.BlockSpec((SPAN, 2 * width), lambda s: (0, 0)),
            pl.BlockSpec((1, heads, LEN, LEN), lambda s: (s, 0, 0, 0)),
            pl.BlockSpec((LEN, width), lambda s: (s, 0)),
        ],
        out_specs=[
            pl.BlockSpec((LEN, 3 * width), lambda s: (s, 0)),
            pl.BlockSpec((SPAN, 2 * width), lambda s: (0, 0)),
        ],
        out_shape=[
            jax.ShapeDtypeStruct((count * LEN, 3 * width), BF16),
            jax.ShapeDtypeStruct((SPAN, 2 * width), F32),
        ],
        compiler_params=pltpu.CompilerParams(vmem_limit_bytes=24 * 1024 * 1024),
        name="attention_backward",
    )(qkv, rel_ahead, probs, d_context)


def normed(values):
    centre = values - jnp.mean(values, axis=-1, keepdims=True)
    inverse = lax.rsqrt(jnp.mean(centre * centre, axis=-1, keepdims=True) + NORM_EPS)
    return centre * inverse, inverse


def norm_backward(upstream, values, gain):
    hat, inverse = normed(values)
    pushed = upstream * gain
    first = jnp.mean(pushed, axis=-1, keepdims=True)
    second = jnp.mean(pushed * hat, axis=-1, keepdims=True)
    back = inverse * (pushed - first - hat * second)
    return back, jnp.sum(upstream * hat, axis=0), jnp.sum(upstream, axis=0)


def gelu(x):
    return 0.5 * x * (1.0 + lax.erf(x * math.sqrt(0.5)))


def gelu_slope(x):
    density = jnp.exp(-0.5 * x * x) * (1.0 / math.sqrt(2.0 * math.pi))
    return 0.5 * (1.0 + lax.erf(x * math.sqrt(0.5))) + x * density


def per_device(
    tokens,
    cotangent,
    w_qkv,
    w_out,
    w_up,
    w_down,
    ln_gain,
    ln_bias,
    positions,
    segments,
    keep_mask,
    buckets,
):
    n = lax.axis_size("shard")
    me = lax.axis_index("shard")
    own = D // n
    heads = H // n
    order = group_order(n)

    staged = lax.axis_size("rep") == 8 and n == 4
    qkv_blocks = deal(w_qkv, 0, me, n, 3)
    up_blocks = deal(w_up, 0, me, n, 1)
    hidden = tokens.astype(F32)
    small_part = jnp.concatenate(
        [
            segments.astype(BF16),
            keep_mask.astype(BF16),
            jnp.stack([ln_gain, ln_bias]).transpose(0, 1, 3, 2).reshape(-1),
        ]
    )
    small_count = small_part.shape[0]
    small_part = jnp.pad(small_part, (0, 16 * D - small_count)).reshape(16, D)
    sides = gather_sides(jnp.concatenate([tokens, small_part], axis=0))
    sides = [side.reshape(-1, LEN + 16, D) for side in sides]
    hidden_sides = [side[:, :LEN].reshape(-1, D) for side in sides]
    small_all = jnp.concatenate([side[:, LEN:] for side in sides], axis=0)
    small_all = small_all.reshape(n, 16 * D)[:, :small_count].astype(F32)
    segment, keep = small_all[:, :LEN], small_all[:, LEN : 2 * LEN]
    allowed = (segment[:, :, None] == segment[:, None, :]) & (keep[:, None, :] == 1.0)
    allowed = (allowed | jnp.eye(LEN, dtype=bool)[None]).astype(F32)
    allowed_sides = (allowed[:2], allowed[2:])
    live_rows = gather_positions(positions, n, me)
    ahead = jnp.concatenate([buckets, buckets[-1:]])
    back = jnp.concatenate([buckets[::-1], buckets[:1]])
    wanted = jnp.concatenate([back, ahead]) - FIRST_ROW
    picks = (wanted[:, None] == jnp.arange(LIVE_ROWS)[None, :]).astype(BF16)
    rows_used = mm(picks, live_rows).astype(BF16)
    rows_ahead = rows_used[SPAN:]
    places = [order.index(place) for place in range(n)]
    places = jnp.take(jnp.array(places), jnp.bitwise_xor(me, jnp.arange(n)))
    norms = jnp.take(small_all[:, 2 * LEN :], places, axis=0).reshape(n, 2, LAYERS, 2, own)
    norms = norms.transpose(1, 2, 3, 0, 4).reshape(2, LAYERS, 2, D)
    gains, biases = norms[0], norms[1]

    weights = []
    for layer in range(LAYERS):
        if layer:
            qkv_blocks = deal(w_qkv, layer, me, n, 3, staged)
            qkv_blocks = [tie(block, up_blocks[-1]) for block in qkv_blocks]
            up_blocks = deal(w_up, layer, me, n, 1, staged)
        qkv_blocks = passed_around(qkv_blocks, n)
        up_blocks = passed_around([tie(block, qkv_blocks[-1]) for block in up_blocks], n)
        qkv_cols = collect(qkv_blocks, me, n, staged and layer > 0)
        up_cols = collect(up_blocks, me, n, staged and layer > 0)
        weights.append((qkv_cols, w_out[layer], up_cols, w_down[layer]))

    kept = []
    for layer in range(LAYERS):
        qkv_cols, out_rows, up_cols, down_rows = weights[layer]
        rel = mm(rows_used, qkv_cols[:, : 2 * own]).astype(BF16)
        qkv = [mm(side, qkv_cols).astype(BF16) for side in hidden_sides]
        attended = [
            attention_forward(side, rel[:SPAN], mask, heads)
            for side, mask in zip(qkv, allowed_sides)
        ]
        context = [side[0] for side in attended]
        probs = [side[1] for side in attended]
        attn_sum = hidden + scatter_sides(*[mm(side, out_rows) for side in context])
        mid = normed(attn_sum)[0] * gains[layer, 0] + biases[layer, 0]
        mid_sides = gather_sides(mid.astype(BF16))
        pre_act = [mm(side, up_cols) for side in mid_sides]
        activation = [gelu(side).astype(BF16) for side in pre_act]
        ffn_sum = mid + scatter_sides(*[mm(side, down_rows) for side in activation])
        kept.append((hidden_sides, qkv, rel[SPAN:], context, probs, attn_sum, mid_sides, pre_act, activation, ffn_sum))
        hidden = normed(ffn_sum)[0] * gains[layer, 1] + biases[layer, 1]
        if layer < LAYERS - 1:
            hidden_sides = gather_sides(hidden.astype(BF16))
    output = hidden.astype(BF16)

    def over_tokens(left, right):
        return mm_tn(left[0], right[0]) + mm_tn(left[1], right[1])

    upstream = cotangent.astype(F32)
    others = jnp.bitwise_xor(me, jnp.arange(n, dtype=jnp.int32))
    shapes = [(LAYERS,) + weight.shape[1:] for weight in (w_qkv, w_out, w_up, w_down)]
    upper = lax.axis_index("rep") % 2
    sums = Sums(jnp.concatenate([upper.reshape(1), others]), shapes)
    grads = {}
    small = [None] * LAYERS
    row_grads = jnp.zeros((SPAN, D), F32)
    top = LAYERS - 1

    def served(*actions):
        if not staged:
            return None

        def meanwhile(sent):
            sums.last = (sums.last, sent)
            for action in actions:
                action()
            return sums.last

        return meanwhile

    def stepping(*names):
        return lambda: sums.step(*names)

    for layer in reversed(range(LAYERS)):
        qkv_cols, out_rows, up_cols, down_rows = weights[layer]
        hidden_sides, qkv, rel, context, probs, attn_sum, mid_sides, pre_act, activation, ffn_sum = kept[layer]
        first = layer == top
        d_ffn, d_gain_two, d_bias_two = norm_backward(upstream, ffn_sum, gains[layer, 1])
        hook = None if first else served(lambda: sums.start("Q1", grads[top][0]))
        branch = gather_sides(d_ffn.astype(BF16), hook)
        d_pre = [
            (mm_nt(side, down_rows) * gelu_slope(pre)).astype(BF16)
            for side, pre in zip(branch, pre_act)
        ]
        g_down = over_tokens(activation, branch).astype(BF16)
        if first:
            hook = served(lambda: sums.start("D1", g_down))
        else:
            hook = served(stepping("D1", "U1"), lambda: sums.start("D0", g_down, grads[top][1]))
        d_mid = d_ffn + scatter_sides(*[mm_nt(side, up_cols) for side in d_pre], hook)
        g_up = over_tokens(mid_sides, d_pre).astype(BF16).reshape(n, own, -1)
        d_attn, d_gain_one, d_bias_one = norm_backward(d_mid, attn_sum, gains[layer, 0])
        hook = None if first else served(stepping("Q1"))
        att = gather_sides(d_attn.astype(BF16), hook)
        d_context = [mm_nt(side, out_rows).astype(BF16) for side in att]
        attended = [
            attention_backward(side, rel, p, grad, heads)
            for side, p, grad in zip(qkv, probs, d_context)
        ]
        d_qkv = [part[0] for part in attended]
        d_rel = (attended[0][1] + attended[1][1]).astype(BF16)
        if first:
            hook = served(stepping("D1"), lambda: sums.start("U1", g_up))
        else:
            hook = served(stepping("D1", "U1"), lambda: sums.start("U0", g_up))
        upstream = d_attn + scatter_sides(*[mm_nt(side, qkv_cols) for side in d_qkv], hook)
        g_out = over_tokens(context, att).astype(BF16)
        g_qkv = over_tokens(hidden_sides, d_qkv) + mm_tn(
            rows_ahead, jnp.concatenate([d_rel, jnp.zeros((SPAN, own), BF16)], axis=1)
        )
        g_qkv = g_qkv.astype(BF16).reshape(n, own, -1)
        row_grads = row_grads + mm_nt(d_rel, qkv_cols[:, : 2 * own])
        small[layer] = (
            jnp.stack([d_gain_one, d_gain_two]),
            jnp.stack([d_bias_one, d_bias_two]),
        )
        grads[layer] = (g_qkv, g_out, g_up, g_down)

    owners = jnp.bitwise_xor(me, jnp.array(order))
    norm_part = jnp.stack(
        [jnp.stack([entry[0] for entry in small]), jnp.stack([entry[1] for entry in small])]
    )
    norm_part = norm_part.reshape(2, LAYERS, 2, n, own).transpose(3, 0, 1, 2, 4)
    norm_part = jnp.take(norm_part, owners, axis=0).reshape(n, 2 * LAYERS * 2 * own)
    norm_part = scatter_sides(norm_part[:2], norm_part[2:])
    position_part = scatter_positions(row_grads, ahead, positions.shape[0], n, me)
    norm_count = 2 * LAYERS * 2 * own
    norm_rows = (norm_count + D - 1) // D
    norm_part = jnp.pad(norm_part.reshape(-1), (0, norm_rows * D - norm_count)).reshape(norm_rows, D)
    packed = jnp.concatenate([position_part, norm_part], axis=0).astype(BF16)

    if staged:
        rows = packed.shape[0]
        packed = jnp.pad(packed, ((0, -rows % 32), (0, 0)))
        finishers = {
            "D1": [(3, 1, 1, 0, 0)],
            "U1": [(2, 1, 1, n, 0)],
            "Q1": [(0, 1, 3, n, 0)],
            "D0": [(3, 0, 1, 0, 0), (1, 1, 1, 0, own * 2)],
            "U0": [(2, 0, 1, n, 0)],
            "Q0": [(0, 0, 3, n, 0)],
            "R": [(1, 0, 1, 0, 0)],
        }
        starters = {"Q0": [g_qkv], "R": [g_out, packed]}
        sums.last = (sums.last, upstream)
        for turn, name in enumerate(TAIL):
            if turn == len(TAIL) - 1:
                sums.place_apart(name, 0, 0, 3, n)
                continue
            if name not in sums.stages:
                sums.start(name, *starters[name])
                continue
            sums.step(name)
            if name in sums.results:
                for target in finishers[name]:
                    sums.place(sums.results[name], *target)
        out_grads = sums.outs
        near, far = [half[own // 2 :] for half in sums.results["R"]]
        lower, higher = jnp.where(upper == 0, near, far), jnp.where(upper == 0, far, near)
        packed = jnp.concatenate([lower, higher], axis=0)[:rows]
    else:
        packed = lax.psum(packed, "rep")
        out_grads = []
        for which, shape in enumerate(shapes):
            out = None
            for layer in range(LAYERS):
                total = grads[layer][which].astype(BF16)
                if which in (0, 2):
                    parts = 3 if which == 0 else 1
                    total = to_owners(total.reshape(n, own, -1), me, n)
                    total = jnp.take(total, others, axis=0).reshape(n, own, parts, -1)
                    total = total.transpose(1, 2, 0, 3).reshape(shape[1:])
                out = put_layer(lax.psum(total, "rep"), layer, out, shape)
            out_grads.append(out)

    grad_positions = packed[:-norm_rows].astype(F32)
    if grad_positions.shape[0] < positions.shape[0]:
        gap = positions.shape[0] - grad_positions.shape[0]
        grad_positions = jnp.where(
            me == 1,
            jnp.pad(grad_positions, ((gap, 0), (0, 0))),
            jnp.where(me == 2, jnp.pad(grad_positions, ((0, gap), (0, 0))), 0.0),
        )
    norm_part = packed[-norm_rows:].astype(F32).reshape(-1)[:norm_count].reshape(2, LAYERS, 2, own).transpose(0, 1, 3, 2)
    return (output, upstream, *out_grads, norm_part[0], norm_part[1], grad_positions)


def solution(mesh):
    tokens = P(("rep", "shard"), None)
    rows = P(None, "shard", None)
    labels = P(("rep", "shard"))
    return jax.shard_map(
        per_device,
        mesh=mesh,
        in_specs=(
            tokens,
            tokens,
            rows,
            rows,
            rows,
            rows,
            rows,
            rows,
            P("shard", None),
            labels,
            labels,
            P(),
        ),
        out_specs=(tokens, tokens, rows, rows, rows, rows, rows, rows, P("shard", None)),
        check_vma=False,
    )
```

```python
from functools import partial
import math

import jax
import jax.numpy as jnp
from jax import lax
from jax.experimental import pallas as pl
from jax.experimental.pallas import tpu as pltpu
from jax.sharding import PartitionSpec as P

D = 1024
H = 16
DH = 64
LAYERS = 2
LEN = 128
SPAN = 2 * LEN
FIRST_ROW = 160
LIVE_ROWS = 192
SCALE = 1.0 / math.sqrt(3 * DH)
NEG_FILL = -1e30
NORM_EPS = 1e-07
F32 = jnp.float32
BF16 = jnp.bfloat16


def mm(a, b):
    return jnp.dot(a, b, preferred_element_type=F32)


def mm_nt(a, b):
    return lax.dot_general(a, b, (((1,), (1,)), ((), ())), preferred_element_type=F32)


def mm_tn(a, b):
    return lax.dot_general(a, b, (((0,), (0,)), ((), ())), preferred_element_type=F32)


def swap(value, axis, mask):
    size = lax.axis_size(axis)
    return lax.ppermute(value, axis, [(i, i ^ mask) for i in range(size)])


def far_order(n):
    span, mask = [0], n // 2
    while mask > 1:
        span = span + [place ^ mask for place in span]
        mask //= 2
    return span[1:]


def group_order(n):
    far = far_order(n)
    return [0, 1] + far + [place ^ 1 for place in far]


def gather_sides(own, meanwhile=None):
    n = lax.axis_size("shard")
    near = jnp.concatenate([own, swap(own, "shard", 1)], axis=0)
    span, mask = own, n // 2
    while mask > 1:
        passed = swap(span, "shard", mask)
        span = passed if mask == 2 and n == 4 else jnp.concatenate([span, passed], axis=0)
        mask //= 2
    far = span if n == 4 else span[own.shape[0] :]
    if meanwhile is not None:
        far = tie(far, meanwhile(own))
    return near, jnp.concatenate([far, swap(far, "shard", 1)], axis=0)


def gather_group(own):
    return jnp.concatenate(gather_sides(own), axis=0)


def scatter_positions(row_grads, ahead, rows, n, me):
    live = jnp.arange(SPAN) < SPAN - 1
    if n == 4 and rows == 128:
        wanted = FIRST_ROW + jnp.arange(LIVE_ROWS)
    else:
        owners = jnp.bitwise_xor(me, jnp.array(group_order(n)))
        wanted = (owners[:, None] * rows + jnp.arange(rows)[None, :]).reshape(-1)
    picks = ((wanted[:, None] == ahead[None, :]) & live[None, :]).astype(BF16)
    by_row = mm(picks, row_grads.astype(BF16))
    if n != 4 or rows != 128:
        return scatter_sides(by_row[: 2 * rows], by_row[2 * rows :])
    size = LIVE_ROWS // 2
    odd = me % 2 == 1
    mine = jnp.where(odd, by_row[:size], by_row[size:])
    total = mine + swap(jnp.where(odd, by_row[size:], by_row[:size]).astype(BF16), "shard", 1).astype(F32)
    return total + swap(total.astype(BF16), "shard", 2).astype(F32)


def scatter_sides(near, far, meanwhile=None):
    n = lax.axis_size("shard")
    half = far.shape[0] // 2
    far = far[:half] + swap(far[half:].astype(BF16), "shard", 1).astype(F32)
    half = near.shape[0] // 2
    near = near[:half] + swap(near[half:].astype(BF16), "shard", 1).astype(F32)
    if n == 4:
        far = far.astype(BF16)
        passed = swap(far, "shard", 2)
        if meanwhile is not None:
            passed = tie(passed, meanwhile(far))
        return near + passed.astype(F32)
    total, mask = jnp.concatenate([near, far], axis=0), 2
    while mask < n:
        half = total.shape[0] // 2
        total = total[:half] + swap(total[half:].astype(BF16), "shard", mask).astype(F32)
        mask *= 2
    return total


def gather_positions(positions, n, me):
    last_row = FIRST_ROW + LIVE_ROWS
    rows = positions.shape[0]
    if n != 4 or rows != 128:
        whole = lax.all_gather(positions, "shard", axis=0, tiled=True)
        return whole[FIRST_ROW:last_row]
    size = LIVE_ROWS // 2
    mine = jnp.where(me == 1, positions[rows - size :], positions[:size])
    passed = lax.ppermute(mine, "shard", [(1, 3), (2, 0)])
    held = jnp.where((me == 1) | (me == 2), mine, passed)
    other = swap(held, "shard", 1)
    low = me % 2 == 1
    return jnp.concatenate([jnp.where(low, held, other), jnp.where(low, other, held)], axis=0)


def copy_blocks_kernel(n, me_ref, *refs):
    for source, target in zip(refs[:n], refs[n:]):
        target[...] = source[0]


def deal(weight, layer, me, n, parts, shared=False):
    rows = weight.shape[1]
    c = weight.shape[2] // (parts * n)
    if c % 128:
        blocks = []
        for mask in range(n):
            other = jnp.bitwise_xor(me, mask)
            pieces = [
                lax.dynamic_slice(weight, (layer, 0, (part * n + other) * c), (1, rows, c))[0]
                for part in range(parts)
            ]
            blocks.append(jnp.concatenate(pieces, axis=1))
        return blocks
    split = 1 if parts > 1 or c % 512 else 4

    count = n - 1 if shared else n

    def source_spec(mask):
        def where(part, cut, me):
            other = jnp.bitwise_xor(me[0], mask + me[1] if shared and mask == 2 else mask)
            return (layer, 0, (part * n + other) * split + cut)

        return pl.BlockSpec((1, rows, c // split), where)

    target = pl.BlockSpec((rows, c // split), lambda part, cut, me: (0, part * split + cut))
    return pl.pallas_call(
        partial(copy_blocks_kernel, count),
        grid_spec=pltpu.PrefetchScalarGridSpec(
            num_scalar_prefetch=1,
            grid=(parts, split),
            in_specs=[source_spec(mask) for mask in range(count)],
            out_specs=[target] * count,
        ),
        out_shape=[jax.ShapeDtypeStruct((rows, parts * c), BF16)] * count,
        compiler_params=pltpu.CompilerParams(vmem_limit_bytes=24 * 1024 * 1024),
        name="deal",
    )(place_of(me), *([weight] * count))


def collect_kernel(n, shared, me_ref, *refs):
    step = pl.program_id(1)
    for at in range(n):
        mask = at
        if shared and at > 1:
            mask = 2 + me_ref[1] if at == 2 else 3 - me_ref[1]

        @pl.when(step == jnp.bitwise_xor(me_ref[0], mask))
        def _():
            refs[n][...] = refs[at][...]


def collect(blocks, me, n, shared):
    rows, width = blocks[0].shape
    if rows % 16 or width % 256:
        whole = jnp.zeros((n * rows, width), BF16)
        for mask, block in enumerate(blocks):
            other = jnp.bitwise_xor(me, mask)
            whole = lax.dynamic_update_slice(whole, block, (other * rows, 0))
        return whole
    c = width // 2
    return pl.pallas_call(
        partial(collect_kernel, n, shared),
        grid_spec=pltpu.PrefetchScalarGridSpec(
            num_scalar_prefetch=1,
            grid=(width // c, n),
            in_specs=[pl.BlockSpec((rows, c), lambda cut, step, me: (0, cut))] * n,
            out_specs=pl.BlockSpec((rows, c), lambda cut, step, me: (step, cut)),
        ),
        out_shape=jax.ShapeDtypeStruct((n * rows, width), BF16),
        compiler_params=pltpu.CompilerParams(vmem_limit_bytes=24 * 1024 * 1024),
        name="collect",
    )(place_of(me), *blocks)


def place_of(me):
    return jnp.stack([me, lax.axis_index("rep") % 2])


def passed_around(blocks, n):
    passed = [swap(block, "shard", mask) if mask else block for mask, block in enumerate(blocks[:2])]
    if len(blocks) == n:
        return passed + [swap(block, "shard", mask + 2) for mask, block in enumerate(blocks[2:])]
    size = lax.axis_size("rep")
    pairs = [(r * n + i, r * n + (i ^ (2 + r % 2))) for r in range(size) for i in range(n)]
    across = lax.ppermute(blocks[2], ("rep", "shard"), pairs)
    return passed + [across, swap(across, "rep", 1)]


def to_owners(columns, me, n):
    blocks = []
    for mask in range(n):
        block = lax.dynamic_index_in_dim(columns, jnp.bitwise_xor(me, mask), 0, keepdims=False)
        blocks.append(swap(block, "shard", mask) if mask else block)
    return jnp.stack(blocks)


def tie(value, after):
    return lax.optimization_barrier((value, after))[0]


INWARDS = [(0, 2), (1, 3), (6, 4), (7, 5)]
ACROSS = [(2, 4), (3, 5), (4, 2), (5, 3)]
OUTWARDS = [(2, 0), (3, 1), (4, 6), (5, 7)]
TAIL = (
    "D0", "U1", "Q1", "Q0", "D1", "R", "U0", "D0", "Q1", "U1", "Q0", "R", "U1", "U0", "D0",
    "Q1", "D1", "Q0", "Q1", "U0", "R", "D0", "U1", "Q1", "R", "U0", "Q0", "R", "U0", "D0",
    "Q0", "Q0", "R", "U0", "Q0",
)


def line_stages(value):
    rep = lax.axis_index("rep")
    for pairs in (INWARDS, ACROSS):
        passed = yield value, lax.ppermute(value, "rep", pairs)
        value = (value.astype(F32) + passed.astype(F32)).astype(BF16)
    passed = yield value, lax.ppermute(value, "rep", OUTWARDS)
    return jnp.where((rep >= 2) & (rep < 6), value, passed)


def halves_of(grads, upper):
    pieces = []
    for grad in grads:
        size = grad.shape[-2] // 2
        pieces.append(lax.dynamic_slice_in_dim(grad, upper * size, size, grad.ndim - 2))
    return pieces[0] if len(pieces) == 1 else jnp.concatenate(pieces, axis=0)


def half_stages(grads):
    upper = lax.axis_index("rep") % 2
    me = lax.axis_index("shard")
    sent = halves_of(grads, 1 - upper)
    held = halves_of(grads, upper)
    passed = yield sent, swap(sent, "rep", 1)
    value = (held.astype(F32) + passed.astype(F32)).astype(BF16)
    value = yield from line_stages(value)
    if value.ndim == 3:
        blocks = []
        for mask in range(value.shape[0]):
            other = jnp.bitwise_xor(me, mask)
            blocks.append(lax.dynamic_index_in_dim(value, other, 0, keepdims=False))
        moved = [swap(block, "shard", mask) if mask else block for mask, block in enumerate(blocks)]
        blocks = yield blocks, moved
        value = jnp.stack(blocks)
    far = yield value, swap(value, "rep", 1)
    return value, far


class Sums:
    def __init__(self, index, shapes):
        self.index, self.shapes = index, shapes
        self.outs = [None] * len(shapes)
        self.stages, self.moving, self.results = {}, {}, {}
        self.last, self.placed, self.last_sent = (), None, {}

    def ordered(self, value):
        out = () if self.placed is None else self.outs[self.placed]
        value, _, out = lax.optimization_barrier((value, self.last, out))
        if self.placed is not None:
            self.outs[self.placed] = out
            self.placed = None
        return value

    def start(self, name, *grads):
        grads = self.ordered([grad.astype(BF16) for grad in grads])
        self.stages[name] = half_stages(grads)
        self.last, self.moving[name] = next(self.stages[name])

    def step(self, *names):
        for name in names:
            moving = self.ordered(self.moving.pop(name))
            try:
                self.last, self.moving[name] = self.stages[name].send(moving)
                self.last_sent[name] = self.last
            except StopIteration as stop:
                self.results[name] = stop.value

    def place_apart(self, name, which, layer, parts, n):
        args = (self.index, layer)
        near = self.ordered(self.last_sent[name])
        out = place_half(near, False, *args, self.outs[which], self.shapes[which], parts, n)
        self.outs[which], self.placed = out, which
        self.step(name)
        far = self.ordered(self.results[name][1])
        out = place_half(far, True, *args, self.outs[which], self.shapes[which], parts, n)
        self.outs[which], self.placed = out, which

    def place(self, total, which, layer, parts, n, offset=0):
        shape, out = self.shapes[which], self.outs[which]
        total = self.ordered(total)
        if isinstance(total, tuple):
            out = place(total, self.index, layer, out, shape, parts, n, offset)
        else:
            out = place_whole(total, self.index, layer, out, shape, parts, n)
        self.outs[which], self.placed = out, which


def place_kernel(parts, n, c, steps, index_ref, near_ref, far_ref, *rest):
    out_ref = rest[-1]

    def put(source):
        if n == 0:
            out_ref[0] = source[...].astype(F32)
            return
        for mask in range(n):
            for part in range(parts):
                at = pl.multiple_of(index_ref[1 + mask] * c + part * n * c, c)
                out_ref[0, :, pl.ds(at, c)] = source[mask, :, part * c : (part + 1) * c].astype(F32)

    @pl.when(pl.program_id(0) < steps)
    def _():
        put(near_ref)

    @pl.when(pl.program_id(0) >= steps)
    def _():
        put(far_ref)


def place(halves, index, layer, out, shape, parts, n, offset):
    size = shape[1] // 2
    rows = size // 4 if size % 64 == 0 else size
    steps, skip = size // rows, offset // rows
    c = shape[2] // (parts * n) if n else 0
    lead = (n,) if n else ()
    block = lead + (rows, parts * c if n else shape[2])
    zeros = (0,) * len(lead)

    def target(s, index):
        first = index[0] * steps + s
        second = (1 - index[0]) * steps + s - steps
        return (layer, jnp.where(s < steps, first, second), 0)

    in_specs = [
        pl.BlockSpec(block, lambda s, index: zeros + (skip + jnp.minimum(s, steps - 1), 0)),
        pl.BlockSpec(block, lambda s, index: zeros + (skip + jnp.maximum(s - steps, 0), 0)),
    ]
    operands = [index, *halves]
    aliases = {}
    if out is not None:
        in_specs.append(pl.BlockSpec(memory_space=pl.ANY))
        operands.append(out)
        aliases = {3: 0}
    return pl.pallas_call(
        partial(place_kernel, parts, n, c, steps),
        grid_spec=pltpu.PrefetchScalarGridSpec(
            num_scalar_prefetch=1,
            grid=(2 * steps,),
            in_specs=in_specs,
            out_specs=pl.BlockSpec((1, rows, shape[2]), target),
        ),
        out_shape=jax.ShapeDtypeStruct(shape, F32),
        input_output_aliases=aliases,
        compiler_params=pltpu.CompilerParams(vmem_limit_bytes=32 * 1024 * 1024),
        name="place",
    )(*operands)


def place_whole_kernel(parts, n, c, index_ref, blocks_ref, *rest):
    out_ref = rest[-1]
    if n == 0:
        out_ref[0] = blocks_ref[...].astype(F32)
        return
    for mask in range(n):
        for part in range(parts):
            at = pl.multiple_of(index_ref[1 + mask] * c + part * n * c, c)
            out_ref[0, :, pl.ds(at, c)] = blocks_ref[mask, :, part * c : (part + 1) * c].astype(F32)


def place_whole(blocks, index, layer, out, shape, parts, n):
    rows = shape[1] // 8
    c = shape[2] // (parts * n) if n else 0
    lead = (n,) if n else ()
    zeros = (0,) * len(lead)
    block = lead + (rows, parts * c if n else shape[2])
    in_specs = [pl.BlockSpec(block, lambda s, index: zeros + (s, 0))]
    operands, aliases = [index, blocks], {}
    if out is not None:
        in_specs.append(pl.BlockSpec(memory_space=pl.ANY))
        operands.append(out)
        aliases = {2: 0}
    return pl.pallas_call(
        partial(place_whole_kernel, parts, n, c),
        grid_spec=pltpu.PrefetchScalarGridSpec(
            num_scalar_prefetch=1,
            grid=(shape[1] // rows,),
            in_specs=in_specs,
            out_specs=pl.BlockSpec((1, rows, shape[2]), lambda s, index: (layer, s, 0)),
        ),
        out_shape=jax.ShapeDtypeStruct(shape, F32),
        input_output_aliases=aliases,
        compiler_params=pltpu.CompilerParams(vmem_limit_bytes=32 * 1024 * 1024),
        name="place_whole",
    )(*operands)


def place_half(source, second, index, layer, out, shape, parts, n):
    size = shape[1] // 2
    rows = size // 4 if size % 64 == 0 else size
    steps, c = size // rows, shape[2] // (parts * n)

    def kernel(index_ref, source_ref, *rest):
        for mask in range(n):
            for part in range(parts):
                at = pl.multiple_of(index_ref[1 + mask] * c + part * n * c, c)
                piece = source_ref[mask, :, part * c : (part + 1) * c]
                rest[-1][0, :, pl.ds(at, c)] = piece.astype(F32)

    def target(s, index):
        half = 1 - index[0] if second else index[0]
        return (layer, half * steps + s, 0)

    in_specs = [pl.BlockSpec((n, rows, parts * c), lambda s, index: (0, s, 0))]
    operands, aliases = [index, source], {}
    if out is not None:
        in_specs.append(pl.BlockSpec(memory_space=pl.ANY))
        operands.append(out)
        aliases = {2: 0}
    return pl.pallas_call(
        kernel,
        grid_spec=pltpu.PrefetchScalarGridSpec(
            num_scalar_prefetch=1,
            grid=(steps,),
            in_specs=in_specs,
            out_specs=pl.BlockSpec((1, rows, shape[2]), target),
        ),
        out_shape=jax.ShapeDtypeStruct(shape, F32),
        input_output_aliases=aliases,
        compiler_params=pltpu.CompilerParams(vmem_limit_bytes=32 * 1024 * 1024),
        name="place_half",
    )(*operands)


def put_layer(total, layer, out, shape):
    out = jnp.zeros(shape, F32) if out is None else out
    return out.at[layer].set(total.astype(F32))


def attention_forward_kernel(heads, qkv_ref, rel_ref, allowed_ref, context_ref, probs_ref):
    width = heads * DH
    allowed = allowed_ref[0] > 0

    def pick(ref, group, head):
        at = group * width + head * DH
        return ref[:, at : at + DH]

    def skew(table):
        return pltpu.roll(table, LEN + 1, 1, stride=1, stride_axis=0)[:, :LEN]

    every = range(heads)
    q = [pick(qkv_ref, 0, head) for head in every]
    k = [pick(qkv_ref, 1, head) for head in every]
    by_key = [mm_nt(q[head], pick(rel_ref, 1, head)) for head in every]
    by_query = [mm_nt(k[head], pick(rel_ref, 0, head)) for head in every]
    direct = [mm_nt(q[head], k[head]) for head in every]
    by_key = [skew(table) for table in by_key]
    by_query = [skew(table) for table in by_query]
    scores = [(direct[head] + by_key[head] + by_query[head].T) * SCALE for head in every]
    scores = [jnp.where(allowed, score, NEG_FILL) for score in scores]
    tops = [jnp.max(score, axis=1, keepdims=True) for score in scores]
    terms = [jnp.exp(score - most) for score, most in zip(scores, tops)]
    totals = [jnp.sum(term, axis=1, keepdims=True) for term in terms]
    probs = [term / total for term, total in zip(terms, totals)]
    for head in every:
        probs_ref[0, head] = probs[head]
    context = [mm(probs[head].astype(BF16), pick(qkv_ref, 2, head)).astype(BF16) for head in every]
    context_ref[...] = jnp.concatenate(context, axis=1)


def attention_forward(qkv, rel_back, allowed, heads):
    count = allowed.shape[0]
    width = heads * DH
    return pl.pallas_call(
        partial(attention_forward_kernel, heads),
        grid=(count,),
        in_specs=[
            pl.BlockSpec((LEN, 3 * width), lambda s: (s, 0)),
            pl.BlockSpec((SPAN, 2 * width), lambda s: (0, 0)),
            pl.BlockSpec((1, LEN, LEN), lambda s: (s, 0, 0)),
        ],
        out_specs=[
            pl.BlockSpec((LEN, width), lambda s: (s, 0)),
            pl.BlockSpec((1, heads, LEN, LEN), lambda s: (s, 0, 0, 0)),
        ],
        out_shape=[
            jax.ShapeDtypeStruct((count * LEN, width), BF16),
            jax.ShapeDtypeStruct((count, heads, LEN, LEN), F32),
        ],
        compiler_params=pltpu.CompilerParams(vmem_limit_bytes=24 * 1024 * 1024),
        name="attention_forward",
    )(qkv, rel_back, allowed)


def attention_backward_kernel(heads, qkv_ref, rel_ref, probs_ref, grad_ref, dqkv_ref, drel_ref):
    width = heads * DH

    @pl.when(pl.program_id(0) == 0)
    def _():
        drel_ref[...] = jnp.zeros_like(drel_ref)

    row = lax.broadcasted_iota(jnp.int32, (LEN, LEN), 0)
    column = lax.broadcasted_iota(jnp.int32, (LEN, LEN), 1)
    flip = jnp.where(row + column == LEN - 1, 1.0, 0.0).astype(BF16)
    blank = jnp.zeros((LEN, LEN), F32)

    def pick(ref, group, head):
        at = group * width + head * DH
        return ref[:, at : at + DH]

    def spread(flipped):
        wide = jnp.concatenate([flipped, blank], axis=1)
        return pltpu.roll(wide, 0, 1, stride=1, stride_axis=0).astype(BF16)

    every = range(heads)
    q, k, v = [[pick(qkv_ref, group, head) for head in every] for group in range(3)]
    grad = [pick(grad_ref, 0, head) for head in every]
    probs = [probs_ref[0, head] for head in every]
    d_probs = [mm_nt(grad[head], v[head]) for head in every]
    d_value = [mm_tn(probs[head].astype(BF16), grad[head]) for head in every]
    inner = [jnp.sum(d_probs[head] * probs[head], axis=1, keepdims=True) for head in every]
    d_scores = [(probs[head] * (d_probs[head] - inner[head])).astype(BF16) for head in every]
    key_side = [mm(d_score, flip) for d_score in d_scores]
    query_side = [mm_tn(d_score, flip) for d_score in d_scores]
    key_side = [spread(flipped) for flipped in key_side]
    query_side = [spread(flipped) for flipped in query_side]
    d_query = [
        (mm(d_scores[head], k[head]) + mm(key_side[head], pick(rel_ref, 1, head))) * SCALE
        for head in every
    ]
    d_key = [
        (mm_tn(d_scores[head], q[head]) + mm(query_side[head], pick(rel_ref, 0, head))) * SCALE
        for head in every
    ]
    dqkv_ref[...] = jnp.concatenate(d_query + d_key + d_value, axis=1).astype(BF16)
    d_rel_q = [mm_tn(query_side[head], k[head]) * SCALE for head in every]
    d_rel_k = [mm_tn(key_side[head], q[head]) * SCALE for head in every]
    drel_ref[...] += jnp.concatenate(d_rel_q + d_rel_k, axis=1)


def attention_backward(qkv, rel_ahead, probs, d_context, heads):
    count = probs.shape[0]
    width = heads * DH
    return pl.pallas_call(
        partial(attention_backward_kernel, heads),
        grid=(count,),
        in_specs=[
            pl.BlockSpec((LEN, 3 * width), lambda s: (s, 0)),
            pl.BlockSpec((SPAN, 2 * width), lambda s: (0, 0)),
            pl.BlockSpec((1, heads, LEN, LEN), lambda s: (s, 0, 0, 0)),
            pl.BlockSpec((LEN, width), lambda s: (s, 0)),
        ],
        out_specs=[
            pl.BlockSpec((LEN, 3 * width), lambda s: (s, 0)),
            pl.BlockSpec((SPAN, 2 * width), lambda s: (0, 0)),
        ],
        out_shape=[
            jax.ShapeDtypeStruct((count * LEN, 3 * width), BF16),
            jax.ShapeDtypeStruct((SPAN, 2 * width), F32),
        ],
        compiler_params=pltpu.CompilerParams(vmem_limit_bytes=24 * 1024 * 1024),
        name="attention_backward",
    )(qkv, rel_ahead, probs, d_context)


def normed(values):
    centre = values - jnp.mean(values, axis=-1, keepdims=True)
    inverse = lax.rsqrt(jnp.mean(centre * centre, axis=-1, keepdims=True) + NORM_EPS)
    return centre * inverse, inverse


def norm_backward(upstream, values, gain):
    hat, inverse = normed(values)
    pushed = upstream * gain
    first = jnp.mean(pushed, axis=-1, keepdims=True)
    second = jnp.mean(pushed * hat, axis=-1, keepdims=True)
    back = inverse * (pushed - first - hat * second)
    return back, jnp.sum(upstream * hat, axis=0), jnp.sum(upstream, axis=0)


def gelu(x):
    return 0.5 * x * (1.0 + lax.erf(x * math.sqrt(0.5)))


def gelu_slope(x):
    density = jnp.exp(-0.5 * x * x) * (1.0 / math.sqrt(2.0 * math.pi))
    return 0.5 * (1.0 + lax.erf(x * math.sqrt(0.5))) + x * density


def per_device(
    tokens,
    cotangent,
    w_qkv,
    w_out,
    w_up,
    w_down,
    ln_gain,
    ln_bias,
    positions,
    segments,
    keep_mask,
    buckets,
):
    n = lax.axis_size("shard")
    me = lax.axis_index("shard")
    own = D // n
    heads = H // n
    order = group_order(n)

    staged = lax.axis_size("rep") == 8 and n == 4
    qkv_blocks = deal(w_qkv, 0, me, n, 3)
    up_blocks = deal(w_up, 0, me, n, 1)
    hidden = tokens.astype(F32)
    small_part = jnp.concatenate(
        [
            segments.astype(BF16),
            keep_mask.astype(BF16),
            jnp.stack([ln_gain, ln_bias]).transpose(0, 1, 3, 2).reshape(-1),
        ]
    )
    small_count = small_part.shape[0]
    small_part = jnp.pad(small_part, (0, 16 * D - small_count)).reshape(16, D)
    sides = gather_sides(jnp.concatenate([tokens, small_part], axis=0))
    sides = [side.reshape(-1, LEN + 16, D) for side in sides]
    hidden_sides = [side[:, :LEN].reshape(-1, D) for side in sides]
    small_all = jnp.concatenate([side[:, LEN:] for side in sides], axis=0)
    small_all = small_all.reshape(n, 16 * D)[:, :small_count].astype(F32)
    segment, keep = small_all[:, :LEN], small_all[:, LEN : 2 * LEN]
    allowed = (segment[:, :, None] == segment[:, None, :]) & (keep[:, None, :] == 1.0)
    allowed = (allowed | jnp.eye(LEN, dtype=bool)[None]).astype(F32)
    allowed_sides = (allowed[:2], allowed[2:])
    live_rows = gather_positions(positions, n, me)
    ahead = jnp.concatenate([buckets, buckets[-1:]])
    back = jnp.concatenate([buckets[::-1], buckets[:1]])
    wanted = jnp.concatenate([back, ahead]) - FIRST_ROW
    picks = (wanted[:, None] == jnp.arange(LIVE_ROWS)[None, :]).astype(BF16)
    rows_used = mm(picks, live_rows).astype(BF16)
    rows_ahead = rows_used[SPAN:]
    places = [order.index(place) for place in range(n)]
    places = jnp.take(jnp.array(places), jnp.bitwise_xor(me, jnp.arange(n)))
    norms = jnp.take(small_all[:, 2 * LEN :], places, axis=0).reshape(n, 2, LAYERS, 2, own)
    norms = norms.transpose(1, 2, 3, 0, 4).reshape(2, LAYERS, 2, D)
    gains, biases = norms[0], norms[1]

    weights = []
    for layer in range(LAYERS):
        if layer:
            qkv_blocks = deal(w_qkv, layer, me, n, 3, staged)
            qkv_blocks = [tie(block, up_blocks[-1]) for block in qkv_blocks]
            up_blocks = deal(w_up, layer, me, n, 1, staged)
        qkv_blocks = passed_around(qkv_blocks, n)
        up_blocks = passed_around([tie(block, qkv_blocks[-1]) for block in up_blocks], n)
        qkv_cols = collect(qkv_blocks, me, n, staged and layer > 0)
        up_cols = collect(up_blocks, me, n, staged and layer > 0)
        weights.append((qkv_cols, w_out[layer], up_cols, w_down[layer]))

    kept = []
    for layer in range(LAYERS):
        qkv_cols, out_rows, up_cols, down_rows = weights[layer]
        rel = mm(rows_used, qkv_cols[:, : 2 * own]).astype(BF16)
        qkv = [mm(side, qkv_cols).astype(BF16) for side in hidden_sides]
        attended = [
            attention_forward(side, rel[:SPAN], mask, heads)
            for side, mask in zip(qkv, allowed_sides)
        ]
        context = [side[0] for side in attended]
        probs = [side[1] for side in attended]
        attn_sum = hidden + scatter_sides(*[mm(side, out_rows) for side in context])
        mid = normed(attn_sum)[0] * gains[layer, 0] + biases[layer, 0]
        mid_sides = gather_sides(mid.astype(BF16))
        pre_act = [mm(side, up_cols) for side in mid_sides]
        activation = [gelu(side).astype(BF16) for side in pre_act]
        ffn_sum = mid + scatter_sides(*[mm(side, down_rows) for side in activation])
        kept.append((hidden_sides, qkv, rel[SPAN:], context, probs, attn_sum, mid_sides, pre_act, activation, ffn_sum))
        hidden = normed(ffn_sum)[0] * gains[layer, 1] + biases[layer, 1]
        if layer < LAYERS - 1:
            hidden_sides = gather_sides(hidden.astype(BF16))
    output = hidden.astype(BF16)

    def over_tokens(left, right):
        return mm_tn(left[0], right[0]) + mm_tn(left[1], right[1])

    upstream = cotangent.astype(F32)
    others = jnp.bitwise_xor(me, jnp.arange(n, dtype=jnp.int32))
    shapes = [(LAYERS,) + weight.shape[1:] for weight in (w_qkv, w_out, w_up, w_down)]
    upper = lax.axis_index("rep") % 2
    sums = Sums(jnp.concatenate([upper.reshape(1), others]), shapes)
    grads = {}
    small = [None] * LAYERS
    row_grads = jnp.zeros((SPAN, D), F32)
    top = LAYERS - 1

    def served(*actions):
        if not staged:
            return None

        def meanwhile(sent):
            sums.last = (sums.last, sent)
            for action in actions:
                action()
            return sums.last

        return meanwhile

    def stepping(*names):
        return lambda: sums.step(*names)

    for layer in reversed(range(LAYERS)):
        qkv_cols, out_rows, up_cols, down_rows = weights[layer]
        hidden_sides, qkv, rel, context, probs, attn_sum, mid_sides, pre_act, activation, ffn_sum = kept[layer]
        first = layer == top
        d_ffn, d_gain_two, d_bias_two = norm_backward(upstream, ffn_sum, gains[layer, 1])
        hook = None if first else served(lambda: sums.start("Q1", grads[top][0]))
        branch = gather_sides(d_ffn.astype(BF16), hook)
        d_pre = [
            (mm_nt(side, down_rows) * gelu_slope(pre)).astype(BF16)
            for side, pre in zip(branch, pre_act)
        ]
        g_down = over_tokens(activation, branch).astype(BF16)
        if first:
            hook = served(lambda: sums.start("D1", g_down))
        else:
            hook = served(stepping("D1", "U1"), lambda: sums.start("D0", g_down, grads[top][1]))
        d_mid = d_ffn + scatter_sides(*[mm_nt(side, up_cols) for side in d_pre], hook)
        g_up = over_tokens(mid_sides, d_pre).astype(BF16).reshape(n, own, -1)
        d_attn, d_gain_one, d_bias_one = norm_backward(d_mid, attn_sum, gains[layer, 0])
        hook = None if first else served(stepping("Q1"))
        att = gather_sides(d_attn.astype(BF16), hook)
        d_context = [mm_nt(side, out_rows).astype(BF16) for side in att]
        attended = [
            attention_backward(side, rel, p, grad, heads)
            for side, p, grad in zip(qkv, probs, d_context)
        ]
        d_qkv = [part[0] for part in attended]
        d_rel = (attended[0][1] + attended[1][1]).astype(BF16)
        if first:
            hook = served(stepping("D1"), lambda: sums.start("U1", g_up))
        else:
            hook = served(stepping("D1", "U1"), lambda: sums.start("U0", g_up))
        upstream = d_attn + scatter_sides(*[mm_nt(side, qkv_cols) for side in d_qkv], hook)
        g_out = over_tokens(context, att).astype(BF16)
        g_qkv = over_tokens(hidden_sides, d_qkv) + mm_tn(
            rows_ahead, jnp.concatenate([d_rel, jnp.zeros((SPAN, own), BF16)], axis=1)
        )
        g_qkv = g_qkv.astype(BF16).reshape(n, own, -1)
        row_grads = row_grads + mm_nt(d_rel, qkv_cols[:, : 2 * own])
        small[layer] = (
            jnp.stack([d_gain_one, d_gain_two]),
            jnp.stack([d_bias_one, d_bias_two]),
        )
        grads[layer] = (g_qkv, g_out, g_up, g_down)

    owners = jnp.bitwise_xor(me, jnp.array(order))
    norm_part = jnp.stack(
        [jnp.stack([entry[0] for entry in small]), jnp.stack([entry[1] for entry in small])]
    )
    norm_part = norm_part.reshape(2, LAYERS, 2, n, own).transpose(3, 0, 1, 2, 4)
    norm_part = jnp.take(norm_part, owners, axis=0).reshape(n, 2 * LAYERS * 2 * own)
    norm_part = scatter_sides(norm_part[:2], norm_part[2:])
    position_part = scatter_positions(row_grads, ahead, positions.shape[0], n, me)
    norm_count = 2 * LAYERS * 2 * own
    norm_rows = (norm_count + D - 1) // D
    norm_part = jnp.pad(norm_part.reshape(-1), (0, norm_rows * D - norm_count)).reshape(norm_rows, D)
    packed = jnp.concatenate([position_part, norm_part], axis=0).astype(BF16)

    if staged:
        rows = packed.shape[0]
        packed = jnp.pad(packed, ((0, -rows % 32), (0, 0)))
        finishers = {
            "D1": [(3, 1, 1, 0, 0)],
            "U1": [(2, 1, 1, n, 0)],
            "Q1": [(0, 1, 3, n, 0)],
            "D0": [(3, 0, 1, 0, 0), (1, 1, 1, 0, own * 2)],
            "U0": [(2, 0, 1, n, 0)],
            "Q0": [(0, 0, 3, n, 0)],
            "R": [(1, 0, 1, 0, 0)],
        }
        starters = {"Q0": [g_qkv], "R": [g_out, packed]}
        sums.last = (sums.last, upstream)
        apart = {len(TAIL) - 2: (2, 0, 1, n), len(TAIL) - 1: (0, 0, 3, n)}
        for turn, name in enumerate(TAIL):
            if turn in apart:
                sums.place_apart(name, *apart[turn])
                continue
            if name not in sums.stages:
                sums.start(name, *starters[name])
                continue
            sums.step(name)
            if name in sums.results:
                for target in finishers[name]:
                    sums.place(sums.results[name], *target)
        out_grads = sums.outs
        near, far = [half[own // 2 :] for half in sums.results["R"]]
        lower, higher = jnp.where(upper == 0, near, far), jnp.where(upper == 0, far, near)
        packed = jnp.concatenate([lower, higher], axis=0)[:rows]
    else:
        packed = lax.psum(packed, "rep")
        out_grads = []
        for which, shape in enumerate(shapes):
            out = None
            for layer in range(LAYERS):
                total = grads[layer][which].astype(BF16)
                if which in (0, 2):
                    parts = 3 if which == 0 else 1
                    total = to_owners(total.reshape(n, own, -1), me, n)
                    total = jnp.take(total, others, axis=0).reshape(n, own, parts, -1)
                    total = total.transpose(1, 2, 0, 3).reshape(shape[1:])
                out = put_layer(lax.psum(total, "rep"), layer, out, shape)
            out_grads.append(out)

    grad_positions = packed[:-norm_rows].astype(F32)
    if grad_positions.shape[0] < positions.shape[0]:
        gap = positions.shape[0] - grad_positions.shape[0]
        grad_positions = jnp.where(
            me == 1,
            jnp.pad(grad_positions, ((gap, 0), (0, 0))),
            jnp.where(me == 2, jnp.pad(grad_positions, ((0, gap), (0, 0))), 0.0),
        )
    norm_part = packed[-norm_rows:].astype(F32).reshape(-1)[:norm_count].reshape(2, LAYERS, 2, own).transpose(0, 1, 3, 2)
    return (output, upstream, *out_grads, norm_part[0], norm_part[1], grad_positions)


def solution(mesh):
    tokens = P(("rep", "shard"), None)
    rows = P(None, "shard", None)
    labels = P(("rep", "shard"))
    return jax.shard_map(
        per_device,
        mesh=mesh,
        in_specs=(
            tokens,
            tokens,
            rows,
            rows,
            rows,
            rows,
            rows,
            rows,
            P("shard", None),
            labels,
            labels,
            P(),
        ),
        out_specs=(tokens, tokens, rows, rows, rows, rows, rows, rows, P("shard", None)),
        check_vma=False,
    )
```
